32 devices in a mesh: brow: 8 (over y, x, core), bcol: 4 (over z).
Axes of the slice: x: 2, y: 2, z: 4, core: 2. Of those that a mesh axis runs over, the one named last changes fastest.
Arguments:
- vectors: bfloat16 [8, 65536], P(None, ('brow', 'bcol')), may hold values from -6 to 6
- tiles: bfloat16 [6144, 4096], P(('brow', 'bcol')), may hold values from -0.29882812 to 0.29882812
- tile_rows: int32 [6144], P(('brow', 'bcol')), may hold values from 0 to 127
- tile_cols: int32 [6144], P(('brow', 'bcol')), may hold values from 0 to 255
- counts: int32 [8, 4], P('brow', 'bcol'), may hold values from 64 to 192, as said below
Outputs:
- product: float32 [8, 65536], P(None, ('brow', 'bcol'))
The draws below stay inside these ranges and needn't reach their ends.
Inputs may be any that keep to these rules, and one draw needn't show every extreme that they name: `counts`: some grid block uses all 192 slots in every draw; every block uses at least a third of them.
All inputs are finite; a program needn't handle non-finite values.
Results may differ from the reference program's by a relative error of at most 0.0003.
Values may be sent and summed in bfloat16 or wider, within the bound.
No kernel may reach another device: no remote copies, remote signals or barrier semaphores. Data moves between devices by JAX's collectives and lax.ppermute only.
A program may use at most 64 MiB of HBM per device.

```python
import jax
import jax.numpy as jnp
from jax import lax

PIECE = 2048
TMAX = 192
VECS = 8
TILE = 64
DIM = 65536
TILES = 6144
N_BROW = 8
N_BCOL = 4


def draw_counts(key, part):
    first_key, second_key = jax.random.split(jax.random.fold_in(key, 17))
    values = jax.random.randint(first_key, (N_BROW * N_BCOL,), TMAX // 3, TMAX + 1)
    picked = jax.random.randint(second_key, (), 0, N_BROW * N_BCOL)
    values = values.at[picked].set(TMAX)
    return values.reshape(N_BROW, N_BCOL).astype(jnp.int32)


def set_ends(drawn, rng, least, largest):
    dims = drawn.shape
    place = [jax.random.randint(jax.random.fold_in(rng, axis), (), 0, dims[axis]) for axis in range(len(dims))]
    drawn = drawn.at[tuple(place)].set(least)
    longest = dims.index(max(dims))
    place[longest] = (place[longest] + 1) % dims[longest]
    return drawn.at[tuple(place)].set(largest)


def block_scale(own_key, dims, cuts, low, largest):
    level, own = 1.0, jax.random.fold_in(own_key, 6)
    for position, shards_of in cuts:
        heights = jnp.exp(jax.random.uniform(jax.random.fold_in(own, position), (shards_of,), jnp.float32, low / len(cuts), largest / len(cuts)))
        level = level * jnp.repeat(heights, dims[position] // shards_of).reshape([-1 if axis == position else 1 for axis in range(len(dims))])
    return level


def gaussian(own_key, shape, width, limit, shards=(), held_as=jnp.bfloat16):
    factor_of = block_scale(own_key, shape, shards, -0.22, 0.18) if shards else 1.0
    values = jax.random.normal(own_key, shape, jnp.float32) * width * factor_of
    return jnp.minimum(jnp.maximum(values, -limit), limit).astype(held_as)


def setup_inputs(seed: int = 0) -> dict:
    key_of = jax.random.split(jax.random.key(seed), 6)
    vectors = gaussian(key_of[0], (VECS, DIM), 1.0, 6.0, ((1, 32),))
    tiles = gaussian(key_of[1], (TILES, TILE * TILE), 0.05, 0.29882812, ((0, 32),))
    tile_rows = set_ends(jax.random.randint(key_of[2], (TILES,), 0, PIECE * N_BCOL // TILE), jax.random.fold_in(key_of[2], 1), 0, (PIECE * N_BCOL // TILE) - 1).astype(jnp.int32)
    tile_cols = set_ends(jax.random.randint(key_of[3], (TILES,), 0, PIECE * N_BROW // TILE), jax.random.fold_in(key_of[3], 1), 0, (PIECE * N_BROW // TILE) - 1).astype(jnp.int32)
    counts = draw_counts(jax.random.fold_in(key_of[5], 71), 0)
    return {"vectors": vectors, "tiles": tiles, "tile_rows": tile_rows, "tile_cols": tile_cols, "counts": counts}


def reference(vectors, tiles, tile_rows, tile_cols, counts):
    lane = jnp.arange(TILE, dtype=jnp.int32)
    slot_ids = jnp.arange(TMAX, dtype=jnp.int32)
    source = vectors.astype(jnp.float32)

    def one_block(carry, index):
        brow_id = index // N_BCOL
        bcol_id = index % N_BCOL
        start = (index * TMAX).astype(jnp.int32)
        blocks = lax.dynamic_slice_in_dim(tiles, start, TMAX, 0).reshape(TMAX, TILE, TILE).astype(jnp.float32)
        rows_here = lax.dynamic_slice_in_dim(tile_rows, start, TMAX, 0)
        cols_here = lax.dynamic_slice_in_dim(tile_cols, start, TMAX, 0)
        live = (slot_ids < counts[brow_id, bcol_id]).astype(jnp.float32)
        global_rows = brow_id * N_BCOL * PIECE + rows_here[:, None] * TILE + lane[None, :]
        offset = cols_here[:, None] * TILE + lane[None, :]
        global_cols = ((offset // PIECE) * N_BCOL + bcol_id) * PIECE + offset % PIECE
        at_cols = source[:, global_cols]
        at_rows = source[:, global_rows]
        forward = jnp.einsum('ktj,tij->kti', at_cols, blocks, precision=lax.Precision.HIGHEST) * live[None, :, None]
        backward = jnp.einsum('kti,tij->ktj', at_rows, blocks, precision=lax.Precision.HIGHEST) * live[None, :, None]
        carry = carry.at[:, global_rows].add(forward)
        carry = carry.at[:, global_cols].add(backward)
        return carry, None

    start_sum = jnp.zeros(vectors.shape, jnp.float32)
    result, _ = lax.scan(one_block, start_sum, jnp.arange(N_BROW * N_BCOL, dtype=jnp.int32))
    return result
```

```python
import jax
import jax.numpy as jnp
from jax import lax
from jax.sharding import PartitionSpec as P

TILE = 64


def partners(x, axis, size):
    return [x] + [lax.ppermute(x, axis, [(i, i ^ d) for i in range(size)]) for d in range(1, size)]


def exchange(parts, axis, size):
    return [parts[0]] + [
        lax.ppermute(parts[d], axis, [(i, i ^ d) for i in range(size)]) for d in range(1, size)
    ]


def body(vectors, tiles, tile_rows, tile_cols, counts):
    width = vectors.shape[0]
    piece = vectors.shape[1]
    slots = tiles.shape[0]
    side = TILE
    n_rows_axis = lax.axis_size("brow")
    n_cols_axis = lax.axis_size("bcol")
    per_piece = piece // side
    row_tiles = per_piece * n_cols_axis
    col_tiles = per_piece * n_rows_axis
    tile_rows = tile_rows ^ (lax.axis_index("bcol") * per_piece)
    tile_cols = tile_cols ^ (lax.axis_index("brow") * per_piece)
    row_pieces = partners(vectors, "bcol", n_cols_axis)
    col_pieces = partners(vectors, "brow", n_rows_axis)
    live = (jnp.arange(slots, dtype=jnp.int32) < counts[0, 0]).astype(jnp.bfloat16)
    row_hot = (tile_rows[:, None] == jnp.arange(row_tiles, dtype=jnp.int32)[None, :]).astype(
        jnp.bfloat16
    ) * live[:, None]
    col_hot = (tile_cols[:, None] == jnp.arange(col_tiles, dtype=jnp.int32)[None, :]).astype(
        jnp.bfloat16
    ) * live[:, None]
    row_hot_wide = row_hot.astype(jnp.float32)
    col_hot_wide = col_hot.astype(jnp.float32)
    blocks = tiles.reshape(slots, side, side)

    row_seg = jnp.concatenate(row_pieces, axis=1).reshape(width, row_tiles, side)
    at_rows = jnp.einsum(
        "tr,kri->tki", row_hot, row_seg, preferred_element_type=jnp.float32
    ).astype(jnp.bfloat16)
    backward = jnp.einsum("tki,tij->tkj", at_rows, blocks, preferred_element_type=jnp.float32)
    partial_cols = jnp.einsum(
        "tc,tkj->kcj", col_hot_wide, backward, precision=lax.Precision.HIGHEST
    ).reshape(width, col_tiles * side)
    from_cols = exchange(jnp.split(partial_cols, n_rows_axis, axis=1), "brow", n_rows_axis)

    col_seg = jnp.concatenate(col_pieces, axis=1).reshape(width, col_tiles, side)
    at_cols = jnp.einsum(
        "tc,kcj->tkj", col_hot, col_seg, preferred_element_type=jnp.float32
    ).astype(jnp.bfloat16)
    forward = jnp.einsum("tkj,tij->tki", at_cols, blocks, preferred_element_type=jnp.float32)
    partial_rows = jnp.einsum(
        "tr,tki->kri", row_hot_wide, forward, precision=lax.Precision.HIGHEST
    ).reshape(width, row_tiles * side)
    from_rows = exchange(jnp.split(partial_rows, n_cols_axis, axis=1), "bcol", n_cols_axis)
    return sum(from_rows) + sum(from_cols)


def solution(mesh):
    return jax.shard_map(
        body,
        mesh=mesh,
        in_specs=(
            P(None, ("brow", "bcol")),
            P(("brow", "bcol"), None),
            P(("brow", "bcol")),
            P(("brow", "bcol")),
            P("brow", "bcol"),
        ),
        out_specs=P(None, ("brow", "bcol")),
        check_vma=False,
    )
```

```python
import jax
import jax.numpy as jnp
from jax import lax
from jax.sharding import PartitionSpec as P

TILE = 64


def gather(x, axis, size):
    return lax.all_to_all(jnp.broadcast_to(x[None], (size,) + x.shape), axis, 0, 0)


def exchange(x, axis, size):
    width = x.shape[0]
    parts = x.reshape(width, size, -1).swapaxes(0, 1)
    return lax.all_to_all(parts, axis, 0, 0).sum(axis=0)


def body(vectors, tiles, tile_rows, tile_cols, counts):
    width = vectors.shape[0]
    piece = vectors.shape[1]
    slots = tiles.shape[0]
    side = TILE
    n_rows_axis = lax.axis_size("brow")
    n_cols_axis = lax.axis_size("bcol")
    per_piece = piece // side
    row_tiles = per_piece * n_cols_axis
    col_tiles = per_piece * n_rows_axis
    row_pieces = gather(vectors, "bcol", n_cols_axis)
    col_pieces = gather(vectors, "brow", n_rows_axis)
    live = (jnp.arange(slots, dtype=jnp.int32) < counts[0, 0]).astype(jnp.bfloat16)
    row_hot = (tile_rows[:, None] == jnp.arange(row_tiles, dtype=jnp.int32)[None, :]).astype(
        jnp.bfloat16
    ) * live[:, None]
    col_hot = (tile_cols[:, None] == jnp.arange(col_tiles, dtype=jnp.int32)[None, :]).astype(
        jnp.bfloat16
    ) * live[:, None]
    row_hot_wide = row_hot.astype(jnp.float32)
    col_hot_wide = col_hot.astype(jnp.float32)
    blocks = tiles.reshape(slots, side, side)

    row_seg = row_pieces.swapaxes(0, 1).reshape(width, row_tiles, side)
    at_rows = jnp.einsum(
        "tr,kri->tki", row_hot, row_seg, preferred_element_type=jnp.float32
    ).astype(jnp.bfloat16)
    backward = jnp.einsum("tki,tij->tkj", at_rows, blocks, preferred_element_type=jnp.float32)
    partial_cols = jnp.einsum(
        "tc,tkj->kcj", col_hot_wide, backward, precision=lax.Precision.HIGHEST
    ).reshape(width, col_tiles * side)
    from_cols = exchange(partial_cols, "brow", n_rows_axis)

    col_seg = col_pieces.swapaxes(0, 1).reshape(width, col_tiles, side)
    at_cols = jnp.einsum(
        "tc,kcj->tkj", col_hot, col_seg, preferred_element_type=jnp.float32
    ).astype(jnp.bfloat16)
    forward = jnp.einsum("tkj,tij->tki", at_cols, blocks, preferred_element_type=jnp.float32)
    partial_rows = jnp.einsum(
        "tr,tki->kri", row_hot_wide, forward, precision=lax.Precision.HIGHEST
    ).reshape(width, row_tiles * side)
    from_rows = exchange(partial_rows, "bcol", n_cols_axis)
    return from_rows + from_cols


def solution(mesh):
    return jax.shard_map(
        body,
        mesh=mesh,
        in_specs=(
            P(None, ("brow", "bcol")),
            P(("brow", "bcol"), None),
            P(("brow", "bcol")),
            P(("brow", "bcol")),
            P("brow", "bcol"),
        ),
        out_specs=P(None, ("brow", "bcol")),
        check_vma=False,
    )
```

```python
import functools

import jax
import jax.numpy as jnp
import numpy as np
from jax import lax
from jax.experimental import pallas as pl
from jax.experimental.pallas import tpu as pltpu
from jax.sharding import PartitionSpec as P

TILE = 64
LANES = 128
HALF = TILE // 2
GROUP = LANES // HALF
F32 = jnp.float32
BF16 = jnp.bfloat16
VMEM = pl.BlockSpec(memory_space=pltpu.VMEM)
SMEM = pl.BlockSpec(memory_space=pltpu.SMEM)
PARAMS = pltpu.CompilerParams(vmem_limit_bytes=48 * 1024 * 1024)


def row_spread():
    out = np.zeros((LANES, 2, 2, GROUP, HALF), np.float32)
    for q in range(2):
        for e in range(2):
            for m in range(HALF):
                out[q * TILE + 2 * m + e, q, e, :, m] = 1
    return jnp.asarray(out.reshape(LANES, 4 * LANES), BF16)


def col_spread():
    out = np.zeros((LANES, 2, 2, 2, TILE), np.float32)
    for q in range(2):
        for e in range(2):
            for j in range(TILE):
                out[q * TILE + j, q, e, e, j] = 1
    return jnp.asarray(out.reshape(LANES, 4 * LANES), BF16)


def row_fold():
    return row_spread().T


def prep_kernel(tiles_ref, out_ref, wide):
    for b in range(tiles_ref.shape[0]):
        wide[b] = tiles_ref[b].astype(F32).reshape(HALF * 8, LANES)
        for s in range(8):
            out_ref[8 * b + s] = wide[b, pl.ds(s, HALF, stride=8), :].astype(BF16)


def prep(tiles):
    slots = tiles.shape[0]
    blocks = slots // 8
    steps = 4 if blocks % 4 == 0 else 1
    view = tiles.reshape(blocks, 8, HALF, LANES).swapaxes(1, 2)
    return pl.pallas_call(
        prep_kernel,
        grid=(steps,),
        in_specs=[pl.BlockSpec((blocks // steps, HALF, 8, LANES), lambda i: (i, 0, 0, 0))],
        out_specs=pl.BlockSpec((slots // steps, HALF, LANES), lambda i: (i, 0, 0)),
        out_shape=jax.ShapeDtypeStruct((slots, HALF, LANES), BF16),
        scratch_shapes=[pltpu.VMEM((blocks // steps, HALF * 8, LANES), F32)],
        compiler_params=PARAMS,
        cost_estimate=pl.CostEstimate(flops=0, bytes_accessed=8 * tiles.size, transcendentals=0),
        name="prep_tiles",
    )(view)


def build_table(piece_refs, spread, table):
    width, piece = piece_refs[0].shape
    pairs = piece // LANES
    for n, ref in enumerate(piece_refs):
        rows = jnp.concatenate([ref[:, p * LANES : (p + 1) * LANES] for p in range(pairs)], axis=0)
        wide = jnp.dot(rows, spread, preferred_element_type=F32)
        wide = wide.reshape(pairs, width, 4 * LANES)
        for q in range(2):
            both = jnp.concatenate(
                [wide[:, :, (2 * q + e) * LANES : (2 * q + e + 1) * LANES] for e in range(2)], axis=1
            ).astype(BF16)
            for p in range(pairs):
                table[n * 2 * pairs + 2 * p + q] = both[p]


def backward_kernel(n_in, n_out, rows_ref, cols_ref, count_ref, spread_ref, tiles_ref, *refs):
    pieces, (keep_ref, give_ref), (table, acc) = refs[:n_in], refs[n_in : n_in + 2], refs[n_in + 2 :]
    width, piece = pieces[0].shape
    per_piece = piece // TILE
    slots = tiles_ref.shape[0]
    build_table(pieces, spread_ref[...], table)
    acc[...] = jnp.zeros_like(acc)
    lane = lax.broadcasted_iota(jnp.int32, (2 * width, LANES), 1)
    masks = [(lane // HALF == s).astype(BF16) for s in range(GROUP)]
    low = lax.broadcasted_iota(jnp.int32, (width, LANES), 1) < TILE
    count = count_ref[0, 0]
    row_flip = lax.axis_index("bcol") * per_piece
    col_flip = lax.axis_index("brow") * per_piece
    spare = n_out * per_piece

    for g in range(slots // GROUP):
        at = [table[rows_ref[g * GROUP + s] ^ row_flip] * masks[s] for s in range(GROUP)]
        block = tiles_ref[g * GROUP : (g + 1) * GROUP].reshape(LANES, LANES)
        out = jnp.dot(jnp.concatenate(at, axis=0), block, preferred_element_type=F32)
        for s in range(GROUP):
            t = g * GROUP + s
            part = out[2 * width * s : 2 * width * (s + 1)]
            part = jnp.where(low, part[:width], part[width:])
            c = jnp.where(t < count, cols_ref[t] ^ col_flip, spare)
            acc[c] += part

    for n in range(n_out):
        dest = (keep_ref if n % 2 == 0 else give_ref).at[n // 2]
        for p in range(per_piece // 2):
            a = acc[n * per_piece + 2 * p]
            b = acc[n * per_piece + 2 * p + 1]
            dest[:, p * LANES : (p + 1) * LANES] = jnp.where(low, a, b) + pltpu.roll(
                jnp.where(low, b, a), TILE, 1
            )


def backward(row_pieces, tiles, tile_rows, tile_cols, counts, n_out):
    n_in = len(row_pieces)
    width, piece = row_pieces[0].shape
    per_piece = piece // TILE
    half = jax.ShapeDtypeStruct((n_out // 2, width, piece), F32)
    return pl.pallas_call(
        functools.partial(backward_kernel, n_in, n_out),
        in_specs=[SMEM] * 3 + [VMEM] * (2 + n_in),
        out_specs=[VMEM] * 2,
        out_shape=[half, half],
        scratch_shapes=[
            pltpu.VMEM((n_in * per_piece, 2 * width, LANES), BF16),
            pltpu.VMEM((n_out * per_piece + 1, width, LANES), F32),
        ],
        compiler_params=PARAMS,
        cost_estimate=pl.CostEstimate(
            flops=2 * tiles.size * 64, bytes_accessed=4 * tiles.size, transcendentals=0
        ),
        name="transpose_product",
    )(tile_rows, tile_cols, counts, row_spread(), tiles, *row_pieces)


def forward_kernel(n_in, n_out, rows_ref, cols_ref, count_ref, spread_ref, fold_ref, tiles_ref, *refs):
    pieces, outs, (table, acc) = refs[:n_in], refs[n_in : n_in + n_out], refs[n_in + n_out :]
    width, piece = pieces[0].shape
    per_piece = piece // TILE
    slots = tiles_ref.shape[0]
    build_table(pieces, spread_ref[...], table)
    acc[...] = jnp.zeros_like(acc)
    lane = lax.broadcasted_iota(jnp.int32, (2 * width, LANES), 1)
    masks = [lane // HALF == s for s in range(GROUP)]
    count = count_ref[0, 0]
    row_flip = lax.axis_index("bcol") * per_piece
    col_flip = lax.axis_index("brow") * per_piece
    spare = n_out * per_piece

    for g in range(slots // GROUP):
        at = [table[cols_ref[g * GROUP + s] ^ col_flip] for s in range(GROUP)]
        block = tiles_ref[g * GROUP : (g + 1) * GROUP].reshape(LANES, LANES)
        out = lax.dot_general(
            jnp.concatenate(at, axis=0),
            block,
            (((1,), (1,)), ((), ())),
            preferred_element_type=F32,
        )
        for s in range(GROUP):
            t = g * GROUP + s
            part = out[2 * width * s : 2 * width * (s + 1)]
            r = jnp.where(t < count, rows_ref[t] ^ row_flip, spare)
            acc[r] += jnp.where(masks[s], part, 0.0)

    fold = fold_ref[...]
    pairs = per_piece // 2
    for n in range(n_out):
        both = acc[n * per_piece : (n + 1) * per_piece].reshape(pairs, 4 * width, LANES)
        blocks = [
            both[:, x * width : (x + 1) * width, :].reshape(pairs * width, LANES) for x in range(4)
        ]
        wide = jnp.concatenate(blocks, axis=1)
        first = wide.astype(BF16)
        rest = (wide - first.astype(F32)).astype(BF16)
        out = jnp.dot(first, fold, preferred_element_type=F32)
        out = out + jnp.dot(rest, fold, preferred_element_type=F32)
        for p in range(pairs):
            outs[n][:, p * LANES : (p + 1) * LANES] = out[p * width : (p + 1) * width]


def forward(col_pieces, tiles, tile_rows, tile_cols, counts, n_out):
    n_in = len(col_pieces)
    width, piece = col_pieces[0].shape
    per_piece = piece // TILE
    return pl.pallas_call(
        functools.partial(forward_kernel, n_in, n_out),
        in_specs=[SMEM] * 3 + [VMEM] * (3 + n_in),
        out_specs=[VMEM] * n_out,
        out_shape=[jax.ShapeDtypeStruct((width, piece), F32)] * n_out,
        scratch_shapes=[
            pltpu.VMEM((n_in * per_piece, 2 * width, LANES), BF16),
            pltpu.VMEM((n_out * per_piece + 1, 2 * width, LANES), F32),
        ],
        compiler_params=PARAMS,
        cost_estimate=pl.CostEstimate(
            flops=2 * tiles.size * 64, bytes_accessed=4 * tiles.size, transcendentals=0
        ),
        name="forward_product",
    )(tile_rows, tile_cols, counts, col_spread(), row_fold(), tiles, *col_pieces)


def pair_sum_kernel(keep_ref, got_ref, *outs):
    for h, out in enumerate(outs):
        out[...] = keep_ref[h + 1] + got_ref[h + 1]


def pair_sum(keep, got):
    parts, width, piece = keep.shape
    return pl.pallas_call(
        pair_sum_kernel,
        in_specs=[VMEM] * 2,
        out_specs=[VMEM] * (parts - 1),
        out_shape=[jax.ShapeDtypeStruct((width, piece), F32)] * (parts - 1),
        compiler_params=PARAMS,
        name="core_pair_sum",
    )(keep, got)


def swap(x, axis, size, d):
    return lax.ppermute(x, axis, [(i, i ^ d) for i in range(size)])


def body(vectors, tiles, tile_rows, tile_cols, counts):
    n_rows = lax.axis_size("brow")
    n_cols = lax.axis_size("bcol")
    row_pieces = [vectors] + [swap(vectors, "bcol", n_cols, d) for d in range(1, n_cols)]
    same_core = [vectors] + [swap(vectors, "brow", n_rows, 2 * h) for h in range(1, n_rows // 2)]
    other_core = [swap(x, "brow", n_rows, 1) for x in same_core]
    col_pieces = [x for pair in zip(same_core, other_core) for x in pair]
    blocks = prep(tiles)

    keep, give = backward(row_pieces, blocks, tile_rows, tile_cols, counts, n_rows)
    got = swap(give, "brow", n_rows, 1)
    mine = forward(col_pieces, blocks, tile_rows, tile_cols, counts, n_cols)
    from_rows = [mine[0]] + [swap(mine[d], "bcol", n_cols, d) for d in range(1, n_cols)]
    sums = pair_sum(keep, got)
    from_cols = [keep[0], got[0]] + [swap(x, "brow", n_rows, 2 * (h + 1)) for h, x in enumerate(sums)]
    return sum(from_rows + from_cols)


def solution(mesh):
    return jax.shard_map(
        body,
        mesh=mesh,
        in_specs=(
            P(None, ("brow", "bcol")),
            P(("brow", "bcol"), None),
            P(("brow", "bcol")),
            P(("brow", "bcol")),
            P("brow", "bcol"),
        ),
        out_specs=P(None, ("brow", "bcol")),
        check_vma=False,
    )
```

```python
import jax
import jax.numpy as jnp
import numpy as np
from jax import lax
from jax.experimental import pallas as pl
from jax.experimental.pallas import tpu as pltpu
from jax.sharding import PartitionSpec as P

TILE = 64
LANES = 128
HALF = TILE // 2
GROUP = LANES // HALF
F32 = jnp.float32
BF16 = jnp.bfloat16
VMEM = pl.BlockSpec(memory_space=pltpu.VMEM)
ANY = pl.BlockSpec(memory_space=pl.ANY)
SMEM = pl.BlockSpec(memory_space=pltpu.SMEM)
PARAMS = pltpu.CompilerParams(vmem_limit_bytes=48 * 1024 * 1024)


def row_spread():
    out = np.zeros((LANES, 2, 2, GROUP, HALF), np.float32)
    for q in range(2):
        for e in range(2):
            for m in range(HALF):
                out[q * TILE + 2 * m + e, q, e, :, m] = 1
    return jnp.asarray(out.reshape(LANES, 4 * LANES), BF16)


def col_spread():
    out = np.zeros((LANES, 2, 2, 2, TILE), np.float32)
    for q in range(2):
        for e in range(2):
            for j in range(TILE):
                out[q * TILE + j, q, e, e, j] = 1
    return jnp.asarray(out.reshape(LANES, 4 * LANES), BF16)


def row_fold():
    return row_spread().T


def prep_kernel(tiles_ref, out_ref, wide):
    for b in range(tiles_ref.shape[0]):
        wide[b] = tiles_ref[b].astype(F32).reshape(HALF * 8, LANES)
        for s in range(8):
            out_ref[8 * b + s] = wide[b, pl.ds(s, HALF, stride=8), :].astype(BF16)


def prep(tiles):
    slots = tiles.shape[0]
    blocks = slots // 8
    view = tiles.reshape(blocks, 8, HALF, LANES).swapaxes(1, 2)
    return pl.pallas_call(
        prep_kernel,
        in_specs=[VMEM],
        out_specs=VMEM,
        out_shape=jax.ShapeDtypeStruct((slots, HALF, LANES), BF16),
        scratch_shapes=[pltpu.VMEM((blocks, HALF * 8, LANES), F32)],
        compiler_params=PARAMS,
        cost_estimate=pl.CostEstimate(flops=0, bytes_accessed=4 * tiles.size, transcendentals=0),
        name="prep_tiles",
    )(view)


def build_table(pieces, spread, table):
    width, piece = pieces[0].shape
    pairs = piece // LANES
    for n, ref in enumerate(pieces):
        rows = jnp.concatenate([ref[:, p * LANES : (p + 1) * LANES] for p in range(pairs)], axis=0)
        wide = jnp.dot(rows, spread, preferred_element_type=F32)
        wide = wide.reshape(pairs, width, 4 * LANES)
        for q in range(2):
            both = jnp.concatenate(
                [wide[:, :, (2 * q + e) * LANES : (2 * q + e + 1) * LANES] for e in range(2)], axis=1
            ).astype(BF16)
            for p in range(pairs):
                table[n * 2 * pairs + 2 * p + q] = both[p]


def backward_kernel(
    rows_ref, cols_ref, count_ref, spread_ref, tiles_ref, seg_ref, after_ref, keep_ref, give_ref, table, acc
):
    pieces = [seg_ref.at[n] for n in range(seg_ref.shape[0])]
    n_out = 2 * keep_ref.shape[0]
    width, piece = pieces[0].shape
    per_piece = piece // TILE
    slots = tiles_ref.shape[0]
    build_table(pieces, spread_ref[...], table)
    acc[...] = jnp.zeros_like(acc)
    lane = lax.broadcasted_iota(jnp.int32, (2 * width, LANES), 1)
    masks = [(lane // HALF == s).astype(BF16) for s in range(GROUP)]
    low = lax.broadcasted_iota(jnp.int32, (width, LANES), 1) < TILE
    count = count_ref[0, 0]
    row_flip = lax.axis_index("bcol") * per_piece
    col_flip = lax.axis_index("brow") * per_piece
    spare = n_out * per_piece

    for g in range(slots // GROUP):
        at = [table[rows_ref[g * GROUP + s] ^ row_flip] * masks[s] for s in range(GROUP)]
        block = tiles_ref[g * GROUP : (g + 1) * GROUP].reshape(LANES, LANES)
        out = jnp.dot(jnp.concatenate(at, axis=0), block, preferred_element_type=F32)
        for s in range(GROUP):
            t = g * GROUP + s
            part = out[2 * width * s : 2 * width * (s + 1)]
            part = jnp.where(low, part[:width], part[width:])
            c = jnp.where(t < count, cols_ref[t] ^ col_flip, spare)
            acc[c] += part

    for n in range(n_out):
        dest = (keep_ref if n % 2 == 0 else give_ref).at[n // 2]
        for p in range(per_piece // 2):
            a = acc[n * per_piece + 2 * p]
            b = acc[n * per_piece + 2 * p + 1]
            dest[:, p * LANES : (p + 1) * LANES] = jnp.where(low, a, b) + pltpu.roll(
                jnp.where(low, b, a), TILE, 1
            )


def backward(segment, tiles, tile_rows, tile_cols, counts, n_out, after):
    n_in, width, piece = segment.shape
    per_piece = piece // TILE
    half = jax.ShapeDtypeStruct((n_out // 2, width, piece), F32)
    return pl.pallas_call(
        backward_kernel,
        in_specs=[SMEM] * 3 + [VMEM] * 3 + [ANY],
        out_specs=[VMEM] * 2,
        out_shape=[half, half],
        scratch_shapes=[
            pltpu.VMEM((n_in * per_piece, 2 * width, LANES), BF16),
            pltpu.VMEM((n_out * per_piece + 1, width, LANES), F32),
        ],
        compiler_params=PARAMS,
        cost_estimate=pl.CostEstimate(
            flops=2 * tiles.size * 64, bytes_accessed=4 * tiles.size, transcendentals=0
        ),
        name="transpose_product",
    )(tile_rows, tile_cols, counts, row_spread(), tiles, segment, after)


def forward_kernel(
    rows_ref,
    cols_ref,
    count_ref,
    spread_ref,
    fold_ref,
    tiles_ref,
    same_ref,
    other_ref,
    after_ref,
    keep_ref,
    give_ref,
    table,
    acc,
):
    pieces = [ref.at[h] for h in range(same_ref.shape[0]) for ref in (same_ref, other_ref)]
    n_out = 2 * keep_ref.shape[0]
    width, piece = pieces[0].shape
    per_piece = piece // TILE
    slots = tiles_ref.shape[0]
    build_table(pieces, spread_ref[...], table)
    acc[...] = jnp.zeros_like(acc)
    lane = lax.broadcasted_iota(jnp.int32, (2 * width, LANES), 1)
    masks = [lane // HALF == s for s in range(GROUP)]
    count = count_ref[0, 0]
    row_flip = lax.axis_index("bcol") * per_piece
    col_flip = lax.axis_index("brow") * per_piece
    spare = n_out * per_piece

    for g in range(slots // GROUP):
        at = [table[cols_ref[g * GROUP + s] ^ col_flip] for s in range(GROUP)]
        block = tiles_ref[g * GROUP : (g + 1) * GROUP].reshape(LANES, LANES)
        out = lax.dot_general(
            jnp.concatenate(at, axis=0),
            block,
            (((1,), (1,)), ((), ())),
            preferred_element_type=F32,
        )
        for s in range(GROUP):
            t = g * GROUP + s
            part = out[2 * width * s : 2 * width * (s + 1)]
            r = jnp.where(t < count, rows_ref[t] ^ row_flip, spare)
            acc[r] += jnp.where(masks[s], part, 0.0)

    fold = fold_ref[...]
    pairs = per_piece // 2
    for n in range(n_out):
        both = acc[n * per_piece : (n + 1) * per_piece].reshape(pairs, 4 * width, LANES)
        blocks = [
            both[:, x * width : (x + 1) * width, :].reshape(pairs * width, LANES) for x in range(4)
        ]
        wide = jnp.concatenate(blocks, axis=1)
        first = wide.astype(BF16)
        rest = (wide - first.astype(F32)).astype(BF16)
        out = jnp.dot(first, fold, preferred_element_type=F32)
        out = out + jnp.dot(rest, fold, preferred_element_type=F32)
        dest = (keep_ref if n % 2 == 0 else give_ref).at[n // 2]
        for p in range(pairs):
            dest[:, p * LANES : (p + 1) * LANES] = out[p * width : (p + 1) * width]


def forward(same, other, tiles, tile_rows, tile_cols, counts, n_out, after):
    n_chips, width, piece = same.shape
    per_piece = piece // TILE
    half = jax.ShapeDtypeStruct((n_out // 2, width, piece), F32)
    return pl.pallas_call(
        forward_kernel,
        in_specs=[SMEM] * 3 + [VMEM] * 5 + [ANY],
        out_specs=[VMEM] * 2,
        out_shape=[half, half],
        scratch_shapes=[
            pltpu.VMEM((2 * n_chips * per_piece, 2 * width, LANES), BF16),
            pltpu.VMEM((n_out * per_piece + 1, 2 * width, LANES), F32),
        ],
        compiler_params=PARAMS,
        cost_estimate=pl.CostEstimate(
            flops=2 * tiles.size * 64, bytes_accessed=4 * tiles.size, transcendentals=0
        ),
        name="forward_product",
    )(tile_rows, tile_cols, counts, col_spread(), row_fold(), tiles, same, other, after)


def stack_kernel(*refs):
    out_ref, at = refs[-1], 0
    for ref in refs[:-2]:
        if len(ref.shape) == 2:
            out_ref[at] = ref[...]
            at += 1
        else:
            out_ref[at : at + ref.shape[0]] = ref[...]
            at += ref.shape[0]


def stack(*parts, after):
    total = sum(x.shape[0] if x.ndim == 3 else 1 for x in parts)
    return pl.pallas_call(
        stack_kernel,
        in_specs=[VMEM] * len(parts) + [ANY],
        out_specs=VMEM,
        out_shape=jax.ShapeDtypeStruct((total,) + parts[0].shape[-2:], parts[0].dtype),
        compiler_params=PARAMS,
        name="stack_pieces",
    )(*parts, after)


def pair_sum_kernel(keep_ref, got_ref, *outs):
    for h, out in enumerate(outs):
        out[...] = keep_ref[h + 1] + got_ref[h + 1]


def pair_sum(keep, got):
    parts, width, piece = keep.shape
    return pl.pallas_call(
        pair_sum_kernel,
        in_specs=[VMEM] * 2,
        out_specs=[VMEM] * (parts - 1),
        out_shape=[jax.ShapeDtypeStruct((width, piece), F32)] * (parts - 1),
        compiler_params=PARAMS,
        name="core_pair_sum",
    )(keep, got)


def split_sum_kernel(keep_ref, got_ref, after_ref, next_keep, next_give):
    for h in range(next_keep.shape[0]):
        next_keep[h] = keep_ref[2 * h] + got_ref[2 * h]
        next_give[h] = keep_ref[2 * h + 1] + got_ref[2 * h + 1]


def split_sum(keep, got, after):
    parts, width, piece = keep.shape
    half = jax.ShapeDtypeStruct((parts // 2, width, piece), F32)
    return pl.pallas_call(
        split_sum_kernel,
        in_specs=[VMEM] * 2 + [ANY],
        out_specs=[VMEM] * 2,
        out_shape=[half, half],
        compiler_params=PARAMS,
        name="halving_sum",
    )(keep, got, after)


def sum_kernel(*refs):
    total = refs[0][...]
    for ref in refs[1:-1]:
        total = total + ref[...]
    refs[-1][...] = total


def sum_pieces(*parts):
    return pl.pallas_call(
        sum_kernel,
        in_specs=[VMEM] * len(parts),
        out_specs=VMEM,
        out_shape=jax.ShapeDtypeStruct(parts[0].shape, F32),
        compiler_params=PARAMS,
        name="sum_pieces",
    )(*parts)


def swap(x, axis, size, d):
    return lax.ppermute(x, axis, [(i, i ^ d) for i in range(size)])


def body(vectors, tiles, tile_rows, tile_cols, counts):
    n_rows = lax.axis_size("brow")
    n_cols = lax.axis_size("bcol")
    chips = [swap(vectors, "brow", n_rows, 2 * h) for h in range(1, n_rows // 2)]
    row_seg, d = vectors, 1
    while d < n_cols:
        row_seg = stack(row_seg, swap(row_seg, "bcol", n_cols, d), after=chips[0])
        d *= 2
    blocks = prep(tiles)
    same = stack(vectors, *chips, after=blocks)
    other = swap(same, "brow", n_rows, 1)

    col_keep, col_give = backward(row_seg, blocks, tile_rows, tile_cols, counts, n_rows, same)
    row_keep, give = forward(same, other, blocks, tile_rows, tile_cols, counts, n_cols, col_give)
    col_got = swap(col_give, "brow", n_rows, 1)
    sums = pair_sum(col_keep, col_got)
    from_chips = [swap(x, "brow", n_rows, 2 * (h + 1)) for h, x in enumerate(sums)]
    row_got, d = swap(give, "bcol", n_cols, 1), 2
    while d < n_cols:
        row_keep, give = split_sum(row_keep, row_got, sums[0])
        row_got = swap(give, "bcol", n_cols, d)
        d *= 2
    total = sum_pieces(col_keep[0] + col_got[0], *from_chips)
    return total + (row_keep[0] + row_got[0])


def solution(mesh):
    return jax.shard_map(
        body,
        mesh=mesh,
        in_specs=(
            P(None, ("brow", "bcol")),
            P(("brow", "bcol"), None),
            P(("brow", "bcol")),
            P(("brow", "bcol")),
            P("brow", "bcol"),
        ),
        out_specs=P(None, ("brow", "bcol")),
        check_vma=False,
    )
```

```python
import functools

import jax
import jax.numpy as jnp
import numpy as np
from jax import lax
from jax.experimental import pallas as pl
from jax.experimental.pallas import tpu as pltpu
from jax.sharding import PartitionSpec as P

TILE = 64
LANES = 128
HALF = TILE // 2
GROUP = LANES // HALF
F32 = jnp.float32
BF16 = jnp.bfloat16
VMEM = pl.BlockSpec(memory_space=pltpu.VMEM)
ANY = pl.BlockSpec(memory_space=pl.ANY)
SMEM = pl.BlockSpec(memory_space=pltpu.SMEM)
PARAMS = pltpu.CompilerParams(vmem_limit_bytes=48 * 1024 * 1024)


def row_spread():
    out = np.zeros((LANES, 2, 2, GROUP, HALF), np.float32)
    for q in range(2):
        for e in range(2):
            for m in range(HALF):
                out[q * TILE + 2 * m + e, q, e, :, m] = 1
    return jnp.asarray(out.reshape(LANES, 4 * LANES), BF16)


def col_spread():
    out = np.zeros((LANES, 2, 2, 2, TILE), np.float32)
    for q in range(2):
        for e in range(2):
            for j in range(TILE):
                out[q * TILE + j, q, e, e, j] = 1
    return jnp.asarray(out.reshape(LANES, 4 * LANES), BF16)


def row_fold():
    return row_spread().T


def prep_kernel(tiles_ref, out_ref, wide):
    for b in range(tiles_ref.shape[0]):
        wide[b] = tiles_ref[b].astype(F32).reshape(HALF * 8, LANES)
        for s in range(8):
            out_ref[8 * b + s] = wide[b, pl.ds(s, HALF, stride=8), :].astype(BF16)


def prep(tiles):
    slots = tiles.shape[0]
    blocks = slots // 8
    view = tiles.reshape(blocks, 8, HALF, LANES).swapaxes(1, 2)
    return pl.pallas_call(
        prep_kernel,
        in_specs=[VMEM],
        out_specs=VMEM,
        out_shape=jax.ShapeDtypeStruct((slots, HALF, LANES), BF16),
        scratch_shapes=[pltpu.VMEM((blocks, HALF * 8, LANES), F32)],
        compiler_params=PARAMS,
        cost_estimate=pl.CostEstimate(flops=0, bytes_accessed=4 * tiles.size, transcendentals=0),
        name="prep_tiles",
    )(view)


def doubled(size):
    order, d = [0], size // 2
    while d > 1:
        order += [x ^ d for x in order]
        d //= 2
    return order


def build_table(pieces, spread, table):
    width, piece = pieces[0][1].shape
    pairs = piece // LANES
    for n, ref in pieces:
        rows = jnp.concatenate([ref[:, p * LANES : (p + 1) * LANES] for p in range(pairs)], axis=0)
        wide = jnp.dot(rows, spread, preferred_element_type=F32)
        wide = wide.reshape(pairs, width, 4 * LANES)
        for q in range(2):
            both = jnp.concatenate(
                [wide[:, :, (2 * q + e) * LANES : (2 * q + e + 1) * LANES] for e in range(2)], axis=1
            ).astype(BF16)
            for p in range(pairs):
                table[n * 2 * pairs + 2 * p + q] = both[p]


def backward_kernel(n_in, rows_ref, cols_ref, count_ref, spread_ref, tiles_ref, *refs):
    pieces = list(enumerate(refs[:n_in]))
    _, keep_ref, give_ref, table, acc = refs[n_in:]
    n_out = 2 * keep_ref.shape[0]
    width, piece = pieces[0][1].shape
    per_piece = piece // TILE
    slots = tiles_ref.shape[0]
    build_table(pieces, spread_ref[...], table)
    acc[...] = jnp.zeros_like(acc)
    lane = lax.broadcasted_iota(jnp.int32, (2 * width, LANES), 1)
    masks = [(lane // HALF == s).astype(BF16) for s in range(GROUP)]
    low = lax.broadcasted_iota(jnp.int32, (width, LANES), 1) < TILE
    count = count_ref[0, 0]
    row_flip = lax.axis_index("bcol") * per_piece
    col_flip = lax.axis_index("brow") * per_piece
    spare = n_out * per_piece

    for g in range(slots // GROUP):
        at = [table[rows_ref[g * GROUP + s] ^ row_flip] * masks[s] for s in range(GROUP)]
        block = tiles_ref[g * GROUP : (g + 1) * GROUP].reshape(LANES, LANES)
        out = jnp.dot(jnp.concatenate(at, axis=0), block, preferred_element_type=F32)
        for s in range(GROUP):
            t = g * GROUP + s
            part = out[2 * width * s : 2 * width * (s + 1)]
            part = jnp.where(low, part[:width], part[width:])
            c = jnp.where(t < count, cols_ref[t] ^ col_flip, spare)
            acc[c] += part

    for n in range(n_out):
        dest = (keep_ref if n % 2 == 0 else give_ref).at[n // 2]
        for p in range(per_piece // 2):
            a = acc[n * per_piece + 2 * p]
            b = acc[n * per_piece + 2 * p + 1]
            dest[:, p * LANES : (p + 1) * LANES] = jnp.where(low, a, b) + pltpu.roll(
                jnp.where(low, b, a), TILE, 1
            )


def backward(pieces, tiles, tile_rows, tile_cols, counts, n_out, after):
    n_in = len(pieces)
    width, piece = pieces[0].shape
    per_piece = piece // TILE
    half = jax.ShapeDtypeStruct((n_out // 2, width, piece), F32)
    return pl.pallas_call(
        functools.partial(backward_kernel, n_in),
        in_specs=[SMEM] * 3 + [VMEM] * (2 + n_in) + [ANY],
        out_specs=[VMEM] * 2,
        out_shape=[half, half],
        scratch_shapes=[
            pltpu.VMEM((n_in * per_piece, 2 * width, LANES), BF16),
            pltpu.VMEM((n_out * per_piece + 1, width, LANES), F32),
        ],
        compiler_params=PARAMS,
        cost_estimate=pl.CostEstimate(
            flops=2 * tiles.size * 64, bytes_accessed=12 * tiles.size, transcendentals=0
        ),
        name="transpose_product",
    )(tile_rows, tile_cols, counts, row_spread(), tiles, *pieces, after)


def forward_kernel(
    rows_ref,
    cols_ref,
    count_ref,
    spread_ref,
    fold_ref,
    tiles_ref,
    same_ref,
    other_ref,
    after_ref,
    *refs,
):
    outs, table, acc = refs[:-2], refs[-2], refs[-1]
    pieces = []
    for at, d in enumerate(doubled(2 * same_ref.shape[0])):
        pieces += [(d, same_ref.at[at]), (d + 1, other_ref.at[at])]
    n_out = len(outs)
    width, piece = pieces[0][1].shape
    per_piece = piece // TILE
    slots = tiles_ref.shape[0]
    build_table(pieces, spread_ref[...], table)
    acc[...] = jnp.zeros_like(acc)
    lane = lax.broadcasted_iota(jnp.int32, (2 * width, LANES), 1)
    masks = [lane // HALF == s for s in range(GROUP)]
    count = count_ref[0, 0]
    row_flip = lax.axis_index("bcol") * per_piece
    col_flip = lax.axis_index("brow") * per_piece
    spare = n_out * per_piece

    for g in range(slots // GROUP):
        at = [table[cols_ref[g * GROUP + s] ^ col_flip] for s in range(GROUP)]
        block = tiles_ref[g * GROUP : (g + 1) * GROUP].reshape(LANES, LANES)
        out = lax.dot_general(
            jnp.concatenate(at, axis=0),
            block,
            (((1,), (1,)), ((), ())),
            preferred_element_type=F32,
        )
        for s in range(GROUP):
            t = g * GROUP + s
            part = out[2 * width * s : 2 * width * (s + 1)]
            r = jnp.where(t < count, rows_ref[t] ^ row_flip, spare)
            acc[r] += jnp.where(masks[s], part, 0.0)

    fold = fold_ref[...]
    pairs = per_piece // 2
    for n in range(n_out):
        both = acc[n * per_piece : (n + 1) * per_piece].reshape(pairs, 4 * width, LANES)
        blocks = [
            both[:, x * width : (x + 1) * width, :].reshape(pairs * width, LANES) for x in range(4)
        ]
        wide = jnp.concatenate(blocks, axis=1)
        first = wide.astype(BF16)
        rest = (wide - first.astype(F32)).astype(BF16)
        out = jnp.dot(first, fold, preferred_element_type=F32)
        out = out + jnp.dot(rest, fold, preferred_element_type=F32)
        for p in range(pairs):
            outs[n][:, p * LANES : (p + 1) * LANES] = out[p * width : (p + 1) * width]


def forward(same, other, tiles, tile_rows, tile_cols, counts, n_out, after):
    n_chips, width, piece = same.shape
    per_piece = piece // TILE
    return pl.pallas_call(
        forward_kernel,
        in_specs=[SMEM] * 3 + [VMEM] * 5 + [ANY],
        out_specs=[VMEM] * n_out,
        out_shape=[jax.ShapeDtypeStruct((width, piece), F32)] * n_out,
        scratch_shapes=[
            pltpu.VMEM((2 * n_chips * per_piece, 2 * width, LANES), BF16),
            pltpu.VMEM((n_out * per_piece + 1, 2 * width, LANES), F32),
        ],
        compiler_params=PARAMS,
        cost_estimate=pl.CostEstimate(
            flops=2 * tiles.size * 64, bytes_accessed=12 * tiles.size, transcendentals=0
        ),
        name="forward_product",
    )(tile_rows, tile_cols, counts, col_spread(), row_fold(), tiles, same, other, after)


def stack_kernel(n_after, *refs):
    out_ref, at = refs[-1], 0
    for ref in refs[: -1 - n_after]:
        if len(ref.shape) == 2:
            out_ref[at] = ref[...]
            at += 1
        else:
            out_ref[at : at + ref.shape[0]] = ref[...]
            at += ref.shape[0]


def stack(*parts, after=()):
    total = sum(x.shape[0] if x.ndim == 3 else 1 for x in parts)
    return pl.pallas_call(
        functools.partial(stack_kernel, len(after)),
        in_specs=[VMEM] * len(parts) + [ANY] * len(after),
        out_specs=VMEM,
        out_shape=jax.ShapeDtypeStruct((total,) + parts[0].shape[-2:], parts[0].dtype),
        compiler_params=PARAMS,
        name="stack_pieces",
    )(*parts, *after)


def split_sum_kernel(keep_ref, got_ref, after_ref, next_keep, next_give):
    for h in range(next_keep.shape[0]):
        next_keep[h] = keep_ref[2 * h] + got_ref[2 * h]
        next_give[h] = keep_ref[2 * h + 1] + got_ref[2 * h + 1]


def split_sum(keep, got, after):
    parts, width, piece = keep.shape
    half = jax.ShapeDtypeStruct((parts // 2, width, piece), F32)
    return pl.pallas_call(
        split_sum_kernel,
        in_specs=[VMEM] * 2 + [ANY],
        out_specs=[VMEM] * 2,
        out_shape=[half, half],
        compiler_params=PARAMS,
        name="halving_sum",
    )(keep, got, after)


def sum_kernel(*refs):
    total = refs[0][...]
    for ref in refs[1:-1]:
        total = total + ref[...]
    refs[-1][...] = total


def sum_pieces(*parts):
    return pl.pallas_call(
        sum_kernel,
        in_specs=[VMEM] * len(parts),
        out_specs=VMEM,
        out_shape=jax.ShapeDtypeStruct(parts[0].shape, F32),
        compiler_params=PARAMS,
        name="sum_pieces",
    )(*parts)


def swap(x, axis, size, d):
    return lax.ppermute(x, axis, [(i, i ^ d) for i in range(size)])


def body(vectors, tiles, tile_rows, tile_cols, counts):
    n_rows = lax.axis_size("brow")
    n_cols = lax.axis_size("bcol")
    own = stack(vectors)
    row_pieces = [own[0]] + [swap(vectors, "bcol", n_cols, d) for d in range(1, n_cols)]
    blocks = prep(tiles)
    same, got, d = own, swap(vectors, "brow", n_rows, n_rows // 2), n_rows // 2
    while d > 1:
        same = stack(same, got, after=(row_pieces[-1], blocks))
        d //= 2
        got = swap(same, "brow", n_rows, d)
    other = got

    keep, give = backward(row_pieces, blocks, tile_rows, tile_cols, counts, n_rows, other)
    mine = forward(same, other, blocks, tile_rows, tile_cols, counts, n_cols, give)
    got, d = swap(give, "brow", n_rows, 1), 2
    while d < n_rows:
        keep, give = split_sum(keep, got, mine[0])
        got = swap(give, "brow", n_rows, d)
        d *= 2
    from_rows = [swap(mine[d], "bcol", n_cols, d) for d in range(1, n_cols)]
    total = sum_pieces(mine[0], *from_rows)
    return total + (keep[0] + got[0])


def solution(mesh):
    return jax.shard_map(
        body,
        mesh=mesh,
        in_specs=(
            P(None, ("brow", "bcol")),
            P(("brow", "bcol"), None),
            P(("brow", "bcol")),
            P(("brow", "bcol")),
            P("brow", "bcol"),
        ),
        out_specs=P(None, ("brow", "bcol")),
        check_vma=False,
    )
```

```python
import functools

import jax
import jax.numpy as jnp
import numpy as np
from jax import lax
from jax.experimental import pallas as pl
from jax.experimental.pallas import tpu as pltpu
from jax.sharding import PartitionSpec as P

TILE = 64
LANES = 128
HALF = TILE // 2
GROUP = LANES // HALF
F32 = jnp.float32
BF16 = jnp.bfloat16
VMEM = pl.BlockSpec(memory_space=pltpu.VMEM)
ANY = pl.BlockSpec(memory_space=pl.ANY)
SMEM = pl.BlockSpec(memory_space=pltpu.SMEM)
PARAMS = pltpu.CompilerParams(vmem_limit_bytes=48 * 1024 * 1024)


def row_spread():
    out = np.zeros((LANES, 2, 2, GROUP, HALF), np.float32)
    for q in range(2):
        for e in range(2):
            for m in range(HALF):
                out[q * TILE + 2 * m + e, q, e, :, m] = 1
    return jnp.asarray(out.reshape(LANES, 4 * LANES), BF16)


def col_spread():
    out = np.zeros((LANES, 2, 2, 2, TILE), np.float32)
    for q in range(2):
        for e in range(2):
            for j in range(TILE):
                out[q * TILE + j, q, e, e, j] = 1
    return jnp.asarray(out.reshape(LANES, 4 * LANES), BF16)


def row_fold():
    return row_spread().T


def prep_kernel(tiles_ref, out_ref, wide):
    for b in range(tiles_ref.shape[0]):
        wide[b] = tiles_ref[b].astype(F32).reshape(HALF * 8, LANES)
        for s in range(8):
            out_ref[8 * b + s] = wide[b, pl.ds(s, HALF, stride=8), :].astype(BF16)


def prep(tiles):
    slots = tiles.shape[0]
    blocks = slots // 8
    view = tiles.reshape(blocks, 8, HALF, LANES).swapaxes(1, 2)
    return pl.pallas_call(
        prep_kernel,
        in_specs=[VMEM],
        out_specs=VMEM,
        out_shape=jax.ShapeDtypeStruct((slots, HALF, LANES), BF16),
        scratch_shapes=[pltpu.VMEM((blocks, HALF * 8, LANES), F32)],
        compiler_params=PARAMS,
        cost_estimate=pl.CostEstimate(flops=0, bytes_accessed=4 * tiles.size, transcendentals=0),
        name="prep_tiles",
    )(view)


def build_table(pieces, spread, table):
    width, piece = pieces[0].shape
    pairs = piece // LANES
    for n, ref in enumerate(pieces):
        rows = jnp.concatenate([ref[:, p * LANES : (p + 1) * LANES] for p in range(pairs)], axis=0)
        wide = jnp.dot(rows, spread, preferred_element_type=F32)
        wide = wide.reshape(pairs, width, 4 * LANES)
        for q in range(2):
            both = jnp.concatenate(
                [wide[:, :, (2 * q + e) * LANES : (2 * q + e + 1) * LANES] for e in range(2)], axis=1
            ).astype(BF16)
            for p in range(pairs):
                table[n * 2 * pairs + 2 * p + q] = both[p]


def backward_kernel(n_in, rows_ref, cols_ref, count_ref, spread_ref, tiles_ref, *refs):
    pieces = refs[:n_in]
    _, keep_ref, give_ref, table, acc = refs[n_in:]
    n_out = 2 * keep_ref.shape[0]
    width, piece = pieces[0].shape
    per_piece = piece // TILE
    slots = tiles_ref.shape[0]
    build_table(pieces, spread_ref[...], table)
    acc[...] = jnp.zeros_like(acc)
    lane = lax.broadcasted_iota(jnp.int32, (2 * width, LANES), 1)
    masks = [(lane // HALF == s).astype(BF16) for s in range(GROUP)]
    low = lax.broadcasted_iota(jnp.int32, (width, LANES), 1) < TILE
    count = count_ref[0, 0]
    row_flip = lax.axis_index("bcol") * per_piece
    col_flip = lax.axis_index("brow") * per_piece
    spare = n_out * per_piece

    for g in range(slots // GROUP):
        at = [table[rows_ref[g * GROUP + s] ^ row_flip] * masks[s] for s in range(GROUP)]
        block = tiles_ref[g * GROUP : (g + 1) * GROUP].reshape(LANES, LANES)
        out = jnp.dot(jnp.concatenate(at, axis=0), block, preferred_element_type=F32)
        for s in range(GROUP):
            t = g * GROUP + s
            part = out[2 * width * s : 2 * width * (s + 1)]
            part = jnp.where(low, part[:width], part[width:])
            c = jnp.where(t < count, cols_ref[t] ^ col_flip, spare)
            acc[c] += part

    for n in range(n_out):
        dest = (keep_ref if n % 2 == 0 else give_ref).at[n // 2]
        for p in range(per_piece // 2):
            a = acc[n * per_piece + 2 * p]
            b = acc[n * per_piece + 2 * p + 1]
            dest[:, p * LANES : (p + 1) * LANES] = jnp.where(low, a, b) + pltpu.roll(
                jnp.where(low, b, a), TILE, 1
            )


def backward(pieces, tiles, tile_rows, tile_cols, counts, n_out, after):
    n_in = len(pieces)
    width, piece = pieces[0].shape
    per_piece = piece // TILE
    half = jax.ShapeDtypeStruct((n_out // 2, width, piece), F32)
    return pl.pallas_call(
        functools.partial(backward_kernel, n_in),
        in_specs=[SMEM] * 3 + [VMEM] * (2 + n_in) + [ANY],
        out_specs=[VMEM] * 2,
        out_shape=[half, half],
        scratch_shapes=[
            pltpu.VMEM((n_in * per_piece, 2 * width, LANES), BF16),
            pltpu.VMEM((n_out * per_piece + 1, width, LANES), F32),
        ],
        compiler_params=PARAMS,
        cost_estimate=pl.CostEstimate(
            flops=2 * tiles.size * 64, bytes_accessed=4 * tiles.size, transcendentals=0
        ),
        name="transpose_product",
    )(tile_rows, tile_cols, counts, row_spread(), tiles, *pieces, after)


def forward_kernel(
    rows_ref,
    cols_ref,
    count_ref,
    spread_ref,
    fold_ref,
    tiles_ref,
    same_ref,
    other_ref,
    after_ref,
    keep_ref,
    give_ref,
    table,
    acc,
):
    pieces = [ref.at[h] for h in range(same_ref.shape[0]) for ref in (same_ref, other_ref)]
    n_out = 2 * keep_ref.shape[0]
    width, piece = pieces[0].shape
    per_piece = piece // TILE
    slots = tiles_ref.shape[0]
    build_table(pieces, spread_ref[...], table)
    acc[...] = jnp.zeros_like(acc)
    lane = lax.broadcasted_iota(jnp.int32, (2 * width, LANES), 1)
    masks = [lane // HALF == s for s in range(GROUP)]
    count = count_ref[0, 0]
    row_flip = lax.axis_index("bcol") * per_piece
    col_flip = lax.axis_index("brow") * per_piece
    spare = n_out * per_piece

    for g in range(slots // GROUP):
        at = [table[cols_ref[g * GROUP + s] ^ col_flip] for s in range(GROUP)]
        block = tiles_ref[g * GROUP : (g + 1) * GROUP].reshape(LANES, LANES)
        out = lax.dot_general(
            jnp.concatenate(at, axis=0),
            block,
            (((1,), (1,)), ((), ())),
            preferred_element_type=F32,
        )
        for s in range(GROUP):
            t = g * GROUP + s
            part = out[2 * width * s : 2 * width * (s + 1)]
            r = jnp.where(t < count, rows_ref[t] ^ row_flip, spare)
            acc[r] += jnp.where(masks[s], part, 0.0)

    fold = fold_ref[...]
    pairs = per_piece // 2
    for n in range(n_out):
        both = acc[n * per_piece : (n + 1) * per_piece].reshape(pairs, 4 * width, LANES)
        blocks = [
            both[:, x * width : (x + 1) * width, :].reshape(pairs * width, LANES) for x in range(4)
        ]
        wide = jnp.concatenate(blocks, axis=1)
        first = wide.astype(BF16)
        rest = (wide - first.astype(F32)).astype(BF16)
        out = jnp.dot(first, fold, preferred_element_type=F32)
        out = out + jnp.dot(rest, fold, preferred_element_type=F32)
        dest = (keep_ref if n % 2 == 0 else give_ref).at[n // 2]
        for p in range(pairs):
            dest[:, p * LANES : (p + 1) * LANES] = out[p * width : (p + 1) * width]


def forward(same, other, tiles, tile_rows, tile_cols, counts, n_out, after):
    n_chips, width, piece = same.shape
    per_piece = piece // TILE
    half = jax.ShapeDtypeStruct((n_out // 2, width, piece), F32)
    return pl.pallas_call(
        forward_kernel,
        in_specs=[SMEM] * 3 + [VMEM] * 5 + [ANY],
        out_specs=[VMEM] * 2,
        out_shape=[half, half],
        scratch_shapes=[
            pltpu.VMEM((2 * n_chips * per_piece, 2 * width, LANES), BF16),
            pltpu.VMEM((n_out * per_piece + 1, 2 * width, LANES), F32),
        ],
        compiler_params=PARAMS,
        cost_estimate=pl.CostEstimate(
            flops=2 * tiles.size * 64, bytes_accessed=4 * tiles.size, transcendentals=0
        ),
        name="forward_product",
    )(tile_rows, tile_cols, counts, col_spread(), row_fold(), tiles, same, other, after)


def stack_kernel(n_after, *refs):
    out_ref, at = refs[-1], 0
    for ref in refs[: -1 - n_after]:
        if len(ref.shape) == 2:
            out_ref[at] = ref[...]
            at += 1
        else:
            out_ref[at : at + ref.shape[0]] = ref[...]
            at += ref.shape[0]


def stack(*parts, after=()):
    total = sum(x.shape[0] if x.ndim == 3 else 1 for x in parts)
    return pl.pallas_call(
        functools.partial(stack_kernel, len(after)),
        in_specs=[VMEM] * len(parts) + [ANY] * len(after),
        out_specs=VMEM,
        out_shape=jax.ShapeDtypeStruct((total,) + parts[0].shape[-2:], parts[0].dtype),
        compiler_params=PARAMS,
        name="stack_pieces",
    )(*parts, *after)


def pair_sum_kernel(keep_ref, got_ref, *outs):
    for h, out in enumerate(outs):
        out[...] = keep_ref[h + 1] + got_ref[h + 1]


def pair_sum(keep, got):
    parts, width, piece = keep.shape
    return pl.pallas_call(
        pair_sum_kernel,
        in_specs=[VMEM] * 2,
        out_specs=[VMEM] * (parts - 1),
        out_shape=[jax.ShapeDtypeStruct((width, piece), F32)] * (parts - 1),
        compiler_params=PARAMS,
        name="core_pair_sum",
    )(keep, got)


def split_sum_kernel(keep_ref, got_ref, after_ref, next_keep, next_give):
    for h in range(next_keep.shape[0]):
        next_keep[h] = keep_ref[2 * h] + got_ref[2 * h]
        next_give[h] = keep_ref[2 * h + 1] + got_ref[2 * h + 1]


def split_sum(keep, got, after):
    parts, width, piece = keep.shape
    half = jax.ShapeDtypeStruct((parts // 2, width, piece), F32)
    return pl.pallas_call(
        split_sum_kernel,
        in_specs=[VMEM] * 2 + [ANY],
        out_specs=[VMEM] * 2,
        out_shape=[half, half],
        compiler_params=PARAMS,
        name="halving_sum",
    )(keep, got, after)


def sum_kernel(*refs):
    total = refs[0][...]
    for ref in refs[1:-1]:
        total = total + ref[...]
    refs[-1][...] = total


def sum_pieces(*parts):
    return pl.pallas_call(
        sum_kernel,
        in_specs=[VMEM] * len(parts),
        out_specs=VMEM,
        out_shape=jax.ShapeDtypeStruct(parts[0].shape, F32),
        compiler_params=PARAMS,
        name="sum_pieces",
    )(*parts)


def swap(x, axis, size, d):
    return lax.ppermute(x, axis, [(i, i ^ d) for i in range(size)])


def body(vectors, tiles, tile_rows, tile_cols, counts):
    n_rows = lax.axis_size("brow")
    n_cols = lax.axis_size("bcol")
    own = stack(vectors)
    chips = [swap(vectors, "brow", n_rows, 2 * h) for h in range(1, n_rows // 2)]
    row_pieces = [own[0]] + [swap(vectors, "bcol", n_cols, d) for d in range(1, n_cols)]
    blocks = prep(tiles)
    same = stack(own, *chips, after=(blocks, *row_pieces[1:]))
    other = swap(same, "brow", n_rows, 1)

    col_keep, col_give = backward(row_pieces, blocks, tile_rows, tile_cols, counts, n_rows, same)
    row_keep, give = forward(same, other, blocks, tile_rows, tile_cols, counts, n_cols, col_give)
    col_got = swap(col_give, "brow", n_rows, 1)
    sums = pair_sum(col_keep, col_got)
    from_chips = [swap(x, "brow", n_rows, 2 * (h + 1)) for h, x in enumerate(sums)]
    row_got, d = swap(give, "bcol", n_cols, 1), 2
    while d < n_cols:
        row_keep, give = split_sum(row_keep, row_got, sums[0])
        row_got = swap(give, "bcol", n_cols, d)
        d *= 2
    total = sum_pieces(col_keep[0] + col_got[0], *from_chips)
    return total + (row_keep[0] + row_got[0])


def solution(mesh):
    return jax.shard_map(
        body,
        mesh=mesh,
        in_specs=(
            P(None, ("brow", "bcol")),
            P(("brow", "bcol"), None),
            P(("brow", "bcol")),
            P(("brow", "bcol")),
            P("brow", "bcol"),
        ),
        out_specs=P(None, ("brow", "bcol")),
        check_vma=False,
    )
```

```python
import functools

import jax
import jax.numpy as jnp
import numpy as np
from jax import lax
from jax.experimental import pallas as pl
from jax.experimental.pallas import tpu as pltpu
from jax.sharding import PartitionSpec as P

TILE = 64
LANES = 128
HALF = TILE // 2
GROUP = LANES // HALF
STEPS = 32000.0
F32 = jnp.float32
BF16 = jnp.bfloat16
VMEM = pl.BlockSpec(memory_space=pltpu.VMEM)
ANY = pl.BlockSpec(memory_space=pl.ANY)
SMEM = pl.BlockSpec(memory_space=pltpu.SMEM)
PARAMS = pltpu.CompilerParams(vmem_limit_bytes=48 * 1024 * 1024)


def row_spread():
    out = np.zeros((LANES, 2, 2, GROUP, HALF), np.float32)
    for q in range(2):
        for e in range(2):
            for m in range(HALF):
                out[q * TILE + 2 * m + e, q, e, :, m] = 1
    return jnp.asarray(out.reshape(LANES, 4 * LANES), BF16)


def col_spread():
    out = np.zeros((LANES, 2, 2, 2, TILE), np.float32)
    for q in range(2):
        for e in range(2):
            for j in range(TILE):
                out[q * TILE + j, q, e, e, j] = 1
    return jnp.asarray(out.reshape(LANES, 4 * LANES), BF16)


def row_fold():
    return row_spread().T


def encode(values, out_ref):
    width, piece = values[0].shape[0], LANES * len(values)
    lane = lax.broadcasted_iota(jnp.int32, (width, LANES), 1)
    exponents = jnp.zeros((width, LANES), F32)
    for n, value in enumerate(values):
        top = jnp.max(jnp.abs(value), axis=1, keepdims=True)
        e = jnp.clip(jnp.ceil(jnp.log2(top)), -100.0, 100.0)
        exponents = jnp.where(lane == n, e, exponents)
        scaled = jnp.floor(value * (STEPS * jnp.exp2(-e)) + 0.5)
        out_ref[:, n * LANES : (n + 1) * LANES] = scaled.astype(jnp.int32).astype(jnp.int16)
    out_ref[:, piece:] = exponents.astype(jnp.int32).astype(jnp.int16)


def decode(ref):
    chunks = ref.shape[1] // LANES - 1
    exponents = ref[:, chunks * LANES :].astype(jnp.int32).astype(F32)
    scales = jnp.exp2(exponents) * (1.0 / STEPS)
    return [
        ref[:, n * LANES : (n + 1) * LANES].astype(jnp.int32).astype(F32) * scales[:, n : n + 1]
        for n in range(chunks)
    ]


def prep_kernel(tiles_ref, out_ref, wide):
    for b in range(tiles_ref.shape[0]):
        wide[b] = tiles_ref[b].astype(F32).reshape(HALF * 8, LANES)
        for s in range(8):
            out_ref[8 * b + s] = wide[b, pl.ds(s, HALF, stride=8), :].astype(BF16)


def prep(tiles):
    slots = tiles.shape[0]
    blocks = slots // 8
    view = tiles.reshape(blocks, 8, HALF, LANES).swapaxes(1, 2)
    return pl.pallas_call(
        prep_kernel,
        in_specs=[VMEM],
        out_specs=VMEM,
        out_shape=jax.ShapeDtypeStruct((slots, HALF, LANES), BF16),
        scratch_shapes=[pltpu.VMEM((blocks, HALF * 8, LANES), F32)],
        compiler_params=PARAMS,
        cost_estimate=pl.CostEstimate(flops=0, bytes_accessed=4 * tiles.size, transcendentals=0),
        name="prep_tiles",
    )(view)


def build_table(pieces, spread, table):
    width, piece = pieces[0].shape
    pairs = piece // LANES
    for n, ref in enumerate(pieces):
        rows = jnp.concatenate([ref[:, p * LANES : (p + 1) * LANES] for p in range(pairs)], axis=0)
        wide = jnp.dot(rows, spread, preferred_element_type=F32)
        wide = wide.reshape(pairs, width, 4 * LANES)
        for q in range(2):
            both = jnp.concatenate(
                [wide[:, :, (2 * q + e) * LANES : (2 * q + e + 1) * LANES] for e in range(2)], axis=1
            ).astype(BF16)
            for p in range(pairs):
                table[n * 2 * pairs + 2 * p + q] = both[p]


def backward_kernel(n_in, rows_ref, cols_ref, count_ref, spread_ref, tiles_ref, *refs):
    pieces = refs[:n_in]
    _, keep_ref, give_ref, table, acc = refs[n_in:]
    n_out = 2 * keep_ref.shape[0]
    width, piece = pieces[0].shape
    per_piece = piece // TILE
    slots = tiles_ref.shape[0]
    build_table(pieces, spread_ref[...], table)
    acc[...] = jnp.zeros_like(acc)
    lane = lax.broadcasted_iota(jnp.int32, (2 * width, LANES), 1)
    masks = [(lane // HALF == s).astype(BF16) for s in range(GROUP)]
    low = lax.broadcasted_iota(jnp.int32, (width, LANES), 1) < TILE
    count = count_ref[0, 0]
    row_flip = lax.axis_index("bcol") * per_piece
    col_flip = lax.axis_index("brow") * per_piece
    spare = n_out * per_piece

    for g in range(slots // GROUP):
        at = [table[rows_ref[g * GROUP + s] ^ row_flip] * masks[s] for s in range(GROUP)]
        block = tiles_ref[g * GROUP : (g + 1) * GROUP].reshape(LANES, LANES)
        out = jnp.dot(jnp.concatenate(at, axis=0), block, preferred_element_type=F32)
        for s in range(GROUP):
            t = g * GROUP + s
            part = out[2 * width * s : 2 * width * (s + 1)]
            part = jnp.where(low, part[:width], part[width:])
            c = jnp.where(t < count, cols_ref[t] ^ col_flip, spare)
            acc[c] += part

    for n in range(n_out):
        dest = (keep_ref if n % 2 == 0 else give_ref).at[n // 2]
        for p in range(per_piece // 2):
            a = acc[n * per_piece + 2 * p]
            b = acc[n * per_piece + 2 * p + 1]
            dest[:, p * LANES : (p + 1) * LANES] = jnp.where(low, a, b) + pltpu.roll(
                jnp.where(low, b, a), TILE, 1
            )


def backward(pieces, tiles, tile_rows, tile_cols, counts, n_out, after):
    n_in = len(pieces)
    width, piece = pieces[0].shape
    per_piece = piece // TILE
    half = jax.ShapeDtypeStruct((n_out // 2, width, piece), F32)
    return pl.pallas_call(
        functools.partial(backward_kernel, n_in),
        in_specs=[SMEM] * 3 + [VMEM] * (2 + n_in) + [ANY],
        out_specs=[VMEM] * 2,
        out_shape=[half, half],
        scratch_shapes=[
            pltpu.VMEM((n_in * per_piece, 2 * width, LANES), BF16),
            pltpu.VMEM((n_out * per_piece + 1, width, LANES), F32),
        ],
        compiler_params=PARAMS,
        cost_estimate=pl.CostEstimate(
            flops=2 * tiles.size * 64, bytes_accessed=4 * tiles.size, transcendentals=0
        ),
        name="transpose_product",
    )(tile_rows, tile_cols, counts, row_spread(), tiles, *pieces, after)


def forward_kernel(
    rows_ref,
    cols_ref,
    count_ref,
    spread_ref,
    fold_ref,
    tiles_ref,
    same_ref,
    other_ref,
    after_ref,
    keep_ref,
    give_ref,
    table,
    acc,
):
    pieces = [ref.at[h] for h in range(same_ref.shape[0]) for ref in (same_ref, other_ref)]
    n_out = 2 * keep_ref.shape[0]
    width, piece = pieces[0].shape
    per_piece = piece // TILE
    slots = tiles_ref.shape[0]
    build_table(pieces, spread_ref[...], table)
    acc[...] = jnp.zeros_like(acc)
    lane = lax.broadcasted_iota(jnp.int32, (2 * width, LANES), 1)
    masks = [lane // HALF == s for s in range(GROUP)]
    count = count_ref[0, 0]
    row_flip = lax.axis_index("bcol") * per_piece
    col_flip = lax.axis_index("brow") * per_piece
    spare = n_out * per_piece

    for g in range(slots // GROUP):
        at = [table[cols_ref[g * GROUP + s] ^ col_flip] for s in range(GROUP)]
        block = tiles_ref[g * GROUP : (g + 1) * GROUP].reshape(LANES, LANES)
        out = lax.dot_general(
            jnp.concatenate(at, axis=0),
            block,
            (((1,), (1,)), ((), ())),
            preferred_element_type=F32,
        )
        for s in range(GROUP):
            t = g * GROUP + s
            part = out[2 * width * s : 2 * width * (s + 1)]
            r = jnp.where(t < count, rows_ref[t] ^ row_flip, spare)
            acc[r] += jnp.where(masks[s], part, 0.0)

    fold = fold_ref[...]
    pairs = per_piece // 2
    for n in range(n_out):
        both = acc[n * per_piece : (n + 1) * per_piece].reshape(pairs, 4 * width, LANES)
        blocks = [
            both[:, x * width : (x + 1) * width, :].reshape(pairs * width, LANES) for x in range(4)
        ]
        wide = jnp.concatenate(blocks, axis=1)
        first = wide.astype(BF16)
        rest = (wide - first.astype(F32)).astype(BF16)
        out = jnp.dot(first, fold, preferred_element_type=F32)
        out = out + jnp.dot(rest, fold, preferred_element_type=F32)
        parts = [out[p * width : (p + 1) * width] for p in range(pairs)]
        if n % 2 == 0:
            for p in range(pairs):
                keep_ref[n // 2, :, p * LANES : (p + 1) * LANES] = parts[p]
        else:
            encode(parts, give_ref.at[n // 2])


def forward(same, other, tiles, tile_rows, tile_cols, counts, n_out, after):
    n_chips, width, piece = same.shape
    per_piece = piece // TILE
    half = jax.ShapeDtypeStruct((n_out // 2, width, piece), F32)
    coded = jax.ShapeDtypeStruct((n_out // 2, width, piece + LANES), jnp.int16)
    return pl.pallas_call(
        forward_kernel,
        in_specs=[SMEM] * 3 + [VMEM] * 5 + [ANY],
        out_specs=[VMEM] * 2,
        out_shape=[half, coded],
        scratch_shapes=[
            pltpu.VMEM((2 * n_chips * per_piece, 2 * width, LANES), BF16),
            pltpu.VMEM((n_out * per_piece + 1, 2 * width, LANES), F32),
        ],
        compiler_params=PARAMS,
        cost_estimate=pl.CostEstimate(
            flops=2 * tiles.size * 64, bytes_accessed=4 * tiles.size, transcendentals=0
        ),
        name="forward_product",
    )(tile_rows, tile_cols, counts, col_spread(), row_fold(), tiles, same, other, after)


def stack_kernel(n_after, *refs):
    out_ref, at = refs[-1], 0
    for ref in refs[: -1 - n_after]:
        if len(ref.shape) == 2:
            out_ref[at] = ref[...]
            at += 1
        else:
            out_ref[at : at + ref.shape[0]] = ref[...]
            at += ref.shape[0]


def stack(*parts, after=()):
    total = sum(x.shape[0] if x.ndim == 3 else 1 for x in parts)
    return pl.pallas_call(
        functools.partial(stack_kernel, len(after)),
        in_specs=[VMEM] * len(parts) + [ANY] * len(after),
        out_specs=VMEM,
        out_shape=jax.ShapeDtypeStruct((total,) + parts[0].shape[-2:], parts[0].dtype),
        compiler_params=PARAMS,
        name="stack_pieces",
    )(*parts, *after)


def pair_sum_kernel(keep_ref, got_ref, *outs):
    for h, out in enumerate(outs):
        out[...] = keep_ref[h + 1] + got_ref[h + 1]


def pair_sum(keep, got):
    parts, width, piece = keep.shape
    return pl.pallas_call(
        pair_sum_kernel,
        in_specs=[VMEM] * 2,
        out_specs=[VMEM] * (parts - 1),
        out_shape=[jax.ShapeDtypeStruct((width, piece), F32)] * (parts - 1),
        compiler_params=PARAMS,
        name="core_pair_sum",
    )(keep, got)


def split_sum_kernel(keep_ref, got_ref, after_ref, next_keep, next_give):
    for h in range(next_keep.shape[0]):
        for n, got in enumerate(decode(got_ref.at[2 * h])):
            at = pl.ds(n * LANES, LANES)
            next_keep[h, :, at] = keep_ref[2 * h, :, at] + got
        sums = [
            keep_ref[2 * h + 1, :, n * LANES : (n + 1) * LANES] + got
            for n, got in enumerate(decode(got_ref.at[2 * h + 1]))
        ]
        encode(sums, next_give.at[h])


def split_sum(keep, got, after):
    parts, width, piece = keep.shape
    return pl.pallas_call(
        split_sum_kernel,
        in_specs=[VMEM] * 2 + [ANY],
        out_specs=[VMEM] * 2,
        out_shape=[
            jax.ShapeDtypeStruct((parts // 2, width, piece), F32),
            jax.ShapeDtypeStruct((parts // 2,) + got.shape[1:], got.dtype),
        ],
        compiler_params=PARAMS,
        name="halving_sum",
    )(keep, got, after)


def last_sum_kernel(*refs):
    chips, (brow_keep, brow_got, keep_ref, got_ref, out_ref) = refs[:-5], refs[-5:]
    for n, got in enumerate(decode(got_ref.at[0])):
        at = pl.ds(n * LANES, LANES)
        total = brow_keep[0, :, at] + brow_got[0, :, at]
        for ref in chips:
            total = total + ref[:, at]
        out_ref[:, at] = total + (keep_ref[0, :, at] + got)


def last_sum(keep, got, brow_keep, brow_got, chips):
    return pl.pallas_call(
        last_sum_kernel,
        in_specs=[VMEM] * (4 + len(chips)),
        out_specs=VMEM,
        out_shape=jax.ShapeDtypeStruct(keep.shape[1:], F32),
        compiler_params=PARAMS,
        name="last_sum",
    )(*chips, brow_keep, brow_got, keep, got)


def swap(x, axis, size, d):
    return lax.ppermute(x, axis, [(i, i ^ d) for i in range(size)])


def body(vectors, tiles, tile_rows, tile_cols, counts):
    n_rows = lax.axis_size("brow")
    n_cols = lax.axis_size("bcol")
    own = stack(vectors)
    chips = [swap(vectors, "brow", n_rows, 2 * h) for h in range(1, n_rows // 2)]
    row_pieces = [own[0]] + [swap(vectors, "bcol", n_cols, d) for d in range(1, n_cols)]
    blocks = prep(tiles)
    same = stack(own, *chips, after=(blocks, *row_pieces[1:]))
    other = swap(same, "brow", n_rows, 1)

    col_keep, col_give = backward(row_pieces, blocks, tile_rows, tile_cols, counts, n_rows, same)
    row_keep, give = forward(same, other, blocks, tile_rows, tile_cols, counts, n_cols, col_give)
    col_got = swap(col_give, "brow", n_rows, 1)
    sums = pair_sum(col_keep, col_got)
    from_chips = [swap(x, "brow", n_rows, 2 * (h + 1)) for h, x in enumerate(sums)]
    row_got, d = swap(give, "bcol", n_cols, 1), 2
    while d < n_cols:
        row_keep, give = split_sum(row_keep, row_got, sums[0])
        row_got = swap(give, "bcol", n_cols, d)
        d *= 2
    return last_sum(row_keep, row_got, col_keep, col_got, from_chips)


def solution(mesh):
    return jax.shard_map(
        body,
        mesh=mesh,
        in_specs=(
            P(None, ("brow", "bcol")),
            P(("brow", "bcol"), None),
            P(("brow", "bcol")),
            P(("brow", "bcol")),
            P("brow", "bcol"),
        ),
        out_specs=P(None, ("brow", "bcol")),
        check_vma=False,
    )
```

```python
import functools

import jax
import jax.numpy as jnp
import numpy as np
from jax import lax
from jax.experimental import pallas as pl
from jax.experimental.pallas import tpu as pltpu
from jax.sharding import PartitionSpec as P

TILE = 64
LANES = 128
HALF = TILE // 2
GROUP = LANES // HALF
STEPS = 32000.0
F32 = jnp.float32
BF16 = jnp.bfloat16
VMEM = pl.BlockSpec(memory_space=pltpu.VMEM)
ANY = pl.BlockSpec(memory_space=pl.ANY)
SMEM = pl.BlockSpec(memory_space=pltpu.SMEM)
PARAMS = pltpu.CompilerParams(vmem_limit_bytes=48 * 1024 * 1024)


def row_spread():
    out = np.zeros((LANES, 2, 2, GROUP, HALF), np.float32)
    for q in range(2):
        for e in range(2):
            for m in range(HALF):
                out[q * TILE + 2 * m + e, q, e, :, m] = 1
    return jnp.asarray(out.reshape(LANES, 4 * LANES), BF16)


def col_spread():
    out = np.zeros((LANES, 2, 2, 2, TILE), np.float32)
    for q in range(2):
        for e in range(2):
            for j in range(TILE):
                out[q * TILE + j, q, e, e, j] = 1
    return jnp.asarray(out.reshape(LANES, 4 * LANES), BF16)


def row_fold():
    return row_spread().T


def encode(values, out_ref):
    width, piece = values[0].shape[0], LANES * len(values)
    lane = lax.broadcasted_iota(jnp.int32, (width, LANES), 1)
    exponents = jnp.zeros((width, LANES), F32)
    for n, value in enumerate(values):
        top = jnp.max(jnp.abs(value), axis=1, keepdims=True)
        e = jnp.clip(jnp.ceil(jnp.log2(top)), -100.0, 100.0)
        exponents = jnp.where(lane == n, e, exponents)
        scaled = jnp.floor(value * (STEPS * jnp.exp2(-e)) + 0.5)
        out_ref[:, n * LANES : (n + 1) * LANES] = scaled.astype(jnp.int32).astype(jnp.int16)
    out_ref[:, piece:] = exponents.astype(jnp.int32).astype(jnp.int16)


def decode(ref):
    chunks = ref.shape[1] // LANES - 1
    exponents = ref[:, chunks * LANES :].astype(jnp.int32).astype(F32)
    scales = jnp.exp2(exponents) * (1.0 / STEPS)
    return [
        ref[:, n * LANES : (n + 1) * LANES].astype(jnp.int32).astype(F32) * scales[:, n : n + 1]
        for n in range(chunks)
    ]


def prep_kernel(tiles_ref, out_ref, wide):
    for b in range(tiles_ref.shape[0]):
        wide[b] = tiles_ref[b].astype(F32).reshape(HALF * 8, LANES)
        for s in range(8):
            out_ref[8 * b + s] = wide[b, pl.ds(s, HALF, stride=8), :].astype(BF16)


def prep(tiles):
    slots = tiles.shape[0]
    blocks = slots // 8
    view = tiles.reshape(blocks, 8, HALF, LANES).swapaxes(1, 2)
    return pl.pallas_call(
        prep_kernel,
        in_specs=[VMEM],
        out_specs=VMEM,
        out_shape=jax.ShapeDtypeStruct((slots, HALF, LANES), BF16),
        scratch_shapes=[pltpu.VMEM((blocks, HALF * 8, LANES), F32)],
        compiler_params=PARAMS,
        cost_estimate=pl.CostEstimate(flops=0, bytes_accessed=4 * tiles.size, transcendentals=0),
        name="prep_tiles",
    )(view)


def build_table(pieces, spread, table):
    width, piece = pieces[0].shape
    pairs = piece // LANES
    for n, ref in enumerate(pieces):
        rows = jnp.concatenate([ref[:, p * LANES : (p + 1) * LANES] for p in range(pairs)], axis=0)
        wide = jnp.dot(rows, spread, preferred_element_type=F32)
        wide = wide.reshape(pairs, width, 4 * LANES)
        for q in range(2):
            both = jnp.concatenate(
                [wide[:, :, (2 * q + e) * LANES : (2 * q + e + 1) * LANES] for e in range(2)], axis=1
            ).astype(BF16)
            for p in range(pairs):
                table[n * 2 * pairs + 2 * p + q] = both[p]


def backward_kernel(n_in, rows_ref, cols_ref, count_ref, spread_ref, tiles_ref, *refs):
    pieces = refs[:n_in]
    _, keep_ref, *give_refs, table, acc = refs[n_in:]
    per_give = give_refs[0].shape[0]
    n_out = 2 * keep_ref.shape[0]
    width, piece = pieces[0].shape
    per_piece = piece // TILE
    slots = tiles_ref.shape[0]
    build_table(pieces, spread_ref[...], table)
    acc[...] = jnp.zeros_like(acc)
    lane = lax.broadcasted_iota(jnp.int32, (2 * width, LANES), 1)
    masks = [(lane // HALF == s).astype(BF16) for s in range(GROUP)]
    low = lax.broadcasted_iota(jnp.int32, (width, LANES), 1) < TILE
    count = count_ref[0, 0]
    row_flip = lax.axis_index("bcol") * per_piece
    col_flip = lax.axis_index("brow") * per_piece
    spare = n_out * per_piece

    for g in range(slots // GROUP):
        at = [table[rows_ref[g * GROUP + s] ^ row_flip] * masks[s] for s in range(GROUP)]
        block = tiles_ref[g * GROUP : (g + 1) * GROUP].reshape(LANES, LANES)
        out = jnp.dot(jnp.concatenate(at, axis=0), block, preferred_element_type=F32)
        for s in range(GROUP):
            t = g * GROUP + s
            part = out[2 * width * s : 2 * width * (s + 1)]
            part = jnp.where(low, part[:width], part[width:])
            c = jnp.where(t < count, cols_ref[t] ^ col_flip, spare)
            acc[c] += part

    for n in range(n_out):
        h = n // 2
        dest = keep_ref.at[h] if n % 2 == 0 else give_refs[h // per_give].at[h % per_give]
        for p in range(per_piece // 2):
            a = acc[n * per_piece + 2 * p]
            b = acc[n * per_piece + 2 * p + 1]
            dest[:, p * LANES : (p + 1) * LANES] = jnp.where(low, a, b) + pltpu.roll(
                jnp.where(low, b, a), TILE, 1
            )


def backward(pieces, tiles, tile_rows, tile_cols, counts, n_out, after):
    n_in = len(pieces)
    width, piece = pieces[0].shape
    per_piece = piece // TILE
    half = jax.ShapeDtypeStruct((n_out // 2, width, piece), F32)
    quarter = jax.ShapeDtypeStruct((n_out // 4, width, piece), F32)
    return pl.pallas_call(
        functools.partial(backward_kernel, n_in),
        in_specs=[SMEM] * 3 + [VMEM] * (2 + n_in) + [ANY],
        out_specs=[VMEM] * 3,
        out_shape=[half, quarter, quarter],
        scratch_shapes=[
            pltpu.VMEM((n_in * per_piece, 2 * width, LANES), BF16),
            pltpu.VMEM((n_out * per_piece + 1, width, LANES), F32),
        ],
        compiler_params=PARAMS,
        cost_estimate=pl.CostEstimate(
            flops=2 * tiles.size * 64, bytes_accessed=4 * tiles.size, transcendentals=0
        ),
        name="transpose_product",
    )(tile_rows, tile_cols, counts, row_spread(), tiles, *pieces, after)


def forward_kernel(
    rows_ref,
    cols_ref,
    count_ref,
    spread_ref,
    fold_ref,
    tiles_ref,
    same_ref,
    other_ref,
    after_ref,
    keep_ref,
    give_ref,
    table,
    acc,
):
    pieces = [ref.at[h] for h in range(same_ref.shape[0]) for ref in (same_ref, other_ref)]
    n_out = 2 * keep_ref.shape[0]
    width, piece = pieces[0].shape
    per_piece = piece // TILE
    slots = tiles_ref.shape[0]
    build_table(pieces, spread_ref[...], table)
    acc[...] = jnp.zeros_like(acc)
    lane = lax.broadcasted_iota(jnp.int32, (2 * width, LANES), 1)
    masks = [lane // HALF == s for s in range(GROUP)]
    count = count_ref[0, 0]
    row_flip = lax.axis_index("bcol") * per_piece
    col_flip = lax.axis_index("brow") * per_piece
    spare = n_out * per_piece

    for g in range(slots // GROUP):
        at = [table[cols_ref[g * GROUP + s] ^ col_flip] for s in range(GROUP)]
        block = tiles_ref[g * GROUP : (g + 1) * GROUP].reshape(LANES, LANES)
        out = lax.dot_general(
            jnp.concatenate(at, axis=0),
            block,
            (((1,), (1,)), ((), ())),
            preferred_element_type=F32,
        )
        for s in range(GROUP):
            t = g * GROUP + s
            part = out[2 * width * s : 2 * width * (s + 1)]
            r = jnp.where(t < count, rows_ref[t] ^ row_flip, spare)
            acc[r] += jnp.where(masks[s], part, 0.0)

    fold = fold_ref[...]
    pairs = per_piece // 2
    for n in range(n_out):
        both = acc[n * per_piece : (n + 1) * per_piece].reshape(pairs, 4 * width, LANES)
        blocks = [
            both[:, x * width : (x + 1) * width, :].reshape(pairs * width, LANES) for x in range(4)
        ]
        wide = jnp.concatenate(blocks, axis=1)
        first = wide.astype(BF16)
        rest = (wide - first.astype(F32)).astype(BF16)
        out = jnp.dot(first, fold, preferred_element_type=F32)
        out = out + jnp.dot(rest, fold, preferred_element_type=F32)
        parts = [out[p * width : (p + 1) * width] for p in range(pairs)]
        if n % 2 == 0:
            for p in range(pairs):
                keep_ref[n // 2, :, p * LANES : (p + 1) * LANES] = parts[p]
        else:
            encode(parts, give_ref.at[n // 2])


def forward(same, other, tiles, tile_rows, tile_cols, counts, n_out, after):
    n_chips, width, piece = same.shape
    per_piece = piece // TILE
    half = jax.ShapeDtypeStruct((n_out // 2, width, piece), F32)
    coded = jax.ShapeDtypeStruct((n_out // 2, width, piece + LANES), jnp.int16)
    return pl.pallas_call(
        forward_kernel,
        in_specs=[SMEM] * 3 + [VMEM] * 5 + [ANY],
        out_specs=[VMEM] * 2,
        out_shape=[half, coded],
        scratch_shapes=[
            pltpu.VMEM((2 * n_chips * per_piece, 2 * width, LANES), BF16),
            pltpu.VMEM((n_out * per_piece + 1, 2 * width, LANES), F32),
        ],
        compiler_params=PARAMS,
        cost_estimate=pl.CostEstimate(
            flops=2 * tiles.size * 64, bytes_accessed=4 * tiles.size, transcendentals=0
        ),
        name="forward_product",
    )(tile_rows, tile_cols, counts, col_spread(), row_fold(), tiles, same, other, after)


def stack_kernel(n_after, *refs):
    out_ref, at = refs[-1], 0
    for ref in refs[: -1 - n_after]:
        if len(ref.shape) == 2:
            out_ref[at] = ref[...]
            at += 1
        else:
            out_ref[at : at + ref.shape[0]] = ref[...]
            at += ref.shape[0]


def stack(*parts, after=()):
    total = sum(x.shape[0] if x.ndim == 3 else 1 for x in parts)
    return pl.pallas_call(
        functools.partial(stack_kernel, len(after)),
        in_specs=[VMEM] * len(parts) + [ANY] * len(after),
        out_specs=VMEM,
        out_shape=jax.ShapeDtypeStruct((total,) + parts[0].shape[-2:], parts[0].dtype),
        compiler_params=PARAMS,
        name="stack_pieces",
    )(*parts, *after)


def pair_sum_kernel(keep_ref, *refs):
    n_chips = keep_ref.shape[0]
    gots, outs = refs[: 1 - n_chips], refs[1 - n_chips :]
    got = [ref.at[h] for ref in gots for h in range(ref.shape[0])]
    for h, out in enumerate(outs):
        out[...] = keep_ref[h + 1] + got[h + 1][...]


def pair_sum(keep, gots):
    parts, width, piece = keep.shape
    return pl.pallas_call(
        pair_sum_kernel,
        in_specs=[VMEM] * (1 + len(gots)),
        out_specs=[VMEM] * (parts - 1),
        out_shape=[jax.ShapeDtypeStruct((width, piece), F32)] * (parts - 1),
        compiler_params=PARAMS,
        name="core_pair_sum",
    )(keep, *gots)


def split_sum_kernel(keep_ref, got_ref, after_ref, next_keep, next_give):
    for h in range(next_keep.shape[0]):
        for n, got in enumerate(decode(got_ref.at[2 * h])):
            at = pl.ds(n * LANES, LANES)
            next_keep[h, :, at] = keep_ref[2 * h, :, at] + got
        sums = [
            keep_ref[2 * h + 1, :, n * LANES : (n + 1) * LANES] + got
            for n, got in enumerate(decode(got_ref.at[2 * h + 1]))
        ]
        encode(sums, next_give.at[h])


def split_sum(keep, got, after):
    parts, width, piece = keep.shape
    return pl.pallas_call(
        split_sum_kernel,
        in_specs=[VMEM] * 2 + [ANY],
        out_specs=[VMEM] * 2,
        out_shape=[
            jax.ShapeDtypeStruct((parts // 2, width, piece), F32),
            jax.ShapeDtypeStruct((parts // 2,) + got.shape[1:], got.dtype),
        ],
        compiler_params=PARAMS,
        name="halving_sum",
    )(keep, got, after)


def last_sum_kernel(*refs):
    chips, (brow_keep, brow_got, keep_ref, got_ref, out_ref) = refs[:-5], refs[-5:]
    for n, got in enumerate(decode(got_ref.at[0])):
        at = pl.ds(n * LANES, LANES)
        total = brow_keep[0, :, at] + brow_got[0, :, at]
        for ref in chips:
            total = total + ref[:, at]
        out_ref[:, at] = total + (keep_ref[0, :, at] + got)


def last_sum(keep, got, brow_keep, brow_got, chips):
    return pl.pallas_call(
        last_sum_kernel,
        in_specs=[VMEM] * (4 + len(chips)),
        out_specs=VMEM,
        out_shape=jax.ShapeDtypeStruct(keep.shape[1:], F32),
        compiler_params=PARAMS,
        name="last_sum",
    )(*chips, brow_keep, brow_got, keep, got)


def swap(x, axis, size, d):
    return lax.ppermute(x, axis, [(i, i ^ d) for i in range(size)])


def body(vectors, tiles, tile_rows, tile_cols, counts):
    n_rows = lax.axis_size("brow")
    n_cols = lax.axis_size("bcol")
    own = stack(vectors)
    chips = [swap(vectors, "brow", n_rows, 2 * h) for h in range(1, n_rows // 2)]
    row_pieces = [own[0]] + [swap(vectors, "bcol", n_cols, d) for d in range(1, n_cols)]
    blocks = prep(tiles)
    same = stack(own, *chips, after=(blocks, *row_pieces[1:]))
    other = swap(same, "brow", n_rows, 1)

    col_keep, *col_give = backward(row_pieces, blocks, tile_rows, tile_cols, counts, n_rows, same)
    row_keep, give = forward(same, other, blocks, tile_rows, tile_cols, counts, n_cols, col_give[0])
    col_got = [swap(x, "brow", n_rows, 1) for x in col_give]
    sums = pair_sum(col_keep, col_got)
    from_chips = [swap(x, "brow", n_rows, 2 * (h + 1)) for h, x in enumerate(sums)]
    row_got, d = swap(give, "bcol", n_cols, 1), 2
    while d < n_cols:
        row_keep, give = split_sum(row_keep, row_got, sums[0])
        row_got = swap(give, "bcol", n_cols, d)
        d *= 2
    return last_sum(row_keep, row_got, col_keep, col_got[0], from_chips)


def solution(mesh):
    return jax.shard_map(
        body,
        mesh=mesh,
        in_specs=(
            P(None, ("brow", "bcol")),
            P(("brow", "bcol"), None),
            P(("brow", "bcol")),
            P(("brow", "bcol")),
            P("brow", "bcol"),
        ),
        out_specs=P(None, ("brow", "bcol")),
        check_vma=False,
    )
```

```python
import functools

import jax
import jax.numpy as jnp
import numpy as np
from jax import lax
from jax.experimental import pallas as pl
from jax.experimental.pallas import tpu as pltpu
from jax.sharding import PartitionSpec as P

TILE = 64
LANES = 128
HALF = TILE // 2
GROUP = LANES // HALF
STEPS = 32000.0
F32 = jnp.float32
BF16 = jnp.bfloat16
VMEM = pl.BlockSpec(memory_space=pltpu.VMEM)
ANY = pl.BlockSpec(memory_space=pl.ANY)
SMEM = pl.BlockSpec(memory_space=pltpu.SMEM)
PARAMS = pltpu.CompilerParams(vmem_limit_bytes=48 * 1024 * 1024)


def row_spread():
    out = np.zeros((LANES, 2, 2, GROUP, HALF), np.float32)
    for q in range(2):
        for e in range(2):
            for m in range(HALF):
                out[q * TILE + 2 * m + e, q, e, :, m] = 1
    return jnp.asarray(out.reshape(LANES, 4 * LANES), BF16)


def col_spread():
    out = np.zeros((LANES, 2, 2, 2, TILE), np.float32)
    for q in range(2):
        for e in range(2):
            for j in range(TILE):
                out[q * TILE + j, q, e, e, j] = 1
    return jnp.asarray(out.reshape(LANES, 4 * LANES), BF16)


def row_fold():
    out = np.zeros((2, 2, 2, GROUP // 2, HALF, LANES), np.float32)
    for q in range(2):
        for e in range(2):
            for m in range(HALF):
                out[q, 0, e, :, m, q * TILE + 2 * m + e] = 1
                out[q, 1, 1 - e, :, m, q * TILE + 2 * m + e] = 1
    return jnp.asarray(out.reshape(4 * LANES, LANES), BF16)


def encode(values, out_ref):
    width, piece = values[0].shape[0], LANES * len(values)
    lane = lax.broadcasted_iota(jnp.int32, (width, LANES), 1)
    exponents = jnp.zeros((width, LANES), F32)
    for n, value in enumerate(values):
        top = jnp.max(jnp.abs(value), axis=1, keepdims=True)
        e = jnp.clip(jnp.ceil(jnp.log2(top)), -100.0, 100.0)
        exponents = jnp.where(lane == n, e, exponents)
        scaled = jnp.floor(value * (STEPS * jnp.exp2(-e)) + 0.5)
        out_ref[:, n * LANES : (n + 1) * LANES] = scaled.astype(jnp.int32).astype(jnp.int16)
    out_ref[:, piece:] = exponents.astype(jnp.int32).astype(jnp.int16)


def decode(ref):
    chunks = ref.shape[1] // LANES - 1
    exponents = ref[:, chunks * LANES :].astype(jnp.int32).astype(F32)
    scales = jnp.exp2(exponents) * (1.0 / STEPS)
    return [
        ref[:, n * LANES : (n + 1) * LANES].astype(jnp.int32).astype(F32) * scales[:, n : n + 1]
        for n in range(chunks)
    ]


def prep_kernel(tiles_ref, out_ref, wide):
    for b in range(tiles_ref.shape[0]):
        wide[b] = tiles_ref[b].astype(F32).reshape(HALF * 8, LANES)
        for s in range(8):
            out_ref[8 * b + s] = wide[b, pl.ds(s, HALF, stride=8), :].astype(BF16)


def prep(tiles):
    slots = tiles.shape[0]
    blocks = slots // 8
    view = tiles.reshape(blocks, 8, HALF, LANES).swapaxes(1, 2)
    return pl.pallas_call(
        prep_kernel,
        in_specs=[VMEM],
        out_specs=VMEM,
        out_shape=jax.ShapeDtypeStruct((slots, HALF, LANES), BF16),
        scratch_shapes=[pltpu.VMEM((blocks, HALF * 8, LANES), F32)],
        compiler_params=PARAMS,
        cost_estimate=pl.CostEstimate(flops=0, bytes_accessed=4 * tiles.size, transcendentals=0),
        name="prep_tiles",
    )(view)


def build_table(pieces, spread, table):
    width, piece = pieces[0].shape
    pairs = piece // LANES
    for n, ref in enumerate(pieces):
        rows = jnp.concatenate([ref[:, p * LANES : (p + 1) * LANES] for p in range(pairs)], axis=0)
        wide = jnp.dot(rows, spread, preferred_element_type=F32)
        wide = wide.reshape(pairs, width, 4 * LANES)
        for q in range(2):
            both = jnp.concatenate(
                [wide[:, :, (2 * q + e) * LANES : (2 * q + e + 1) * LANES] for e in range(2)], axis=1
            ).astype(BF16)
            for p in range(pairs):
                table[n * 2 * pairs + 2 * p + q] = both[p]


def backward_kernel(n_in, rows_ref, cols_ref, count_ref, spread_ref, tiles_ref, *refs):
    pieces = refs[:n_in]
    _, keep_ref, *give_refs, table, acc_a, acc_b = refs[n_in:]
    per_give = give_refs[0].shape[0]
    n_out = 2 * keep_ref.shape[0]
    width, piece = pieces[0].shape
    per_piece = piece // TILE
    slots = tiles_ref.shape[0]
    build_table(pieces, spread_ref[...], table)
    for acc in (acc_a, acc_b):
        acc[...] = jnp.zeros_like(acc)
    lane = lax.broadcasted_iota(jnp.int32, (2 * width, LANES), 1)
    masks = [(lane // HALF == s).astype(BF16) for s in range(GROUP)]
    low = lax.broadcasted_iota(jnp.int32, (width, LANES), 1) < TILE
    count = count_ref[0, 0]
    row_flip = lax.axis_index("bcol") * per_piece
    col_flip = lax.axis_index("brow") * per_piece
    spare = n_out * per_piece

    for g in range(slots // GROUP):
        at = [table[rows_ref[g * GROUP + s] ^ row_flip] * masks[s] for s in range(GROUP)]
        block = tiles_ref[g * GROUP : (g + 1) * GROUP].reshape(LANES, LANES)
        out = jnp.dot(jnp.concatenate(at, axis=0), block, preferred_element_type=F32)
        for s in range(GROUP):
            t = g * GROUP + s
            part = out[2 * width * s : 2 * width * (s + 1)]
            part = jnp.where(low, part[:width], part[width:])
            c = jnp.where(t < count, cols_ref[t] ^ col_flip, spare)
            acc = acc_a if s % 2 == 0 else acc_b
            acc[c] += part

    for n in range(n_out):
        h = n // 2
        dest = keep_ref.at[h] if n % 2 == 0 else give_refs[h // per_give].at[h % per_give]
        for p in range(per_piece // 2):
            at = n * per_piece + 2 * p
            a = acc_a[at] + acc_b[at]
            b = acc_a[at + 1] + acc_b[at + 1]
            dest[:, p * LANES : (p + 1) * LANES] = jnp.where(low, a, b) + pltpu.roll(
                jnp.where(low, b, a), TILE, 1
            )


def backward(pieces, tiles, tile_rows, tile_cols, counts, n_out, after):
    n_in = len(pieces)
    width, piece = pieces[0].shape
    per_piece = piece // TILE
    half = jax.ShapeDtypeStruct((n_out // 2, width, piece), F32)
    quarter = jax.ShapeDtypeStruct((n_out // 4, width, piece), F32)
    return pl.pallas_call(
        functools.partial(backward_kernel, n_in),
        in_specs=[SMEM] * 3 + [VMEM] * (2 + n_in) + [ANY],
        out_specs=[VMEM] * 3,
        out_shape=[half, quarter, quarter],
        scratch_shapes=[
            pltpu.VMEM((n_in * per_piece, 2 * width, LANES), BF16),
            pltpu.VMEM((n_out * per_piece + 1, width, LANES), F32),
            pltpu.VMEM((n_out * per_piece + 1, width, LANES), F32),
        ],
        compiler_params=PARAMS,
        cost_estimate=pl.CostEstimate(
            flops=2 * tiles.size * 64, bytes_accessed=4 * tiles.size, transcendentals=0
        ),
        name="transpose_product",
    )(tile_rows, tile_cols, counts, row_spread(), tiles, *pieces, after)


def forward_kernel(
    rows_ref,
    cols_ref,
    count_ref,
    spread_ref,
    fold_ref,
    tiles_ref,
    same_ref,
    other_ref,
    after_ref,
    keep_ref,
    give_ref,
    table,
    acc_a,
    acc_b,
):
    pieces = [ref.at[h] for h in range(same_ref.shape[0]) for ref in (same_ref, other_ref)]
    n_out = 2 * keep_ref.shape[0]
    width, piece = pieces[0].shape
    per_piece = piece // TILE
    slots = tiles_ref.shape[0]
    build_table(pieces, spread_ref[...], table)
    for acc in (acc_a, acc_b):
        acc[...] = jnp.zeros_like(acc)
    lane = lax.broadcasted_iota(jnp.int32, (width, LANES), 1)
    masks = [lane // HALF == s for s in range(GROUP)]
    count = count_ref[0, 0]
    row_flip = lax.axis_index("bcol") * per_piece
    col_flip = lax.axis_index("brow") * per_piece
    spare = n_out * per_piece

    for g in range(slots // GROUP):
        at = [table[cols_ref[g * GROUP + s] ^ col_flip] for s in range(GROUP)]
        block = tiles_ref[g * GROUP : (g + 1) * GROUP].reshape(LANES, LANES)
        out = lax.dot_general(
            jnp.concatenate(at, axis=0),
            block,
            (((1,), (1,)), ((), ())),
            preferred_element_type=F32,
        )
        for s in range(GROUP):
            t = g * GROUP + s
            part = out[2 * width * s : 2 * width * (s + 1)]
            r = jnp.where(t < count, rows_ref[t] ^ row_flip, spare)
            part = jnp.where(
                masks[s],
                part[:width],
                jnp.where(masks[(s + 2) % GROUP], pltpu.roll(part[width:], TILE, 1), 0.0),
            )
            acc = acc_a if s < 2 else acc_b
            acc[r] += part

    fold = fold_ref[...]
    pairs = per_piece // 2
    for n in range(n_out):
        blocks = []
        for q in range(2):
            for acc in (acc_a, acc_b):
                both = acc[n * per_piece : (n + 1) * per_piece].reshape(pairs, 2 * width, LANES)
                blocks.append(both[:, q * width : (q + 1) * width, :].reshape(pairs * width, LANES))
        wide = jnp.concatenate(blocks, axis=1)
        first = wide.astype(BF16)
        rest = (wide - first.astype(F32)).astype(BF16)
        out = jnp.dot(first, fold, preferred_element_type=F32)
        out = out + jnp.dot(rest, fold, preferred_element_type=F32)
        parts = [out[p * width : (p + 1) * width] for p in range(pairs)]
        if n % 2 == 0:
            for p in range(pairs):
                keep_ref[n // 2, :, p * LANES : (p + 1) * LANES] = parts[p]
        else:
            encode(parts, give_ref.at[n // 2])


def forward(same, other, tiles, tile_rows, tile_cols, counts, n_out, after):
    n_chips, width, piece = same.shape
    per_piece = piece // TILE
    half = jax.ShapeDtypeStruct((n_out // 2, width, piece), F32)
    coded = jax.ShapeDtypeStruct((n_out // 2, width, piece + LANES), jnp.int16)
    return pl.pallas_call(
        forward_kernel,
        in_specs=[SMEM] * 3 + [VMEM] * 5 + [ANY],
        out_specs=[VMEM] * 2,
        out_shape=[half, coded],
        scratch_shapes=[
            pltpu.VMEM((2 * n_chips * per_piece, 2 * width, LANES), BF16),
            pltpu.VMEM((n_out * per_piece + 1, width, LANES), F32),
            pltpu.VMEM((n_out * per_piece + 1, width, LANES), F32),
        ],
        compiler_params=PARAMS,
        cost_estimate=pl.CostEstimate(
            flops=2 * tiles.size * 64, bytes_accessed=4 * tiles.size, transcendentals=0
        ),
        name="forward_product",
    )(tile_rows, tile_cols, counts, col_spread(), row_fold(), tiles, same, other, after)


def stack_kernel(n_after, *refs):
    out_ref, at = refs[-1], 0
    for ref in refs[: -1 - n_after]:
        if len(ref.shape) == 2:
            out_ref[at] = ref[...]
            at += 1
        else:
            out_ref[at : at + ref.shape[0]] = ref[...]
            at += ref.shape[0]


def stack(*parts, after=()):
    total = sum(x.shape[0] if x.ndim == 3 else 1 for x in parts)
    return pl.pallas_call(
        functools.partial(stack_kernel, len(after)),
        in_specs=[VMEM] * len(parts) + [ANY] * len(after),
        out_specs=VMEM,
        out_shape=jax.ShapeDtypeStruct((total,) + parts[0].shape[-2:], parts[0].dtype),
        compiler_params=PARAMS,
        name="stack_pieces",
    )(*parts, *after)


def pair_sum_kernel(keep_ref, *refs):
    n_chips = keep_ref.shape[0]
    gots, outs = refs[: 1 - n_chips], refs[1 - n_chips :]
    got = [ref.at[h] for ref in gots for h in range(ref.shape[0])]
    for h, out in enumerate(outs):
        out[...] = keep_ref[h + 1] + got[h + 1][...]


def pair_sum(keep, gots):
    parts, width, piece = keep.shape
    return pl.pallas_call(
        pair_sum_kernel,
        in_specs=[VMEM] * (1 + len(gots)),
        out_specs=[VMEM] * (parts - 1),
        out_shape=[jax.ShapeDtypeStruct((width, piece), F32)] * (parts - 1),
        compiler_params=PARAMS,
        name="core_pair_sum",
    )(keep, *gots)


def split_sum_kernel(keep_ref, got_ref, after_ref, next_keep, next_give):
    for h in range(next_keep.shape[0]):
        for n, got in enumerate(decode(got_ref.at[2 * h])):
            at = pl.ds(n * LANES, LANES)
            next_keep[h, :, at] = keep_ref[2 * h, :, at] + got
        sums = [
            keep_ref[2 * h + 1, :, n * LANES : (n + 1) * LANES] + got
            for n, got in enumerate(decode(got_ref.at[2 * h + 1]))
        ]
        encode(sums, next_give.at[h])


def split_sum(keep, got, after):
    parts, width, piece = keep.shape
    return pl.pallas_call(
        split_sum_kernel,
        in_specs=[VMEM] * 2 + [ANY],
        out_specs=[VMEM] * 2,
        out_shape=[
            jax.ShapeDtypeStruct((parts // 2, width, piece), F32),
            jax.ShapeDtypeStruct((parts // 2,) + got.shape[1:], got.dtype),
        ],
        compiler_params=PARAMS,
        name="halving_sum",
    )(keep, got, after)


def last_sum_kernel(*refs):
    chips, (brow_keep, brow_got, keep_ref, got_ref, out_ref) = refs[:-5], refs[-5:]
    for n, got in enumerate(decode(got_ref.at[0])):
        at = pl.ds(n * LANES, LANES)
        total = brow_keep[0, :, at] + brow_got[0, :, at]
        for ref in chips:
            total = total + ref[:, at]
        out_ref[:, at] = total + (keep_ref[0, :, at] + got)


def last_sum(keep, got, brow_keep, brow_got, chips):
    return pl.pallas_call(
        last_sum_kernel,
        in_specs=[VMEM] * (4 + len(chips)),
        out_specs=VMEM,
        out_shape=jax.ShapeDtypeStruct(keep.shape[1:], F32),
        compiler_params=PARAMS,
        name="last_sum",
    )(*chips, brow_keep, brow_got, keep, got)


def swap(x, axis, size, d):
    return lax.ppermute(x, axis, [(i, i ^ d) for i in range(size)])


def body(vectors, tiles, tile_rows, tile_cols, counts):
    n_rows = lax.axis_size("brow")
    n_cols = lax.axis_size("bcol")
    own = stack(vectors)
    chips = [swap(vectors, "brow", n_rows, 2 * h) for h in range(1, n_rows // 2)]
    row_pieces = [own[0]] + [swap(vectors, "bcol", n_cols, d) for d in range(1, n_cols)]
    blocks = prep(tiles)
    same = stack(own, *chips, after=(blocks, *row_pieces[1:]))
    other = swap(same, "brow", n_rows, 1)

    col_keep, *col_give = backward(row_pieces, blocks, tile_rows, tile_cols, counts, n_rows, same)
    row_keep, give = forward(same, other, blocks, tile_rows, tile_cols, counts, n_cols, col_give[0])
    col_got = [swap(x, "brow", n_rows, 1) for x in col_give]
    sums = pair_sum(col_keep, col_got)
    from_chips = [swap(x, "brow", n_rows, 2 * (h + 1)) for h, x in enumerate(sums)]
    row_got, d = swap(give, "bcol", n_cols, 1), 2
    while d < n_cols:
        row_keep, give = split_sum(row_keep, row_got, sums[0])
        row_got = swap(give, "bcol", n_cols, d)
        d *= 2
    return last_sum(row_keep, row_got, col_keep, col_got[0], from_chips)


def solution(mesh):
    return jax.shard_map(
        body,
        mesh=mesh,
        in_specs=(
            P(None, ("brow", "bcol")),
            P(("brow", "bcol"), None),
            P(("brow", "bcol")),
            P(("brow", "bcol")),
            P("brow", "bcol"),
        ),
        out_specs=P(None, ("brow", "bcol")),
        check_vma=False,
    )
```

```python
import functools

import jax
import jax.numpy as jnp
import numpy as np
from jax import lax
from jax.experimental import pallas as pl
from jax.experimental.pallas import tpu as pltpu
from jax.sharding import PartitionSpec as P

TILE = 64
LANES = 128
HALF = TILE // 2
GROUP = LANES // HALF
STEPS = 32000.0
F32 = jnp.float32
BF16 = jnp.bfloat16
VMEM = pl.BlockSpec(memory_space=pltpu.VMEM)
ANY = pl.BlockSpec(memory_space=pl.ANY)
SMEM = pl.BlockSpec(memory_space=pltpu.SMEM)
PARAMS = pltpu.CompilerParams(vmem_limit_bytes=48 * 1024 * 1024)


def row_spread():
    out = np.zeros((LANES, 2, 2, GROUP, HALF), np.float32)
    for q in range(2):
        for e in range(2):
            for m in range(HALF):
                out[q * TILE + 2 * m + e, q, e, :, m] = 1
    return jnp.asarray(out.reshape(LANES, 4 * LANES), BF16)


def row_fold():
    out = np.zeros((2, 2, 2, GROUP // 2, HALF, LANES), np.float32)
    for q in range(2):
        for e in range(2):
            for m in range(HALF):
                out[q, 0, e, :, m, q * TILE + 2 * m + e] = 1
                out[q, 1, 1 - e, :, m, q * TILE + 2 * m + e] = 1
    return jnp.asarray(out.reshape(4 * LANES, LANES), BF16)


def encode(values, out_ref):
    width, piece = values[0].shape[0], LANES * len(values)
    lane = lax.broadcasted_iota(jnp.int32, (width, LANES), 1)
    exponents = jnp.zeros((width, LANES), F32)
    for n, value in enumerate(values):
        top = jnp.max(jnp.abs(value), axis=1, keepdims=True)
        e = jnp.clip(jnp.ceil(jnp.log2(top)), -100.0, 100.0)
        exponents = jnp.where(lane == n, e, exponents)
        scaled = jnp.floor(value * (STEPS * jnp.exp2(-e)) + 0.5)
        out_ref[:, n * LANES : (n + 1) * LANES] = scaled.astype(jnp.int32).astype(jnp.int16)
    out_ref[:, piece:] = exponents.astype(jnp.int32).astype(jnp.int16)


def decode(ref):
    chunks = ref.shape[1] // LANES - 1
    exponents = ref[:, chunks * LANES :].astype(jnp.int32).astype(F32)
    scales = jnp.exp2(exponents) * (1.0 / STEPS)
    return [
        ref[:, n * LANES : (n + 1) * LANES].astype(jnp.int32).astype(F32) * scales[:, n : n + 1]
        for n in range(chunks)
    ]


def prep_kernel(tiles_ref, out_ref, wide):
    for b in range(tiles_ref.shape[0]):
        wide[b] = tiles_ref[b].astype(F32).reshape(HALF * 8, LANES)
        for s in range(8):
            out_ref[8 * b + s] = wide[b, pl.ds(s, HALF, stride=8), :].astype(BF16)


def prep(tiles):
    slots = tiles.shape[0]
    blocks = slots // 8
    view = tiles.reshape(blocks, 8, HALF, LANES).swapaxes(1, 2)
    return pl.pallas_call(
        prep_kernel,
        in_specs=[VMEM],
        out_specs=VMEM,
        out_shape=jax.ShapeDtypeStruct((slots, HALF, LANES), BF16),
        scratch_shapes=[pltpu.VMEM((blocks, HALF * 8, LANES), F32)],
        compiler_params=PARAMS,
        cost_estimate=pl.CostEstimate(flops=0, bytes_accessed=4 * tiles.size, transcendentals=0),
        name="prep_tiles",
    )(view)


def build_table(pieces, spread, table):
    width, piece = pieces[0].shape
    pairs = piece // LANES
    for n, ref in enumerate(pieces):
        rows = jnp.concatenate([ref[:, p * LANES : (p + 1) * LANES] for p in range(pairs)], axis=0)
        wide = jnp.dot(rows, spread, preferred_element_type=F32)
        wide = wide.reshape(pairs, width, 4 * LANES)
        for q in range(2):
            both = jnp.concatenate(
                [wide[:, :, (2 * q + e) * LANES : (2 * q + e + 1) * LANES] for e in range(2)], axis=1
            ).astype(BF16)
            for p in range(pairs):
                table[n * 2 * pairs + 2 * p + q] = both[p]


def backward_kernel(n_in, rows_ref, cols_ref, count_ref, spread_ref, tiles_ref, *refs):
    pieces = refs[:n_in]
    _, keep_ref, *give_refs, table, acc_a, acc_b = refs[n_in:]
    per_give = give_refs[0].shape[0]
    n_out = 2 * keep_ref.shape[0]
    width, piece = pieces[0].shape
    per_piece = piece // TILE
    slots = tiles_ref.shape[0]
    build_table(pieces, spread_ref[...], table)
    for acc in (acc_a, acc_b):
        acc[...] = jnp.zeros_like(acc)
    lane = lax.broadcasted_iota(jnp.int32, (2 * width, LANES), 1)
    masks = [(lane // HALF == s).astype(BF16) for s in range(GROUP)]
    low = lax.broadcasted_iota(jnp.int32, (width, LANES), 1) < TILE
    count = count_ref[0, 0]
    row_flip = lax.axis_index("bcol") * per_piece
    col_flip = lax.axis_index("brow") * per_piece
    spare = n_out * per_piece

    for g in range(slots // GROUP):
        at = [table[rows_ref[g * GROUP + s] ^ row_flip] * masks[s] for s in range(GROUP)]
        block = tiles_ref[g * GROUP : (g + 1) * GROUP].reshape(LANES, LANES)
        out = jnp.dot(jnp.concatenate(at, axis=0), block, preferred_element_type=F32)
        for s in range(GROUP):
            t = g * GROUP + s
            part = out[2 * width * s : 2 * width * (s + 1)]
            part = jnp.where(low, part[:width], part[width:])
            c = jnp.where(t < count, cols_ref[t] ^ col_flip, spare)
            acc = acc_a if s % 2 == 0 else acc_b
            acc[c] += part

    for n in range(n_out):
        h = n // 2
        dest = keep_ref.at[h] if n % 2 == 0 else give_refs[h // per_give].at[h % per_give]
        for p in range(per_piece // 2):
            at = n * per_piece + 2 * p
            a = acc_a[at] + acc_b[at]
            b = acc_a[at + 1] + acc_b[at + 1]
            dest[:, p * LANES : (p + 1) * LANES] = jnp.where(low, a, b) + pltpu.roll(
                jnp.where(low, b, a), TILE, 1
            )


def backward(pieces, tiles, tile_rows, tile_cols, counts, n_out, after):
    n_in = len(pieces)
    width, piece = pieces[0].shape
    per_piece = piece // TILE
    half = jax.ShapeDtypeStruct((n_out // 2, width, piece), F32)
    quarter = jax.ShapeDtypeStruct((n_out // 4, width, piece), F32)
    return pl.pallas_call(
        functools.partial(backward_kernel, n_in),
        in_specs=[SMEM] * 3 + [VMEM] * (2 + n_in) + [ANY],
        out_specs=[VMEM] * 3,
        out_shape=[half, quarter, quarter],
        scratch_shapes=[
            pltpu.VMEM((n_in * per_piece, 2 * width, LANES), BF16),
            pltpu.VMEM((n_out * per_piece + 1, width, LANES), F32),
            pltpu.VMEM((n_out * per_piece + 1, width, LANES), F32),
        ],
        compiler_params=PARAMS,
        cost_estimate=pl.CostEstimate(
            flops=2 * tiles.size * 64, bytes_accessed=4 * tiles.size, transcendentals=0
        ),
        name="transpose_product",
    )(tile_rows, tile_cols, counts, row_spread(), tiles, *pieces, after)


def double_table(pieces, table):
    width, piece = pieces[0].shape
    low = lax.broadcasted_iota(jnp.int32, (width, LANES), 1) < TILE
    for n, ref in enumerate(pieces):
        for p in range(piece // LANES):
            pair = ref[:, p * LANES : (p + 1) * LANES].astype(F32)
            turned = pltpu.roll(pair, TILE, 1)
            at = (n * piece + p * LANES) // TILE
            table[at] = jnp.where(low, pair, turned)
            table[at + 1] = jnp.where(low, turned, pair)


def forward_kernel(
    rows_ref,
    cols_ref,
    count_ref,
    fold_ref,
    tiles_ref,
    same_ref,
    other_ref,
    after_ref,
    keep_ref,
    give_ref,
    table,
    acc_a,
    acc_b,
):
    pieces = [ref.at[h] for h in range(same_ref.shape[0]) for ref in (same_ref, other_ref)]
    n_out = 2 * keep_ref.shape[0]
    width, piece = pieces[0].shape
    per_piece = piece // TILE
    slots = tiles_ref.shape[0]
    double_table(pieces, table)
    for acc in (acc_a, acc_b):
        acc[...] = jnp.zeros_like(acc)
    lane = lax.broadcasted_iota(jnp.int32, (width, LANES), 1)
    masks = [lane // HALF == s for s in range(GROUP)]
    wide_lane = lax.broadcasted_iota(jnp.int32, (LANES, LANES), 1)
    parity = [(wide_lane // TILE == e).astype(BF16) for e in range(2)]
    count = count_ref[0, 0]
    row_flip = lax.axis_index("bcol") * per_piece
    col_flip = lax.axis_index("brow") * per_piece
    spare = n_out * per_piece

    for g in range(slots // GROUP):
        at = [table[cols_ref[g * GROUP + s] ^ col_flip] for s in range(GROUP)]
        block = tiles_ref[g * GROUP : (g + 1) * GROUP].reshape(LANES, LANES)
        turned = jnp.concatenate([block[LANES // 2 :], block[: LANES // 2]], axis=0)
        out = lax.dot_general(
            jnp.concatenate(at, axis=0).astype(BF16),
            jnp.concatenate([block * parity[0], turned * parity[1]], axis=0),
            (((1,), (1,)), ((), ())),
            preferred_element_type=F32,
        )
        for s in range(GROUP):
            t = g * GROUP + s
            part = out[width * s : width * (s + 1)]
            r = jnp.where(t < count, rows_ref[t] ^ row_flip, spare)
            part = jnp.where(
                masks[s], part[:, :LANES], jnp.where(masks[(s + 2) % GROUP], part[:, LANES:], 0.0)
            )
            acc = acc_a if s < 2 else acc_b
            acc[r] += part

    fold = fold_ref[...]
    pairs = per_piece // 2
    for n in range(n_out):
        blocks = []
        for q in range(2):
            for acc in (acc_a, acc_b):
                both = acc[n * per_piece : (n + 1) * per_piece].reshape(pairs, 2 * width, LANES)
                blocks.append(both[:, q * width : (q + 1) * width, :].reshape(pairs * width, LANES))
        wide = jnp.concatenate(blocks, axis=1)
        first = wide.astype(BF16)
        rest = (wide - first.astype(F32)).astype(BF16)
        out = jnp.dot(first, fold, preferred_element_type=F32)
        out = out + jnp.dot(rest, fold, preferred_element_type=F32)
        parts = [out[p * width : (p + 1) * width] for p in range(pairs)]
        if n % 2 == 0:
            for p in range(pairs):
                keep_ref[n // 2, :, p * LANES : (p + 1) * LANES] = parts[p]
        else:
            encode(parts, give_ref.at[n // 2])


def forward(same, other, tiles, tile_rows, tile_cols, counts, n_out, after):
    n_chips, width, piece = same.shape
    per_piece = piece // TILE
    half = jax.ShapeDtypeStruct((n_out // 2, width, piece), F32)
    coded = jax.ShapeDtypeStruct((n_out // 2, width, piece + LANES), jnp.int16)
    return pl.pallas_call(
        forward_kernel,
        in_specs=[SMEM] * 3 + [VMEM] * 4 + [ANY],
        out_specs=[VMEM] * 2,
        out_shape=[half, coded],
        scratch_shapes=[
            pltpu.VMEM((2 * n_chips * per_piece, width, LANES), F32),
            pltpu.VMEM((n_out * per_piece + 1, width, LANES), F32),
            pltpu.VMEM((n_out * per_piece + 1, width, LANES), F32),
        ],
        compiler_params=PARAMS,
        cost_estimate=pl.CostEstimate(
            flops=2 * tiles.size * 64, bytes_accessed=4 * tiles.size, transcendentals=0
        ),
        name="forward_product",
    )(tile_rows, tile_cols, counts, row_fold(), tiles, same, other, after)


def stack_kernel(n_after, *refs):
    out_ref, at = refs[-1], 0
    for ref in refs[: -1 - n_after]:
        if len(ref.shape) == 2:
            out_ref[at] = ref[...]
            at += 1
        else:
            out_ref[at : at + ref.shape[0]] = ref[...]
            at += ref.shape[0]


def stack(*parts, after=()):
    total = sum(x.shape[0] if x.ndim == 3 else 1 for x in parts)
    return pl.pallas_call(
        functools.partial(stack_kernel, len(after)),
        in_specs=[VMEM] * len(parts) + [ANY] * len(after),
        out_specs=VMEM,
        out_shape=jax.ShapeDtypeStruct((total,) + parts[0].shape[-2:], parts[0].dtype),
        compiler_params=PARAMS,
        name="stack_pieces",
    )(*parts, *after)


def pair_sum_kernel(keep_ref, *refs):
    n_chips = keep_ref.shape[0]
    gots, outs = refs[: 1 - n_chips], refs[1 - n_chips :]
    got = [ref.at[h] for ref in gots for h in range(ref.shape[0])]
    for h, out in enumerate(outs):
        out[...] = keep_ref[h + 1] + got[h + 1][...]


def pair_sum(keep, gots):
    parts, width, piece = keep.shape
    return pl.pallas_call(
        pair_sum_kernel,
        in_specs=[VMEM] * (1 + len(gots)),
        out_specs=[VMEM] * (parts - 1),
        out_shape=[jax.ShapeDtypeStruct((width, piece), F32)] * (parts - 1),
        compiler_params=PARAMS,
        name="core_pair_sum",
    )(keep, *gots)


def split_sum_kernel(keep_ref, got_ref, after_ref, next_keep, next_give):
    for h in range(next_keep.shape[0]):
        for n, got in enumerate(decode(got_ref.at[2 * h])):
            at = pl.ds(n * LANES, LANES)
            next_keep[h, :, at] = keep_ref[2 * h, :, at] + got
        sums = [
            keep_ref[2 * h + 1, :, n * LANES : (n + 1) * LANES] + got
            for n, got in enumerate(decode(got_ref.at[2 * h + 1]))
        ]
        encode(sums, next_give.at[h])


def split_sum(keep, got, after):
    parts, width, piece = keep.shape
    return pl.pallas_call(
        split_sum_kernel,
        in_specs=[VMEM] * 2 + [ANY],
        out_specs=[VMEM] * 2,
        out_shape=[
            jax.ShapeDtypeStruct((parts // 2, width, piece), F32),
            jax.ShapeDtypeStruct((parts // 2,) + got.shape[1:], got.dtype),
        ],
        compiler_params=PARAMS,
        name="halving_sum",
    )(keep, got, after)


def last_sum_kernel(*refs):
    chips, (brow_keep, brow_got, keep_ref, got_ref, out_ref) = refs[:-5], refs[-5:]
    for n, got in enumerate(decode(got_ref.at[0])):
        at = pl.ds(n * LANES, LANES)
        total = brow_keep[0, :, at] + brow_got[0, :, at]
        for ref in chips:
            total = total + ref[:, at]
        out_ref[:, at] = total + (keep_ref[0, :, at] + got)


def last_sum(keep, got, brow_keep, brow_got, chips):
    return pl.pallas_call(
        last_sum_kernel,
        in_specs=[VMEM] * (4 + len(chips)),
        out_specs=VMEM,
        out_shape=jax.ShapeDtypeStruct(keep.shape[1:], F32),
        compiler_params=PARAMS,
        name="last_sum",
    )(*chips, brow_keep, brow_got, keep, got)


def swap(x, axis, size, d):
    return lax.ppermute(x, axis, [(i, i ^ d) for i in range(size)])


def body(vectors, tiles, tile_rows, tile_cols, counts):
    n_rows = lax.axis_size("brow")
    n_cols = lax.axis_size("bcol")
    own = stack(vectors)
    chips = [swap(vectors, "brow", n_rows, 2 * h) for h in range(1, n_rows // 2)]
    row_pieces = [own[0]] + [swap(vectors, "bcol", n_cols, d) for d in range(1, n_cols)]
    blocks = prep(tiles)
    same = stack(own, *chips, after=(blocks, *row_pieces[1:]))
    other = swap(same, "brow", n_rows, 1)

    col_keep, *col_give = backward(row_pieces, blocks, tile_rows, tile_cols, counts, n_rows, same)
    row_keep, give = forward(same, other, blocks, tile_rows, tile_cols, counts, n_cols, col_give[0])
    col_got = [swap(x, "brow", n_rows, 1) for x in col_give]
    sums = pair_sum(col_keep, col_got)
    from_chips = [swap(x, "brow", n_rows, 2 * (h + 1)) for h, x in enumerate(sums)]
    row_got, d = swap(give, "bcol", n_cols, 1), 2
    while d < n_cols:
        row_keep, give = split_sum(row_keep, row_got, sums[0])
        row_got = swap(give, "bcol", n_cols, d)
        d *= 2
    return last_sum(row_keep, row_got, col_keep, col_got[0], from_chips)


def solution(mesh):
    return jax.shard_map(
        body,
        mesh=mesh,
        in_specs=(
            P(None, ("brow", "bcol")),
            P(("brow", "bcol"), None),
            P(("brow", "bcol")),
            P(("brow", "bcol")),
            P("brow", "bcol"),
        ),
        out_specs=P(None, ("brow", "bcol")),
        check_vma=False,
    )
```

```python
import functools

import jax
import jax.numpy as jnp
import numpy as np
from jax import lax
from jax.experimental import pallas as pl
from jax.experimental.pallas import tpu as pltpu
from jax.sharding import PartitionSpec as P

TILE = 64
LANES = 128
HALF = TILE // 2
GROUP = LANES // HALF
STEPS = 32000.0
F32 = jnp.float32
BF16 = jnp.bfloat16
VMEM = pl.BlockSpec(memory_space=pltpu.VMEM)
ANY = pl.BlockSpec(memory_space=pl.ANY)
SMEM = pl.BlockSpec(memory_space=pltpu.SMEM)
PARAMS = pltpu.CompilerParams(vmem_limit_bytes=48 * 1024 * 1024)


def row_spread():
    out = np.zeros((LANES, 2, 2, GROUP, HALF), np.float32)
    for q in range(2):
        for e in range(2):
            for m in range(HALF):
                out[q * TILE + 2 * m + e, q, e, :, m] = 1
    return jnp.asarray(out.reshape(LANES, 4 * LANES), BF16)


def row_fold():
    out = np.zeros((2, 2, 2, GROUP // 2, HALF, LANES), np.float32)
    for q in range(2):
        for e in range(2):
            for m in range(HALF):
                out[q, 0, e, :, m, q * TILE + 2 * m + e] = 1
                out[q, 1, 1 - e, :, m, q * TILE + 2 * m + e] = 1
    return jnp.asarray(out.reshape(4 * LANES, LANES), BF16)


def encode(values, out_ref):
    width, piece = values[0].shape[0], LANES * len(values)
    lane = lax.broadcasted_iota(jnp.int32, (width, LANES), 1)
    exponents = jnp.zeros((width, LANES), F32)
    for n, value in enumerate(values):
        top = jnp.max(jnp.abs(value), axis=1, keepdims=True)
        e = jnp.clip(jnp.ceil(jnp.log2(top)), -100.0, 100.0)
        exponents = jnp.where(lane == n, e, exponents)
        scaled = jnp.floor(value * (STEPS * jnp.exp2(-e)) + 0.5)
        out_ref[:, n * LANES : (n + 1) * LANES] = scaled.astype(jnp.int32).astype(jnp.int16)
    out_ref[:, piece:] = exponents.astype(jnp.int32).astype(jnp.int16)


def decode(ref):
    chunks = ref.shape[1] // LANES - 1
    exponents = ref[:, chunks * LANES :].astype(jnp.int32).astype(F32)
    scales = jnp.exp2(exponents) * (1.0 / STEPS)
    return [
        ref[:, n * LANES : (n + 1) * LANES].astype(jnp.int32).astype(F32) * scales[:, n : n + 1]
        for n in range(chunks)
    ]


def prep_kernel(tiles_ref, out_ref, wide):
    for b in range(tiles_ref.shape[0]):
        wide[b] = tiles_ref[b].astype(F32).reshape(HALF * 8, LANES)
        for s in range(8):
            out_ref[8 * b + s] = wide[b, pl.ds(s, HALF, stride=8), :].astype(BF16)


def prep(tiles):
    slots = tiles.shape[0]
    blocks = slots // 8
    view = tiles.reshape(blocks, 8, HALF, LANES).swapaxes(1, 2)
    return pl.pallas_call(
        prep_kernel,
        in_specs=[VMEM],
        out_specs=VMEM,
        out_shape=jax.ShapeDtypeStruct((slots, HALF, LANES), BF16),
        scratch_shapes=[pltpu.VMEM((blocks, HALF * 8, LANES), F32)],
        compiler_params=PARAMS,
        cost_estimate=pl.CostEstimate(flops=0, bytes_accessed=4 * tiles.size, transcendentals=0),
        name="prep_tiles",
    )(view)


def build_table(pieces, spread, table):
    width, piece = pieces[0].shape
    pairs = piece // LANES
    for n, ref in enumerate(pieces):
        rows = jnp.concatenate([ref[:, p * LANES : (p + 1) * LANES] for p in range(pairs)], axis=0)
        wide = jnp.dot(rows, spread, preferred_element_type=F32)
        wide = wide.reshape(pairs, width, 4 * LANES)
        for q in range(2):
            both = jnp.concatenate(
                [wide[:, :, (2 * q + e) * LANES : (2 * q + e + 1) * LANES] for e in range(2)], axis=1
            ).astype(BF16)
            for p in range(pairs):
                table[n * 2 * pairs + 2 * p + q] = both[p]


def backward_kernel(n_in, rows_ref, cols_ref, count_ref, spread_ref, tiles_ref, *refs):
    pieces = refs[:n_in]
    _, keep_ref, *give_refs, table, acc_a, acc_b = refs[n_in:]
    per_give = give_refs[0].shape[0]
    n_out = 2 * keep_ref.shape[0]
    width, piece = pieces[0].shape
    per_piece = piece // TILE
    slots = tiles_ref.shape[0]
    build_table(pieces, spread_ref[...], table)
    for acc in (acc_a, acc_b):
        acc[...] = jnp.zeros_like(acc)
    lane = lax.broadcasted_iota(jnp.int32, (2 * width, LANES), 1)
    masks = [(lane // HALF == s).astype(BF16) for s in range(GROUP)]
    low = lax.broadcasted_iota(jnp.int32, (width, LANES), 1) < TILE
    count = count_ref[0, 0]
    row_flip = lax.axis_index("bcol") * per_piece
    col_flip = lax.axis_index("brow") * per_piece
    spare = n_out * per_piece

    for g in range(slots // GROUP):
        at = [table[rows_ref[g * GROUP + s] ^ row_flip] * masks[s] for s in range(GROUP)]
        block = tiles_ref[g * GROUP : (g + 1) * GROUP].reshape(LANES, LANES)
        out = jnp.dot(jnp.concatenate(at, axis=0), block, preferred_element_type=F32)
        for s in range(GROUP):
            t = g * GROUP + s
            part = out[2 * width * s : 2 * width * (s + 1)]
            part = jnp.where(low, part[:width], part[width:])
            c = jnp.where(t < count, cols_ref[t] ^ col_flip, spare)
            acc = acc_a if s % 2 == 0 else acc_b
            acc[c] += part

    for n in range(n_out):
        h = n // 2
        dest = keep_ref.at[h] if n % 2 == 0 else give_refs[h // per_give].at[h % per_give]
        for p in range(per_piece // 2):
            at = n * per_piece + 2 * p
            a = acc_a[at] + acc_b[at]
            b = acc_a[at + 1] + acc_b[at + 1]
            dest[:, p * LANES : (p + 1) * LANES] = jnp.where(low, a, b) + pltpu.roll(
                jnp.where(low, b, a), TILE, 1
            )


def backward(pieces, tiles, tile_rows, tile_cols, counts, n_out, after):
    n_in = len(pieces)
    width, piece = pieces[0].shape
    per_piece = piece // TILE
    half = jax.ShapeDtypeStruct((n_out // 2, width, piece), F32)
    quarter = jax.ShapeDtypeStruct((n_out // 4, width, piece), F32)
    return pl.pallas_call(
        functools.partial(backward_kernel, n_in),
        in_specs=[SMEM] * 3 + [VMEM] * (2 + n_in) + [ANY],
        out_specs=[VMEM] * 3,
        out_shape=[half, quarter, quarter],
        scratch_shapes=[
            pltpu.VMEM((n_in * per_piece, 2 * width, LANES), BF16),
            pltpu.VMEM((n_out * per_piece + 1, width, LANES), F32),
            pltpu.VMEM((n_out * per_piece + 1, width, LANES), F32),
        ],
        compiler_params=PARAMS,
        cost_estimate=pl.CostEstimate(
            flops=2 * tiles.size * 64, bytes_accessed=4 * tiles.size, transcendentals=0
        ),
        name="transpose_product",
    )(tile_rows, tile_cols, counts, row_spread(), tiles, *pieces, after)


def double_table(pieces, table):
    width, piece = pieces[0].shape
    low = lax.broadcasted_iota(jnp.int32, (width, LANES), 1) < TILE
    for n, ref in enumerate(pieces):
        for p in range(piece // LANES):
            pair = ref[:, p * LANES : (p + 1) * LANES].astype(F32)
            turned = pltpu.roll(pair, TILE, 1)
            at = (n * piece + p * LANES) // TILE
            table[at] = jnp.where(low, pair, turned)
            table[at + 1] = jnp.where(low, turned, pair)


def forward_kernel(
    rows_ref,
    cols_ref,
    count_ref,
    fold_ref,
    tiles_ref,
    same_ref,
    other_ref,
    after_ref,
    keep_ref,
    give_ref,
    table,
    acc_a,
    acc_b,
):
    pieces = [ref.at[h] for h in range(same_ref.shape[0]) for ref in (same_ref, other_ref)]
    n_out = 2 * keep_ref.shape[0]
    width, piece = pieces[0].shape
    per_piece = piece // TILE
    slots = tiles_ref.shape[0]
    double_table(pieces, table)
    for acc in (acc_a, acc_b):
        acc[...] = jnp.zeros_like(acc)
    lane = lax.broadcasted_iota(jnp.int32, (width, LANES), 1)
    masks = [lane // HALF == s for s in range(GROUP)]
    wide_lane = lax.broadcasted_iota(jnp.int32, (LANES, LANES), 1)
    parity = [(wide_lane // TILE == e).astype(BF16) for e in range(2)]
    count = count_ref[0, 0]
    row_flip = lax.axis_index("bcol") * per_piece
    col_flip = lax.axis_index("brow") * per_piece
    spare = n_out * per_piece

    for g in range(slots // GROUP):
        at = [table[cols_ref[g * GROUP + s] ^ col_flip] for s in range(GROUP)]
        block = tiles_ref[g * GROUP : (g + 1) * GROUP].reshape(LANES, LANES)
        turned = jnp.concatenate([block[LANES // 2 :], block[: LANES // 2]], axis=0)
        out = lax.dot_general(
            jnp.concatenate(at, axis=0).astype(BF16),
            jnp.concatenate([block * parity[0], turned * parity[1]], axis=0),
            (((1,), (1,)), ((), ())),
            preferred_element_type=F32,
        )
        for s in range(GROUP):
            t = g * GROUP + s
            part = out[width * s : width * (s + 1)]
            r = jnp.where(t < count, rows_ref[t] ^ row_flip, spare)
            part = jnp.where(
                masks[s], part[:, :LANES], jnp.where(masks[(s + 2) % GROUP], part[:, LANES:], 0.0)
            )
            acc = acc_a if s < 2 else acc_b
            acc[r] += part

    fold = fold_ref[...]
    pairs = per_piece // 2
    for n in range(n_out):
        blocks = []
        for q in range(2):
            for acc in (acc_a, acc_b):
                both = acc[n * per_piece : (n + 1) * per_piece].reshape(pairs, 2 * width, LANES)
                blocks.append(both[:, q * width : (q + 1) * width, :].reshape(pairs * width, LANES))
        wide = jnp.concatenate(blocks, axis=1)
        first = wide.astype(BF16)
        rest = (wide - first.astype(F32)).astype(BF16)
        out = jnp.dot(first, fold, preferred_element_type=F32)
        out = out + jnp.dot(rest, fold, preferred_element_type=F32)
        parts = [out[p * width : (p + 1) * width] for p in range(pairs)]
        if n % 2 == 0:
            for p in range(pairs):
                keep_ref[n // 2, :, p * LANES : (p + 1) * LANES] = parts[p]
        else:
            encode(parts, give_ref.at[n // 2])


def forward(same, other, tiles, tile_rows, tile_cols, counts, n_out, after):
    n_chips, width, piece = same.shape
    per_piece = piece // TILE
    half = jax.ShapeDtypeStruct((n_out // 2, width, piece), F32)
    coded = jax.ShapeDtypeStruct((n_out // 2, width, piece + LANES), jnp.int16)
    return pl.pallas_call(
        forward_kernel,
        in_specs=[SMEM] * 3 + [VMEM] * 4 + [ANY],
        out_specs=[VMEM] * 2,
        out_shape=[half, coded],
        scratch_shapes=[
            pltpu.VMEM((2 * n_chips * per_piece, width, LANES), F32),
            pltpu.VMEM((n_out * per_piece + 1, width, LANES), F32),
            pltpu.VMEM((n_out * per_piece + 1, width, LANES), F32),
        ],
        compiler_params=PARAMS,
        cost_estimate=pl.CostEstimate(
            flops=2 * tiles.size * 64, bytes_accessed=4 * tiles.size, transcendentals=0
        ),
        name="forward_product",
    )(tile_rows, tile_cols, counts, row_fold(), tiles, same, other, after)


def stack_kernel(n_after, *refs):
    out_ref, at = refs[-1], 0
    for ref in refs[: -1 - n_after]:
        if len(ref.shape) == 2:
            out_ref[at] = ref[...]
            at += 1
        else:
            out_ref[at : at + ref.shape[0]] = ref[...]
            at += ref.shape[0]


def stack(*parts, after=()):
    total = sum(x.shape[0] if x.ndim == 3 else 1 for x in parts)
    return pl.pallas_call(
        functools.partial(stack_kernel, len(after)),
        in_specs=[VMEM] * len(parts) + [ANY] * len(after),
        out_specs=VMEM,
        out_shape=jax.ShapeDtypeStruct((total,) + parts[0].shape[-2:], parts[0].dtype),
        compiler_params=PARAMS,
        name="stack_pieces",
    )(*parts, *after)


def pair_sum_kernel(after_ref, keep_ref, *refs):
    n_chips = keep_ref.shape[0]
    gots, outs = refs[: 1 - n_chips], refs[1 - n_chips :]
    got = [ref.at[h] for ref in gots for h in range(ref.shape[0])]
    for h, out in enumerate(outs):
        out[...] = keep_ref[h + 1] + got[h + 1][...]


def pair_sum(keep, gots, after):
    parts, width, piece = keep.shape
    return pl.pallas_call(
        pair_sum_kernel,
        in_specs=[ANY] + [VMEM] * (1 + len(gots)),
        out_specs=[VMEM] * (parts - 1),
        out_shape=[jax.ShapeDtypeStruct((width, piece), F32)] * (parts - 1),
        compiler_params=PARAMS,
        name="core_pair_sum",
    )(after, keep, *gots)


def split_sum_kernel(keep_ref, got_ref, after_ref, next_keep, next_give):
    for h in range(next_keep.shape[0]):
        for n, got in enumerate(decode(got_ref.at[2 * h])):
            at = pl.ds(n * LANES, LANES)
            next_keep[h, :, at] = keep_ref[2 * h, :, at] + got
        sums = [
            keep_ref[2 * h + 1, :, n * LANES : (n + 1) * LANES] + got
            for n, got in enumerate(decode(got_ref.at[2 * h + 1]))
        ]
        encode(sums, next_give.at[h])


def split_sum(keep, got, after):
    parts, width, piece = keep.shape
    return pl.pallas_call(
        split_sum_kernel,
        in_specs=[VMEM] * 2 + [ANY],
        out_specs=[VMEM] * 2,
        out_shape=[
            jax.ShapeDtypeStruct((parts // 2, width, piece), F32),
            jax.ShapeDtypeStruct((parts // 2,) + got.shape[1:], got.dtype),
        ],
        compiler_params=PARAMS,
        name="halving_sum",
    )(keep, got, after)


def last_sum_kernel(*refs):
    chips, (brow_keep, brow_got, keep_ref, got_ref, out_ref) = refs[:-5], refs[-5:]
    for n, got in enumerate(decode(got_ref.at[0])):
        at = pl.ds(n * LANES, LANES)
        total = brow_keep[0, :, at] + brow_got[0, :, at]
        for ref in chips:
            total = total + ref[:, at]
        out_ref[:, at] = total + (keep_ref[0, :, at] + got)


def last_sum(keep, got, brow_keep, brow_got, chips):
    return pl.pallas_call(
        last_sum_kernel,
        in_specs=[VMEM] * (4 + len(chips)),
        out_specs=VMEM,
        out_shape=jax.ShapeDtypeStruct(keep.shape[1:], F32),
        compiler_params=PARAMS,
        name="last_sum",
    )(*chips, brow_keep, brow_got, keep, got)


def swap(x, axis, size, d):
    return lax.ppermute(x, axis, [(i, i ^ d) for i in range(size)])


def body(vectors, tiles, tile_rows, tile_cols, counts):
    n_rows = lax.axis_size("brow")
    n_cols = lax.axis_size("bcol")
    own = stack(vectors)
    chips = [swap(vectors, "brow", n_rows, 2 * h) for h in range(1, n_rows // 2)]
    blocks = prep(tiles)
    same = stack(own, *chips, after=(blocks,))
    other = swap(same, "brow", n_rows, 1)
    row_pieces = [own[0]] + [swap(vectors, "bcol", n_cols, d) for d in range(1, n_cols)]

    row_keep, give = forward(same, other, blocks, tile_rows, tile_cols, counts, n_cols, own)
    col_keep, *col_give = backward(row_pieces, blocks, tile_rows, tile_cols, counts, n_rows, give)
    col_got = [swap(x, "brow", n_rows, 1) for x in col_give]
    sums = pair_sum(col_keep, col_got, give)
    from_chips = [swap(x, "brow", n_rows, 2 * (h + 1)) for h, x in enumerate(sums)]
    row_got, d = swap(give, "bcol", n_cols, 1), 2
    while d < n_cols:
        row_keep, give = split_sum(row_keep, row_got, sums[0])
        row_got = swap(give, "bcol", n_cols, d)
        d *= 2
    return last_sum(row_keep, row_got, col_keep, col_got[0], from_chips)


def solution(mesh):
    return jax.shard_map(
        body,
        mesh=mesh,
        in_specs=(
            P(None, ("brow", "bcol")),
            P(("brow", "bcol"), None),
            P(("brow", "bcol")),
            P(("brow", "bcol")),
            P("brow", "bcol"),
        ),
        out_specs=P(None, ("brow", "bcol")),
        check_vma=False,
    )
```

```python
import functools

import jax
import jax.numpy as jnp
import numpy as np
from jax import lax
from jax.experimental import pallas as pl
from jax.experimental.pallas import tpu as pltpu
from jax.sharding import PartitionSpec as P

TILE = 64
LANES = 128
HALF = TILE // 2
GROUP = LANES // HALF
STEPS = 32000.0
F32 = jnp.float32
BF16 = jnp.bfloat16
VMEM = pl.BlockSpec(memory_space=pltpu.VMEM)
ANY = pl.BlockSpec(memory_space=pl.ANY)
SMEM = pl.BlockSpec(memory_space=pltpu.SMEM)
PARAMS = pltpu.CompilerParams(vmem_limit_bytes=48 * 1024 * 1024)


def row_spread():
    out = np.zeros((LANES, 2, 2, GROUP, HALF), np.float32)
    for q in range(2):
        for e in range(2):
            for m in range(HALF):
                out[q * TILE + 2 * m + e, q, e, :, m] = 1
    return jnp.asarray(out.reshape(LANES, 4 * LANES), BF16)


def row_fold():
    out = np.zeros((2, 2, 2, GROUP // 2, HALF, LANES), np.float32)
    for q in range(2):
        for e in range(2):
            for m in range(HALF):
                out[q, 0, e, :, m, q * TILE + 2 * m + e] = 1
                out[q, 1, 1 - e, :, m, q * TILE + 2 * m + e] = 1
    return jnp.asarray(out.reshape(4 * LANES, LANES), BF16)


def encode(values, out_ref):
    width, piece = values[0].shape[0], LANES * len(values)
    lane = lax.broadcasted_iota(jnp.int32, (width, LANES), 1)
    exponents = jnp.zeros((width, LANES), F32)
    for n, value in enumerate(values):
        top = jnp.max(jnp.abs(value), axis=1, keepdims=True)
        e = jnp.clip(jnp.ceil(jnp.log2(top)), -100.0, 100.0)
        exponents = jnp.where(lane == n, e, exponents)
        scaled = jnp.floor(value * (STEPS * jnp.exp2(-e)) + 0.5)
        out_ref[:, n * LANES : (n + 1) * LANES] = scaled.astype(jnp.int32).astype(jnp.int16)
    out_ref[:, piece:] = exponents.astype(jnp.int32).astype(jnp.int16)


def decode(ref):
    chunks = ref.shape[1] // LANES - 1
    exponents = ref[:, chunks * LANES :].astype(jnp.int32).astype(F32)
    scales = jnp.exp2(exponents) * (1.0 / STEPS)
    return [
        ref[:, n * LANES : (n + 1) * LANES].astype(jnp.int32).astype(F32) * scales[:, n : n + 1]
        for n in range(chunks)
    ]


def prep_kernel(tiles_ref, out_ref, wide):
    for b in range(tiles_ref.shape[0]):
        wide[b] = tiles_ref[b].astype(F32).reshape(HALF * 8, LANES)
        for s in range(8):
            out_ref[8 * b + s] = wide[b, pl.ds(s, HALF, stride=8), :].astype(BF16)


def prep(tiles):
    slots = tiles.shape[0]
    blocks = slots // 8
    view = tiles.reshape(blocks, 8, HALF, LANES).swapaxes(1, 2)
    return pl.pallas_call(
        prep_kernel,
        in_specs=[VMEM],
        out_specs=VMEM,
        out_shape=jax.ShapeDtypeStruct((slots, HALF, LANES), BF16),
        scratch_shapes=[pltpu.VMEM((blocks, HALF * 8, LANES), F32)],
        compiler_params=PARAMS,
        cost_estimate=pl.CostEstimate(flops=0, bytes_accessed=4 * tiles.size, transcendentals=0),
        name="prep_tiles",
    )(view)


def build_table(pieces, spread, table):
    width, piece = pieces[0].shape
    pairs = piece // LANES
    for n, ref in enumerate(pieces):
        rows = jnp.concatenate([ref[:, p * LANES : (p + 1) * LANES] for p in range(pairs)], axis=0)
        wide = jnp.dot(rows, spread, preferred_element_type=F32)
        wide = wide.reshape(pairs, width, 4 * LANES)
        for q in range(2):
            both = jnp.concatenate(
                [wide[:, :, (2 * q + e) * LANES : (2 * q + e + 1) * LANES] for e in range(2)], axis=1
            ).astype(BF16)
            for p in range(pairs):
                table[n * 2 * pairs + 2 * p + q] = both[p]


def backward_kernel(
    rows_ref, cols_ref, count_ref, spread_ref, tiles_ref, seg_ref, after_ref, keep_ref, *refs
):
    pieces = [seg_ref.at[n] for n in range(seg_ref.shape[0])]
    *give_refs, table, acc_a, acc_b = refs
    per_give = give_refs[0].shape[0]
    n_out = 2 * keep_ref.shape[0]
    width, piece = pieces[0].shape
    per_piece = piece // TILE
    slots = tiles_ref.shape[0]
    build_table(pieces, spread_ref[...], table)
    for acc in (acc_a, acc_b):
        acc[...] = jnp.zeros_like(acc)
    lane = lax.broadcasted_iota(jnp.int32, (2 * width, LANES), 1)
    masks = [(lane // HALF == s).astype(BF16) for s in range(GROUP)]
    low = lax.broadcasted_iota(jnp.int32, (width, LANES), 1) < TILE
    count = count_ref[0, 0]
    row_flip = lax.axis_index("bcol") * per_piece
    col_flip = lax.axis_index("brow") * per_piece
    spare = n_out * per_piece

    for g in range(slots // GROUP):
        at = [table[rows_ref[g * GROUP + s] ^ row_flip] * masks[s] for s in range(GROUP)]
        block = tiles_ref[g * GROUP : (g + 1) * GROUP].reshape(LANES, LANES)
        out = jnp.dot(jnp.concatenate(at, axis=0), block, preferred_element_type=F32)
        for s in range(GROUP):
            t = g * GROUP + s
            part = out[2 * width * s : 2 * width * (s + 1)]
            part = jnp.where(low, part[:width], part[width:])
            c = jnp.where(t < count, cols_ref[t] ^ col_flip, spare)
            acc = acc_a if s % 2 == 0 else acc_b
            acc[c] += part

    for n in range(n_out):
        h = n // 2
        dest = keep_ref.at[h] if n % 2 == 0 else give_refs[h // per_give].at[h % per_give]
        for p in range(per_piece // 2):
            at = n * per_piece + 2 * p
            a = acc_a[at] + acc_b[at]
            b = acc_a[at + 1] + acc_b[at + 1]
            dest[:, p * LANES : (p + 1) * LANES] = jnp.where(low, a, b) + pltpu.roll(
                jnp.where(low, b, a), TILE, 1
            )


def backward(segment, tiles, tile_rows, tile_cols, counts, n_out, after):
    n_in, width, piece = segment.shape
    per_piece = piece // TILE
    half = jax.ShapeDtypeStruct((n_out // 2, width, piece), F32)
    quarter = jax.ShapeDtypeStruct((n_out // 4, width, piece), F32)
    return pl.pallas_call(
        backward_kernel,
        in_specs=[SMEM] * 3 + [VMEM] * 3 + [ANY],
        out_specs=[VMEM] * 3,
        out_shape=[half, quarter, quarter],
        scratch_shapes=[
            pltpu.VMEM((n_in * per_piece, 2 * width, LANES), BF16),
            pltpu.VMEM((n_out * per_piece + 1, width, LANES), F32),
            pltpu.VMEM((n_out * per_piece + 1, width, LANES), F32),
        ],
        compiler_params=PARAMS,
        cost_estimate=pl.CostEstimate(
            flops=2 * tiles.size * 64, bytes_accessed=4 * tiles.size, transcendentals=0
        ),
        name="transpose_product",
    )(tile_rows, tile_cols, counts, row_spread(), tiles, segment, after)


def double_table(pieces, table):
    width, piece = pieces[0].shape
    low = lax.broadcasted_iota(jnp.int32, (width, LANES), 1) < TILE
    for n, ref in enumerate(pieces):
        for p in range(piece // LANES):
            pair = ref[:, p * LANES : (p + 1) * LANES].astype(F32)
            turned = pltpu.roll(pair, TILE, 1)
            at = (n * piece + p * LANES) // TILE
            table[at] = jnp.where(low, pair, turned)
            table[at + 1] = jnp.where(low, turned, pair)


def forward_kernel(
    rows_ref,
    cols_ref,
    count_ref,
    fold_ref,
    tiles_ref,
    same_ref,
    other_ref,
    after_ref,
    keep_ref,
    give_ref,
    table,
    acc_a,
    acc_b,
):
    pieces = [ref.at[h] for h in range(same_ref.shape[0]) for ref in (same_ref, other_ref)]
    n_out = 2 * keep_ref.shape[0]
    width, piece = pieces[0].shape
    per_piece = piece // TILE
    slots = tiles_ref.shape[0]
    double_table(pieces, table)
    for acc in (acc_a, acc_b):
        acc[...] = jnp.zeros_like(acc)
    lane = lax.broadcasted_iota(jnp.int32, (width, LANES), 1)
    masks = [lane // HALF == s for s in range(GROUP)]
    wide_lane = lax.broadcasted_iota(jnp.int32, (LANES, LANES), 1)
    parity = [(wide_lane // TILE == e).astype(BF16) for e in range(2)]
    count = count_ref[0, 0]
    row_flip = lax.axis_index("bcol") * per_piece
    col_flip = lax.axis_index("brow") * per_piece
    spare = n_out * per_piece

    for g in range(slots // GROUP):
        at = [table[cols_ref[g * GROUP + s] ^ col_flip] for s in range(GROUP)]
        block = tiles_ref[g * GROUP : (g + 1) * GROUP].reshape(LANES, LANES)
        turned = jnp.concatenate([block[LANES // 2 :], block[: LANES // 2]], axis=0)
        out = lax.dot_general(
            jnp.concatenate(at, axis=0).astype(BF16),
            jnp.concatenate([block * parity[0], turned * parity[1]], axis=0),
            (((1,), (1,)), ((), ())),
            preferred_element_type=F32,
        )
        for s in range(GROUP):
            t = g * GROUP + s
            part = out[width * s : width * (s + 1)]
            r = jnp.where(t < count, rows_ref[t] ^ row_flip, spare)
            part = jnp.where(
                masks[s], part[:, :LANES], jnp.where(masks[(s + 2) % GROUP], part[:, LANES:], 0.0)
            )
            acc = acc_a if s < 2 else acc_b
            acc[r] += part

    fold = fold_ref[...]
    pairs = per_piece // 2
    for n in range(n_out):
        blocks = []
        for q in range(2):
            for acc in (acc_a, acc_b):
                both = acc[n * per_piece : (n + 1) * per_piece].reshape(pairs, 2 * width, LANES)
                blocks.append(both[:, q * width : (q + 1) * width, :].reshape(pairs * width, LANES))
        wide = jnp.concatenate(blocks, axis=1)
        first = wide.astype(BF16)
        rest = (wide - first.astype(F32)).astype(BF16)
        out = jnp.dot(first, fold, preferred_element_type=F32)
        out = out + jnp.dot(rest, fold, preferred_element_type=F32)
        parts = [out[p * width : (p + 1) * width] for p in range(pairs)]
        if n % 2 == 0:
            for p in range(pairs):
                keep_ref[n // 2, :, p * LANES : (p + 1) * LANES] = parts[p]
        else:
            encode(parts, give_ref.at[n // 2])


def forward(same, other, tiles, tile_rows, tile_cols, counts, n_out, after):
    n_chips, width, piece = same.shape
    per_piece = piece // TILE
    half = jax.ShapeDtypeStruct((n_out // 2, width, piece), F32)
    coded = jax.ShapeDtypeStruct((n_out // 2, width, piece + LANES), jnp.int16)
    return pl.pallas_call(
        forward_kernel,
        in_specs=[SMEM] * 3 + [VMEM] * 4 + [ANY],
        out_specs=[VMEM] * 2,
        out_shape=[half, coded],
        scratch_shapes=[
            pltpu.VMEM((2 * n_chips * per_piece, width, LANES), F32),
            pltpu.VMEM((n_out * per_piece + 1, width, LANES), F32),
            pltpu.VMEM((n_out * per_piece + 1, width, LANES), F32),
        ],
        compiler_params=PARAMS,
        cost_estimate=pl.CostEstimate(
            flops=2 * tiles.size * 64, bytes_accessed=4 * tiles.size, transcendentals=0
        ),
        name="forward_product",
    )(tile_rows, tile_cols, counts, row_fold(), tiles, same, other, after)


def stack_kernel(n_after, *refs):
    out_ref, at = refs[-1], 0
    for ref in refs[: -1 - n_after]:
        if len(ref.shape) == 2:
            out_ref[at] = ref[...]
            at += 1
        else:
            out_ref[at : at + ref.shape[0]] = ref[...]
            at += ref.shape[0]


def stack(*parts, after=()):
    total = sum(x.shape[0] if x.ndim == 3 else 1 for x in parts)
    return pl.pallas_call(
        functools.partial(stack_kernel, len(after)),
        in_specs=[VMEM] * len(parts) + [ANY] * len(after),
        out_specs=VMEM,
        out_shape=jax.ShapeDtypeStruct((total,) + parts[0].shape[-2:], parts[0].dtype),
        compiler_params=PARAMS,
        name="stack_pieces",
    )(*parts, *after)


def pair_sum_kernel(keep_ref, *refs):
    n_chips = keep_ref.shape[0]
    gots, outs = refs[: 1 - n_chips], refs[1 - n_chips :]
    got = [ref.at[h] for ref in gots for h in range(ref.shape[0])]
    for h, out in enumerate(outs):
        out[...] = keep_ref[h + 1] + got[h + 1][...]


def pair_sum(keep, gots):
    parts, width, piece = keep.shape
    return pl.pallas_call(
        pair_sum_kernel,
        in_specs=[VMEM] * (1 + len(gots)),
        out_specs=[VMEM] * (parts - 1),
        out_shape=[jax.ShapeDtypeStruct((width, piece), F32)] * (parts - 1),
        compiler_params=PARAMS,
        name="core_pair_sum",
    )(keep, *gots)


def split_sum_kernel(keep_ref, got_ref, after_ref, next_keep, next_give):
    for h in range(next_keep.shape[0]):
        for n, got in enumerate(decode(got_ref.at[2 * h])):
            at = pl.ds(n * LANES, LANES)
            next_keep[h, :, at] = keep_ref[2 * h, :, at] + got
        sums = [
            keep_ref[2 * h + 1, :, n * LANES : (n + 1) * LANES] + got
            for n, got in enumerate(decode(got_ref.at[2 * h + 1]))
        ]
        encode(sums, next_give.at[h])


def split_sum(keep, got, after):
    parts, width, piece = keep.shape
    return pl.pallas_call(
        split_sum_kernel,
        in_specs=[VMEM] * 2 + [ANY],
        out_specs=[VMEM] * 2,
        out_shape=[
            jax.ShapeDtypeStruct((parts // 2, width, piece), F32),
            jax.ShapeDtypeStruct((parts // 2,) + got.shape[1:], got.dtype),
        ],
        compiler_params=PARAMS,
        name="halving_sum",
    )(keep, got, after)


def last_sum_kernel(*refs):
    chips, (brow_keep, brow_got, keep_ref, got_ref, out_ref) = refs[:-5], refs[-5:]
    for n, got in enumerate(decode(got_ref.at[0])):
        at = pl.ds(n * LANES, LANES)
        total = brow_keep[0, :, at] + brow_got[0, :, at]
        for ref in chips:
            total = total + ref[:, at]
        out_ref[:, at] = total + (keep_ref[0, :, at] + got)


def last_sum(keep, got, brow_keep, brow_got, chips):
    return pl.pallas_call(
        last_sum_kernel,
        in_specs=[VMEM] * (4 + len(chips)),
        out_specs=VMEM,
        out_shape=jax.ShapeDtypeStruct(keep.shape[1:], F32),
        compiler_params=PARAMS,
        name="last_sum",
    )(*chips, brow_keep, brow_got, keep, got)


def swap(x, axis, size, d):
    return lax.ppermute(x, axis, [(i, i ^ d) for i in range(size)])


def body(vectors, tiles, tile_rows, tile_cols, counts):
    n_rows = lax.axis_size("brow")
    n_cols = lax.axis_size("bcol")
    own = stack(vectors)
    chips = [swap(vectors, "brow", n_rows, 2 * h) for h in range(1, n_rows // 2)]
    segment, d = own, 1
    while d < n_cols:
        segment = stack(segment, swap(segment if d > 1 else vectors[None], "bcol", n_cols, d))
        d *= 2
    blocks = prep(tiles)
    same = stack(own, *chips, after=(blocks,))
    other = swap(same, "brow", n_rows, 1)

    col_keep, *col_give = backward(segment, blocks, tile_rows, tile_cols, counts, n_rows, same)
    row_keep, give = forward(same, other, blocks, tile_rows, tile_cols, counts, n_cols, col_give[0])
    col_got = [swap(x, "brow", n_rows, 1) for x in col_give]
    sums = pair_sum(col_keep, col_got)
    from_chips = [swap(x, "brow", n_rows, 2 * (h + 1)) for h, x in enumerate(sums)]
    row_got, d = swap(give, "bcol", n_cols, 1), 2
    while d < n_cols:
        row_keep, give = split_sum(row_keep, row_got, sums[0])
        row_got = swap(give, "bcol", n_cols, d)
        d *= 2
    return last_sum(row_keep, row_got, col_keep, col_got[0], from_chips)


def solution(mesh):
    return jax.shard_map(
        body,
        mesh=mesh,
        in_specs=(
            P(None, ("brow", "bcol")),
            P(("brow", "bcol"), None),
            P(("brow", "bcol")),
            P(("brow", "bcol")),
            P("brow", "bcol"),
        ),
        out_specs=P(None, ("brow", "bcol")),
        check_vma=False,
    )
```

```python
import functools

import jax
import jax.numpy as jnp
import numpy as np
from jax import lax
from jax.experimental import pallas as pl
from jax.experimental.pallas import tpu as pltpu
from jax.sharding import PartitionSpec as P

TILE = 64
LANES = 128
HALF = TILE // 2
GROUP = LANES // HALF
STEPS = 32000.0
F32 = jnp.float32
BF16 = jnp.bfloat16
VMEM = pl.BlockSpec(memory_space=pltpu.VMEM)
ANY = pl.BlockSpec(memory_space=pl.ANY)
SMEM = pl.BlockSpec(memory_space=pltpu.SMEM)
PARAMS = pltpu.CompilerParams(vmem_limit_bytes=48 * 1024 * 1024)


def row_spread():
    out = np.zeros((LANES, 2, 2, GROUP, HALF), np.float32)
    for q in range(2):
        for e in range(2):
            for m in range(HALF):
                out[q * TILE + 2 * m + e, q, e, :, m] = 1
    return jnp.asarray(out.reshape(LANES, 4 * LANES), BF16)


def row_fold():
    out = np.zeros((2, 2, 2, GROUP // 2, HALF, LANES), np.float32)
    for q in range(2):
        for e in range(2):
            for m in range(HALF):
                out[q, 0, e, :, m, q * TILE + 2 * m + e] = 1
                out[q, 1, 1 - e, :, m, q * TILE + 2 * m + e] = 1
    return jnp.asarray(out.reshape(4 * LANES, LANES), BF16)


def encode(values, out_ref):
    width, piece = values[0].shape[0], LANES * len(values)
    lane = lax.broadcasted_iota(jnp.int32, (width, LANES), 1)
    exponents = jnp.zeros((width, LANES), F32)
    for n, value in enumerate(values):
        top = jnp.max(jnp.abs(value), axis=1, keepdims=True)
        e = jnp.clip(jnp.ceil(jnp.log2(top)), -100.0, 100.0)
        exponents = jnp.where(lane == n, e, exponents)
        scaled = jnp.floor(value * (STEPS * jnp.exp2(-e)) + 0.5)
        out_ref[:, n * LANES : (n + 1) * LANES] = scaled.astype(jnp.int32).astype(jnp.int16)
    out_ref[:, piece:] = exponents.astype(jnp.int32).astype(jnp.int16)


def decode(ref):
    chunks = ref.shape[1] // LANES - 1
    exponents = ref[:, chunks * LANES :].astype(jnp.int32).astype(F32)
    scales = jnp.exp2(exponents) * (1.0 / STEPS)
    return [
        ref[:, n * LANES : (n + 1) * LANES].astype(jnp.int32).astype(F32) * scales[:, n : n + 1]
        for n in range(chunks)
    ]


def prep_kernel(tiles_ref, out_ref, wide):
    for b in range(tiles_ref.shape[0]):
        wide[b] = tiles_ref[b].astype(F32).reshape(HALF * 8, LANES)
        for s in range(8):
            out_ref[8 * b + s] = wide[b, pl.ds(s, HALF, stride=8), :].astype(BF16)


def prep(tiles):
    slots = tiles.shape[0]
    blocks = slots // 8
    view = tiles.reshape(blocks, 8, HALF, LANES).swapaxes(1, 2)
    return pl.pallas_call(
        prep_kernel,
        in_specs=[VMEM],
        out_specs=VMEM,
        out_shape=jax.ShapeDtypeStruct((slots, HALF, LANES), BF16),
        scratch_shapes=[pltpu.VMEM((blocks, HALF * 8, LANES), F32)],
        compiler_params=PARAMS,
        cost_estimate=pl.CostEstimate(flops=0, bytes_accessed=4 * tiles.size, transcendentals=0),
        name="prep_tiles",
    )(view)


def build_table(pieces, spread, table):
    width, piece = pieces[0].shape
    pairs = piece // LANES
    for n, ref in enumerate(pieces):
        rows = jnp.concatenate([ref[:, p * LANES : (p + 1) * LANES] for p in range(pairs)], axis=0)
        wide = jnp.dot(rows, spread, preferred_element_type=F32)
        wide = wide.reshape(pairs, width, 4 * LANES)
        for q in range(2):
            both = jnp.concatenate(
                [wide[:, :, (2 * q + e) * LANES : (2 * q + e + 1) * LANES] for e in range(2)], axis=1
            ).astype(BF16)
            for p in range(pairs):
                table[n * 2 * pairs + 2 * p + q] = both[p]


def backward_kernel(
    rows_ref, cols_ref, count_ref, spread_ref, tiles_ref, seg_ref, after_ref, keep_ref, *refs
):
    pieces = [seg_ref.at[n] for n in range(seg_ref.shape[0])]
    *give_refs, table, acc_a, acc_b = refs
    per_give = give_refs[0].shape[0]
    n_out = 2 * keep_ref.shape[0]
    width, piece = pieces[0].shape
    per_piece = piece // TILE
    slots = tiles_ref.shape[0]
    build_table(pieces, spread_ref[...], table)
    for acc in (acc_a, acc_b):
        acc[...] = jnp.zeros_like(acc)
    lane = lax.broadcasted_iota(jnp.int32, (2 * width, LANES), 1)
    masks = [(lane // HALF == s).astype(BF16) for s in range(GROUP)]
    low = lax.broadcasted_iota(jnp.int32, (width, LANES), 1) < TILE
    count = count_ref[0, 0]
    row_flip = lax.axis_index("bcol") * per_piece
    col_flip = lax.axis_index("brow") * per_piece
    spare = n_out * per_piece

    for g in range(slots // GROUP):
        at = [table[rows_ref[g * GROUP + s] ^ row_flip] * masks[s] for s in range(GROUP)]
        block = tiles_ref[g * GROUP : (g + 1) * GROUP].reshape(LANES, LANES)
        out = jnp.dot(jnp.concatenate(at, axis=0), block, preferred_element_type=F32)
        for s in range(GROUP):
            t = g * GROUP + s
            part = out[2 * width * s : 2 * width * (s + 1)]
            part = jnp.where(low, part[:width], part[width:])
            c = jnp.where(t < count, cols_ref[t] ^ col_flip, spare)
            acc = acc_a if s % 2 == 0 else acc_b
            acc[c] += part

    for n in range(n_out):
        h = n // 2
        dest = keep_ref.at[h] if n % 2 == 0 else give_refs[h // per_give].at[h % per_give]
        for p in range(per_piece // 2):
            at = n * per_piece + 2 * p
            a = acc_a[at] + acc_b[at]
            b = acc_a[at + 1] + acc_b[at + 1]
            dest[:, p * LANES : (p + 1) * LANES] = jnp.where(low, a, b) + pltpu.roll(
                jnp.where(low, b, a), TILE, 1
            )


def backward(segment, tiles, tile_rows, tile_cols, counts, n_out, after):
    n_in, width, piece = segment.shape
    per_piece = piece // TILE
    half = jax.ShapeDtypeStruct((n_out // 2, width, piece), F32)
    quarter = jax.ShapeDtypeStruct((n_out // 4, width, piece), F32)
    return pl.pallas_call(
        backward_kernel,
        in_specs=[SMEM] * 3 + [VMEM] * 3 + [ANY],
        out_specs=[VMEM] * 3,
        out_shape=[half, quarter, quarter],
        scratch_shapes=[
            pltpu.VMEM((n_in * per_piece, 2 * width, LANES), BF16),
            pltpu.VMEM((n_out * per_piece + 1, width, LANES), F32),
            pltpu.VMEM((n_out * per_piece + 1, width, LANES), F32),
        ],
        compiler_params=PARAMS,
        cost_estimate=pl.CostEstimate(
            flops=2 * tiles.size * 64, bytes_accessed=4 * tiles.size, transcendentals=0
        ),
        name="transpose_product",
    )(tile_rows, tile_cols, counts, row_spread(), tiles, segment, after)


def double_table(pieces, table):
    width, piece = pieces[0].shape
    low = lax.broadcasted_iota(jnp.int32, (width, LANES), 1) < TILE
    for n, ref in enumerate(pieces):
        for p in range(piece // LANES):
            pair = ref[:, p * LANES : (p + 1) * LANES].astype(F32)
            turned = pltpu.roll(pair, TILE, 1)
            at = (n * piece + p * LANES) // TILE
            table[at] = jnp.where(low, pair, turned)
            table[at + 1] = jnp.where(low, turned, pair)


def forward_kernel(
    rows_ref,
    cols_ref,
    count_ref,
    fold_ref,
    tiles_ref,
    same_ref,
    other_ref,
    after_ref,
    keep_ref,
    give_ref,
    table,
    acc_a,
    acc_b,
):
    pieces = [ref.at[h] for h in range(same_ref.shape[0]) for ref in (same_ref, other_ref)]
    n_out = 2 * keep_ref.shape[0]
    width, piece = pieces[0].shape
    per_piece = piece // TILE
    slots = tiles_ref.shape[0]
    double_table(pieces, table)
    for acc in (acc_a, acc_b):
        acc[...] = jnp.zeros_like(acc)
    lane = lax.broadcasted_iota(jnp.int32, (width, LANES), 1)
    masks = [lane // HALF == s for s in range(GROUP)]
    wide_lane = lax.broadcasted_iota(jnp.int32, (LANES, LANES), 1)
    parity = [(wide_lane // TILE == e).astype(BF16) for e in range(2)]
    count = count_ref[0, 0]
    row_flip = lax.axis_index("bcol") * per_piece
    col_flip = lax.axis_index("brow") * per_piece
    spare = n_out * per_piece

    for g in range(slots // GROUP):
        at = [table[cols_ref[g * GROUP + s] ^ col_flip] for s in range(GROUP)]
        block = tiles_ref[g * GROUP : (g + 1) * GROUP].reshape(LANES, LANES)
        turned = jnp.concatenate([block[LANES // 2 :], block[: LANES // 2]], axis=0)
        out = lax.dot_general(
            jnp.concatenate(at, axis=0).astype(BF16),
            jnp.concatenate([block * parity[0], turned * parity[1]], axis=0),
            (((1,), (1,)), ((), ())),
            preferred_element_type=F32,
        )
        for s in range(GROUP):
            t = g * GROUP + s
            part = out[width * s : width * (s + 1)]
            r = jnp.where(t < count, rows_ref[t] ^ row_flip, spare)
            part = jnp.where(
                masks[s], part[:, :LANES], jnp.where(masks[(s + 2) % GROUP], part[:, LANES:], 0.0)
            )
            acc = acc_a if s < 2 else acc_b
            acc[r] += part

    fold = fold_ref[...]
    pairs = per_piece // 2
    for n in range(n_out):
        blocks = []
        for q in range(2):
            for acc in (acc_a, acc_b):
                both = acc[n * per_piece : (n + 1) * per_piece].reshape(pairs, 2 * width, LANES)
                blocks.append(both[:, q * width : (q + 1) * width, :].reshape(pairs * width, LANES))
        wide = jnp.concatenate(blocks, axis=1)
        first = wide.astype(BF16)
        rest = (wide - first.astype(F32)).astype(BF16)
        out = jnp.dot(first, fold, preferred_element_type=F32)
        out = out + jnp.dot(rest, fold, preferred_element_type=F32)
        parts = [out[p * width : (p + 1) * width] for p in range(pairs)]
        if n % 2 == 0:
            for p in range(pairs):
                keep_ref[n // 2, :, p * LANES : (p + 1) * LANES] = parts[p]
        else:
            encode(parts, give_ref.at[n // 2])


def forward(same, other, tiles, tile_rows, tile_cols, counts, n_out, after):
    n_chips, width, piece = same.shape
    per_piece = piece // TILE
    half = jax.ShapeDtypeStruct((n_out // 2, width, piece), F32)
    coded = jax.ShapeDtypeStruct((n_out // 2, width, piece + LANES), jnp.int16)
    return pl.pallas_call(
        forward_kernel,
        in_specs=[SMEM] * 3 + [VMEM] * 4 + [ANY],
        out_specs=[VMEM] * 2,
        out_shape=[half, coded],
        scratch_shapes=[
            pltpu.VMEM((2 * n_chips * per_piece, width, LANES), F32),
            pltpu.VMEM((n_out * per_piece + 1, width, LANES), F32),
            pltpu.VMEM((n_out * per_piece + 1, width, LANES), F32),
        ],
        compiler_params=PARAMS,
        cost_estimate=pl.CostEstimate(
            flops=2 * tiles.size * 64, bytes_accessed=4 * tiles.size, transcendentals=0
        ),
        name="forward_product",
    )(tile_rows, tile_cols, counts, row_fold(), tiles, same, other, after)


def stack_kernel(n_after, *refs):
    out_ref, at = refs[-1], 0
    for ref in refs[: -1 - n_after]:
        if len(ref.shape) == 2:
            out_ref[at] = ref[...]
            at += 1
        else:
            out_ref[at : at + ref.shape[0]] = ref[...]
            at += ref.shape[0]


def stack(*parts, after=()):
    total = sum(x.shape[0] if x.ndim == 3 else 1 for x in parts)
    return pl.pallas_call(
        functools.partial(stack_kernel, len(after)),
        in_specs=[VMEM] * len(parts) + [ANY] * len(after),
        out_specs=VMEM,
        out_shape=jax.ShapeDtypeStruct((total,) + parts[0].shape[-2:], parts[0].dtype),
        compiler_params=PARAMS,
        name="stack_pieces",
    )(*parts, *after)


def pair_sum_kernel(keep_ref, *refs):
    n_chips = keep_ref.shape[0]
    gots, outs = refs[: 1 - n_chips], refs[1 - n_chips :]
    got = [ref.at[h] for ref in gots for h in range(ref.shape[0])]
    for h, out in enumerate(outs):
        out[...] = keep_ref[h + 1] + got[h + 1][...]


def pair_sum(keep, gots):
    parts, width, piece = keep.shape
    return pl.pallas_call(
        pair_sum_kernel,
        in_specs=[VMEM] * (1 + len(gots)),
        out_specs=[VMEM] * (parts - 1),
        out_shape=[jax.ShapeDtypeStruct((width, piece), F32)] * (parts - 1),
        compiler_params=PARAMS,
        name="core_pair_sum",
    )(keep, *gots)


def split_sum_kernel(keep_ref, got_ref, after_ref, next_keep, next_give):
    for h in range(next_keep.shape[0]):
        for n, got in enumerate(decode(got_ref.at[2 * h])):
            at = pl.ds(n * LANES, LANES)
            next_keep[h, :, at] = keep_ref[2 * h, :, at] + got
        sums = [
            keep_ref[2 * h + 1, :, n * LANES : (n + 1) * LANES] + got
            for n, got in enumerate(decode(got_ref.at[2 * h + 1]))
        ]
        encode(sums, next_give.at[h])


def split_sum(keep, got, after):
    parts, width, piece = keep.shape
    return pl.pallas_call(
        split_sum_kernel,
        in_specs=[VMEM] * 2 + [ANY],
        out_specs=[VMEM] * 2,
        out_shape=[
            jax.ShapeDtypeStruct((parts // 2, width, piece), F32),
            jax.ShapeDtypeStruct((parts // 2,) + got.shape[1:], got.dtype),
        ],
        compiler_params=PARAMS,
        name="halving_sum",
    )(keep, got, after)


def last_sum_kernel(*refs):
    chips, (brow_keep, brow_got, keep_ref, got_ref, out_ref) = refs[:-5], refs[-5:]
    for n, got in enumerate(decode(got_ref.at[0])):
        at = pl.ds(n * LANES, LANES)
        total = brow_keep[0, :, at] + brow_got[0, :, at]
        for ref in chips:
            total = total + ref[:, at]
        out_ref[:, at] = total + (keep_ref[0, :, at] + got)


def last_sum(keep, got, brow_keep, brow_got, chips):
    return pl.pallas_call(
        last_sum_kernel,
        in_specs=[VMEM] * (4 + len(chips)),
        out_specs=VMEM,
        out_shape=jax.ShapeDtypeStruct(keep.shape[1:], F32),
        compiler_params=PARAMS,
        name="last_sum",
    )(*chips, brow_keep, brow_got, keep, got)


def swap(x, axis, size, d):
    return lax.ppermute(x, axis, [(i, i ^ d) for i in range(size)])


def body(vectors, tiles, tile_rows, tile_cols, counts):
    n_rows = lax.axis_size("brow")
    n_cols = lax.axis_size("bcol")
    own = stack(vectors)
    chips = [swap(vectors, "brow", n_rows, 2 * h) for h in range(1, n_rows // 2)]
    segment, d = own, 1
    while d < n_cols:
        segment = stack(segment, swap(segment if d > 1 else vectors[None], "bcol", n_cols, d), after=tuple(chips[:1]))
        d *= 2
    blocks = prep(tiles)
    same = stack(own, *chips, after=(blocks, segment))
    other = swap(same, "brow", n_rows, 1)

    col_keep, *col_give = backward(segment, blocks, tile_rows, tile_cols, counts, n_rows, same)
    row_keep, give = forward(same, other, blocks, tile_rows, tile_cols, counts, n_cols, col_give[0])
    col_got = [swap(x, "brow", n_rows, 1) for x in col_give]
    sums = pair_sum(col_keep, col_got)
    from_chips = [swap(x, "brow", n_rows, 2 * (h + 1)) for h, x in enumerate(sums)]
    row_got, d = swap(give, "bcol", n_cols, 1), 2
    while d < n_cols:
        row_keep, give = split_sum(row_keep, row_got, sums[0])
        row_got = swap(give, "bcol", n_cols, d)
        d *= 2
    return last_sum(row_keep, row_got, col_keep, col_got[0], from_chips)


def solution(mesh):
    return jax.shard_map(
        body,
        mesh=mesh,
        in_specs=(
            P(None, ("brow", "bcol")),
            P(("brow", "bcol"), None),
            P(("brow", "bcol")),
            P(("brow", "bcol")),
            P("brow", "bcol"),
        ),
        out_specs=P(None, ("brow", "bcol")),
        check_vma=False,
    )
```

```python
import functools

import jax
import jax.numpy as jnp
import numpy as np
from jax import lax
from jax.experimental import pallas as pl
from jax.experimental.pallas import tpu as pltpu
from jax.sharding import PartitionSpec as P

TILE = 64
LANES = 128
HALF = TILE // 2
GROUP = LANES // HALF
STEPS = 32000.0
F32 = jnp.float32
BF16 = jnp.bfloat16
VMEM = pl.BlockSpec(memory_space=pltpu.VMEM)
ANY = pl.BlockSpec(memory_space=pl.ANY)
SMEM = pl.BlockSpec(memory_space=pltpu.SMEM)
PARAMS = pltpu.CompilerParams(vmem_limit_bytes=48 * 1024 * 1024)


def row_spread():
    out = np.zeros((LANES, 2, 2, GROUP, HALF), np.float32)
    for q in range(2):
        for e in range(2):
            for m in range(HALF):
                out[q * TILE + 2 * m + e, q, e, :, m] = 1
    return jnp.asarray(out.reshape(LANES, 4 * LANES), BF16)


def row_fold():
    out = np.zeros((2, 2, 2, GROUP // 2, HALF, LANES), np.float32)
    for q in range(2):
        for e in range(2):
            for m in range(HALF):
                out[q, 0, e, :, m, q * TILE + 2 * m + e] = 1
                out[q, 1, 1 - e, :, m, q * TILE + 2 * m + e] = 1
    return jnp.asarray(out.reshape(4 * LANES, LANES), BF16)


def encode(values, out_ref):
    width, piece = values[0].shape[0], LANES * len(values)
    lane = lax.broadcasted_iota(jnp.int32, (width, LANES), 1)
    exponents = jnp.zeros((width, LANES), F32)
    for n, value in enumerate(values):
        top = jnp.max(jnp.abs(value), axis=1, keepdims=True)
        e = jnp.clip(jnp.ceil(jnp.log2(top)), -100.0, 100.0)
        exponents = jnp.where(lane == n, e, exponents)
        scaled = jnp.floor(value * (STEPS * jnp.exp2(-e)) + 0.5)
        out_ref[:, n * LANES : (n + 1) * LANES] = scaled.astype(jnp.int32).astype(jnp.int16)
    out_ref[:, piece:] = exponents.astype(jnp.int32).astype(jnp.int16)


def decode(ref):
    chunks = ref.shape[1] // LANES - 1
    exponents = ref[:, chunks * LANES :].astype(jnp.int32).astype(F32)
    scales = jnp.exp2(exponents) * (1.0 / STEPS)
    return [
        ref[:, n * LANES : (n + 1) * LANES].astype(jnp.int32).astype(F32) * scales[:, n : n + 1]
        for n in range(chunks)
    ]


def prep_kernel(tiles_ref, out_ref, wide):
    for b in range(tiles_ref.shape[0]):
        wide[b] = tiles_ref[b].astype(F32).reshape(HALF * 8, LANES)
        for s in range(8):
            out_ref[8 * b + s] = wide[b, pl.ds(s, HALF, stride=8), :].astype(BF16)


def prep(tiles):
    slots = tiles.shape[0]
    blocks = slots // 8
    view = tiles.reshape(blocks, 8, HALF, LANES).swapaxes(1, 2)
    return pl.pallas_call(
        prep_kernel,
        in_specs=[VMEM],
        out_specs=VMEM,
        out_shape=jax.ShapeDtypeStruct((slots, HALF, LANES), BF16),
        scratch_shapes=[pltpu.VMEM((blocks, HALF * 8, LANES), F32)],
        compiler_params=PARAMS,
        cost_estimate=pl.CostEstimate(flops=0, bytes_accessed=4 * tiles.size, transcendentals=0),
        name="prep_tiles",
    )(view)


def doubled(size):
    order, d = [0], size // 2
    while d > 0:
        order += [x ^ d for x in order]
        d //= 2
    return order


def build_table(pieces, spread, table):
    width, piece = pieces[0].shape
    pairs = piece // LANES
    for n, ref in enumerate(pieces):
        rows = jnp.concatenate([ref[:, p * LANES : (p + 1) * LANES] for p in range(pairs)], axis=0)
        wide = jnp.dot(rows, spread, preferred_element_type=F32)
        wide = wide.reshape(pairs, width, 4 * LANES)
        for q in range(2):
            both = jnp.concatenate(
                [wide[:, :, (2 * q + e) * LANES : (2 * q + e + 1) * LANES] for e in range(2)], axis=1
            ).astype(BF16)
            for p in range(pairs):
                table[n * 2 * pairs + 2 * p + q] = both[p]


def backward_kernel(
    rows_ref, cols_ref, count_ref, spread_ref, tiles_ref, seg_ref, after_ref, keep_ref, *refs
):
    pieces = [seg_ref.at[at] for at in np.argsort(doubled(seg_ref.shape[0]))]
    *give_refs, table, acc_a, acc_b = refs
    per_give = give_refs[0].shape[0]
    n_out = 2 * keep_ref.shape[0]
    width, piece = pieces[0].shape
    per_piece = piece // TILE
    slots = tiles_ref.shape[0]
    build_table(pieces, spread_ref[...], table)
    for acc in (acc_a, acc_b):
        acc[...] = jnp.zeros_like(acc)
    lane = lax.broadcasted_iota(jnp.int32, (2 * width, LANES), 1)
    masks = [(lane // HALF == s).astype(BF16) for s in range(GROUP)]
    low = lax.broadcasted_iota(jnp.int32, (width, LANES), 1) < TILE
    count = count_ref[0, 0]
    row_flip = lax.axis_index("bcol") * per_piece
    col_flip = lax.axis_index("brow") * per_piece
    spare = n_out * per_piece

    for g in range(slots // GROUP):
        at = [table[rows_ref[g * GROUP + s] ^ row_flip] * masks[s] for s in range(GROUP)]
        block = tiles_ref[g * GROUP : (g + 1) * GROUP].reshape(LANES, LANES)
        out = jnp.dot(jnp.concatenate(at, axis=0), block, preferred_element_type=F32)
        for s in range(GROUP):
            t = g * GROUP + s
            part = out[2 * width * s : 2 * width * (s + 1)]
            part = jnp.where(low, part[:width], part[width:])
            c = jnp.where(t < count, cols_ref[t] ^ col_flip, spare)
            acc = acc_a if s % 2 == 0 else acc_b
            acc[c] += part

    for n in range(n_out):
        h = n // 2
        dest = keep_ref.at[h] if n % 2 == 0 else give_refs[h // per_give].at[h % per_give]
        for p in range(per_piece // 2):
            at = n * per_piece + 2 * p
            a = acc_a[at] + acc_b[at]
            b = acc_a[at + 1] + acc_b[at + 1]
            dest[:, p * LANES : (p + 1) * LANES] = jnp.where(low, a, b) + pltpu.roll(
                jnp.where(low, b, a), TILE, 1
            )


def backward(segment, tiles, tile_rows, tile_cols, counts, n_out, after):
    n_in, width, piece = segment.shape
    per_piece = piece // TILE
    half = jax.ShapeDtypeStruct((n_out // 2, width, piece), F32)
    quarter = jax.ShapeDtypeStruct((n_out // 4, width, piece), F32)
    return pl.pallas_call(
        backward_kernel,
        in_specs=[SMEM] * 3 + [VMEM] * 3 + [ANY],
        out_specs=[VMEM] * 3,
        out_shape=[half, quarter, quarter],
        scratch_shapes=[
            pltpu.VMEM((n_in * per_piece, 2 * width, LANES), BF16),
            pltpu.VMEM((n_out * per_piece + 1, width, LANES), F32),
            pltpu.VMEM((n_out * per_piece + 1, width, LANES), F32),
        ],
        compiler_params=PARAMS,
        cost_estimate=pl.CostEstimate(
            flops=2 * tiles.size * 64, bytes_accessed=4 * tiles.size, transcendentals=0
        ),
        name="transpose_product",
    )(tile_rows, tile_cols, counts, row_spread(), tiles, segment, after)


def double_table(pieces, table):
    width, piece = pieces[0].shape
    low = lax.broadcasted_iota(jnp.int32, (width, LANES), 1) < TILE
    for n, ref in enumerate(pieces):
        for p in range(piece // LANES):
            pair = ref[:, p * LANES : (p + 1) * LANES].astype(F32)
            turned = pltpu.roll(pair, TILE, 1)
            at = (n * piece + p * LANES) // TILE
            table[at] = jnp.where(low, pair, turned)
            table[at + 1] = jnp.where(low, turned, pair)


def forward_kernel(
    rows_ref,
    cols_ref,
    count_ref,
    fold_ref,
    tiles_ref,
    same_ref,
    other_ref,
    after_ref,
    keep_ref,
    give_ref,
    table,
    acc_a,
    acc_b,
):
    pieces = [ref.at[h] for h in range(same_ref.shape[0]) for ref in (same_ref, other_ref)]
    n_out = 2 * keep_ref.shape[0]
    width, piece = pieces[0].shape
    per_piece = piece // TILE
    slots = tiles_ref.shape[0]
    double_table(pieces, table)
    for acc in (acc_a, acc_b):
        acc[...] = jnp.zeros_like(acc)
    lane = lax.broadcasted_iota(jnp.int32, (width, LANES), 1)
    masks = [lane // HALF == s for s in range(GROUP)]
    wide_lane = lax.broadcasted_iota(jnp.int32, (LANES, LANES), 1)
    parity = [(wide_lane // TILE == e).astype(BF16) for e in range(2)]
    count = count_ref[0, 0]
    row_flip = lax.axis_index("bcol") * per_piece
    col_flip = lax.axis_index("brow") * per_piece
    spare = n_out * per_piece

    for g in range(slots // GROUP):
        at = [table[cols_ref[g * GROUP + s] ^ col_flip] for s in range(GROUP)]
        block = tiles_ref[g * GROUP : (g + 1) * GROUP].reshape(LANES, LANES)
        turned = jnp.concatenate([block[LANES // 2 :], block[: LANES // 2]], axis=0)
        out = lax.dot_general(
            jnp.concatenate(at, axis=0).astype(BF16),
            jnp.concatenate([block * parity[0], turned * parity[1]], axis=0),
            (((1,), (1,)), ((), ())),
            preferred_element_type=F32,
        )
        for s in range(GROUP):
            t = g * GROUP + s
            part = out[width * s : width * (s + 1)]
            r = jnp.where(t < count, rows_ref[t] ^ row_flip, spare)
            part = jnp.where(
                masks[s], part[:, :LANES], jnp.where(masks[(s + 2) % GROUP], part[:, LANES:], 0.0)
            )
            acc = acc_a if s < 2 else acc_b
            acc[r] += part

    fold = fold_ref[...]
    pairs = per_piece // 2
    for n in range(n_out):
        blocks = []
        for q in range(2):
            for acc in (acc_a, acc_b):
                both = acc[n * per_piece : (n + 1) * per_piece].reshape(pairs, 2 * width, LANES)
                blocks.append(both[:, q * width : (q + 1) * width, :].reshape(pairs * width, LANES))
        wide = jnp.concatenate(blocks, axis=1)
        first = wide.astype(BF16)
        rest = (wide - first.astype(F32)).astype(BF16)
        out = jnp.dot(first, fold, preferred_element_type=F32)
        out = out + jnp.dot(rest, fold, preferred_element_type=F32)
        parts = [out[p * width : (p + 1) * width] for p in range(pairs)]
        if n < n_out // 2:
            for p in range(pairs):
                keep_ref[n, :, p * LANES : (p + 1) * LANES] = parts[p]
        else:
            encode(parts, give_ref.at[n - n_out // 2])


def forward(same, other, tiles, tile_rows, tile_cols, counts, n_out, after):
    n_chips, width, piece = same.shape
    per_piece = piece // TILE
    half = jax.ShapeDtypeStruct((n_out // 2, width, piece), F32)
    coded = jax.ShapeDtypeStruct((n_out // 2, width, piece + LANES), jnp.int16)
    return pl.pallas_call(
        forward_kernel,
        in_specs=[SMEM] * 3 + [VMEM] * 4 + [ANY],
        out_specs=[VMEM] * 2,
        out_shape=[half, coded],
        scratch_shapes=[
            pltpu.VMEM((2 * n_chips * per_piece, width, LANES), F32),
            pltpu.VMEM((n_out * per_piece + 1, width, LANES), F32),
            pltpu.VMEM((n_out * per_piece + 1, width, LANES), F32),
        ],
        compiler_params=PARAMS,
        cost_estimate=pl.CostEstimate(
            flops=2 * tiles.size * 64, bytes_accessed=4 * tiles.size, transcendentals=0
        ),
        name="forward_product",
    )(tile_rows, tile_cols, counts, row_fold(), tiles, same, other, after)


def stack_kernel(n_after, *refs):
    out_ref, at = refs[-1], 0
    for ref in refs[: -1 - n_after]:
        if len(ref.shape) == 2:
            out_ref[at] = ref[...]
            at += 1
        else:
            out_ref[at : at + ref.shape[0]] = ref[...]
            at += ref.shape[0]


def stack(*parts, after=()):
    total = sum(x.shape[0] if x.ndim == 3 else 1 for x in parts)
    return pl.pallas_call(
        functools.partial(stack_kernel, len(after)),
        in_specs=[VMEM] * len(parts) + [ANY] * len(after),
        out_specs=VMEM,
        out_shape=jax.ShapeDtypeStruct((total,) + parts[0].shape[-2:], parts[0].dtype),
        compiler_params=PARAMS,
        name="stack_pieces",
    )(*parts, *after)


def pair_sum_kernel(keep_ref, *refs):
    n_chips = keep_ref.shape[0]
    gots, outs = refs[: 1 - n_chips], refs[1 - n_chips :]
    got = [ref.at[h] for ref in gots for h in range(ref.shape[0])]
    for h, out in enumerate(outs):
        out[...] = keep_ref[h + 1] + got[h + 1][...]


def pair_sum(keep, gots):
    parts, width, piece = keep.shape
    return pl.pallas_call(
        pair_sum_kernel,
        in_specs=[VMEM] * (1 + len(gots)),
        out_specs=[VMEM] * (parts - 1),
        out_shape=[jax.ShapeDtypeStruct((width, piece), F32)] * (parts - 1),
        compiler_params=PARAMS,
        name="core_pair_sum",
    )(keep, *gots)


def split_sum_kernel(keep_ref, got_ref, after_ref, next_keep, next_give):
    half = next_keep.shape[0]
    for h in range(half):
        for n, got in enumerate(decode(got_ref.at[h])):
            at = pl.ds(n * LANES, LANES)
            next_keep[h, :, at] = keep_ref[h, :, at] + got
        sums = [
            keep_ref[half + h, :, n * LANES : (n + 1) * LANES] + got
            for n, got in enumerate(decode(got_ref.at[half + h]))
        ]
        encode(sums, next_give.at[h])


def split_sum(keep, got, after):
    parts, width, piece = keep.shape
    return pl.pallas_call(
        split_sum_kernel,
        in_specs=[VMEM] * 2 + [ANY],
        out_specs=[VMEM] * 2,
        out_shape=[
            jax.ShapeDtypeStruct((parts // 2, width, piece), F32),
            jax.ShapeDtypeStruct((parts // 2,) + got.shape[1:], got.dtype),
        ],
        compiler_params=PARAMS,
        name="halving_sum",
    )(keep, got, after)


def last_sum_kernel(*refs):
    chips, (brow_keep, brow_got, keep_ref, got_ref, out_ref) = refs[:-5], refs[-5:]
    for n, got in enumerate(decode(got_ref.at[0])):
        at = pl.ds(n * LANES, LANES)
        total = brow_keep[0, :, at] + brow_got[0, :, at]
        for ref in chips:
            total = total + ref[:, at]
        out_ref[:, at] = total + (keep_ref[0, :, at] + got)


def last_sum(keep, got, brow_keep, brow_got, chips):
    return pl.pallas_call(
        last_sum_kernel,
        in_specs=[VMEM] * (4 + len(chips)),
        out_specs=VMEM,
        out_shape=jax.ShapeDtypeStruct(keep.shape[1:], F32),
        compiler_params=PARAMS,
        name="last_sum",
    )(*chips, brow_keep, brow_got, keep, got)


def swap(x, axis, size, d):
    return lax.ppermute(x, axis, [(i, i ^ d) for i in range(size)])


def body(vectors, tiles, tile_rows, tile_cols, counts):
    n_rows = lax.axis_size("brow")
    n_cols = lax.axis_size("bcol")
    own = stack(vectors)
    chips = [swap(vectors, "brow", n_rows, 2 * h) for h in range(1, n_rows // 2)]
    segment, d = own, n_cols // 2
    while d > 0:
        first = d == n_cols // 2
        segment = stack(segment, swap(vectors[None] if first else segment, "bcol", n_cols, d))
        d //= 2
    blocks = prep(tiles)
    same = stack(own, *chips, after=(blocks,))
    other = swap(same, "brow", n_rows, 1)

    col_keep, *col_give = backward(segment, blocks, tile_rows, tile_cols, counts, n_rows, same)
    row_keep, give = forward(same, other, blocks, tile_rows, tile_cols, counts, n_cols, col_give[0])
    col_got = [swap(x, "brow", n_rows, 1) for x in col_give]
    sums = pair_sum(col_keep, col_got)
    from_chips = [swap(x, "brow", n_rows, 2 * (h + 1)) for h, x in enumerate(sums)]
    row_got, d = swap(give, "bcol", n_cols, n_cols // 2), n_cols // 4
    while d > 0:
        row_keep, give = split_sum(row_keep, row_got, sums[0])
        row_got = swap(give, "bcol", n_cols, d)
        d //= 2
    return last_sum(row_keep, row_got, col_keep, col_got[0], from_chips)


def solution(mesh):
    return jax.shard_map(
        body,
        mesh=mesh,
        in_specs=(
            P(None, ("brow", "bcol")),
            P(("brow", "bcol"), None),
            P(("brow", "bcol")),
            P(("brow", "bcol")),
            P("brow", "bcol"),
        ),
        out_specs=P(None, ("brow", "bcol")),
        check_vma=False,
    )
```

```python
import functools

import jax
import jax.numpy as jnp
import numpy as np
from jax import lax
from jax.experimental import pallas as pl
from jax.experimental.pallas import tpu as pltpu
from jax.sharding import PartitionSpec as P

TILE = 64
LANES = 128
HALF = TILE // 2
GROUP = LANES // HALF
STEPS = 32000.0
F32 = jnp.float32
BF16 = jnp.bfloat16
VMEM = pl.BlockSpec(memory_space=pltpu.VMEM)
ANY = pl.BlockSpec(memory_space=pl.ANY)
SMEM = pl.BlockSpec(memory_space=pltpu.SMEM)
PARAMS = pltpu.CompilerParams(vmem_limit_bytes=48 * 1024 * 1024)


def row_spread():
    out = np.zeros((LANES, 2, 2, GROUP, HALF), np.float32)
    for q in range(2):
        for e in range(2):
            for m in range(HALF):
                out[q * TILE + 2 * m + e, q, e, :, m] = 1
    return jnp.asarray(out.reshape(LANES, 4 * LANES), BF16)


def row_fold():
    out = np.zeros((2, 2, 2, GROUP // 2, HALF, LANES), np.float32)
    for q in range(2):
        for e in range(2):
            for m in range(HALF):
                out[q, 0, e, :, m, q * TILE + 2 * m + e] = 1
                out[q, 1, 1 - e, :, m, q * TILE + 2 * m + e] = 1
    return jnp.asarray(out.reshape(4 * LANES, LANES), BF16)


def encode(values, out_ref):
    width, piece = values[0].shape[0], LANES * len(values)
    lane = lax.broadcasted_iota(jnp.int32, (width, LANES), 1)
    exponents = jnp.zeros((width, LANES), F32)
    for n, value in enumerate(values):
        top = jnp.max(jnp.abs(value), axis=1, keepdims=True)
        e = jnp.clip(jnp.ceil(jnp.log2(top)), -100.0, 100.0)
        exponents = jnp.where(lane == n, e, exponents)
        scaled = jnp.floor(value * (STEPS * jnp.exp2(-e)) + 0.5)
        out_ref[:, n * LANES : (n + 1) * LANES] = scaled.astype(jnp.int32).astype(jnp.int16)
    out_ref[:, piece:] = exponents.astype(jnp.int32).astype(jnp.int16)


def decode(ref):
    chunks = ref.shape[1] // LANES - 1
    exponents = ref[:, chunks * LANES :].astype(jnp.int32).astype(F32)
    scales = jnp.exp2(exponents) * (1.0 / STEPS)
    return [
        ref[:, n * LANES : (n + 1) * LANES].astype(jnp.int32).astype(F32) * scales[:, n : n + 1]
        for n in range(chunks)
    ]


def prep_kernel(tiles_ref, out_ref, wide):
    for b in range(tiles_ref.shape[0]):
        wide[b] = tiles_ref[b].astype(F32).reshape(HALF * 8, LANES)
        for s in range(8):
            out_ref[8 * b + s] = wide[b, pl.ds(s, HALF, stride=8), :].astype(BF16)


def prep(tiles):
    slots = tiles.shape[0]
    blocks = slots // 8
    view = tiles.reshape(blocks, 8, HALF, LANES).swapaxes(1, 2)
    return pl.pallas_call(
        prep_kernel,
        in_specs=[VMEM],
        out_specs=VMEM,
        out_shape=jax.ShapeDtypeStruct((slots, HALF, LANES), BF16),
        scratch_shapes=[pltpu.VMEM((blocks, HALF * 8, LANES), F32)],
        compiler_params=PARAMS,
        cost_estimate=pl.CostEstimate(flops=0, bytes_accessed=4 * tiles.size, transcendentals=0),
        name="prep_tiles",
    )(view)


def doubled(size):
    order, d = [0], size // 2
    while d > 0:
        order += [x ^ d for x in order]
        d //= 2
    return order


def build_table(pieces, spread, table):
    width, piece = pieces[0].shape
    pairs = piece // LANES
    for n, ref in enumerate(pieces):
        rows = jnp.concatenate([ref[:, p * LANES : (p + 1) * LANES] for p in range(pairs)], axis=0)
        wide = jnp.dot(rows, spread, preferred_element_type=F32)
        wide = wide.reshape(pairs, width, 4 * LANES)
        for q in range(2):
            both = jnp.concatenate(
                [wide[:, :, (2 * q + e) * LANES : (2 * q + e + 1) * LANES] for e in range(2)], axis=1
            ).astype(BF16)
            for p in range(pairs):
                table[n * 2 * pairs + 2 * p + q] = both[p]


def backward_kernel(
    rows_ref, cols_ref, count_ref, spread_ref, tiles_ref, seg_ref, after_ref, keep_ref, *refs
):
    pieces = [seg_ref.at[at] for at in np.argsort(doubled(seg_ref.shape[0]))]
    *give_refs, table, acc_a, acc_b = refs
    per_give = give_refs[0].shape[0]
    n_out = 2 * keep_ref.shape[0]
    width, piece = pieces[0].shape
    per_piece = piece // TILE
    slots = tiles_ref.shape[0]
    build_table(pieces, spread_ref[...], table)
    for acc in (acc_a, acc_b):
        acc[...] = jnp.zeros_like(acc)
    lane = lax.broadcasted_iota(jnp.int32, (2 * width, LANES), 1)
    masks = [(lane // HALF == s).astype(BF16) for s in range(GROUP)]
    low = lax.broadcasted_iota(jnp.int32, (width, LANES), 1) < TILE
    count = count_ref[0, 0]
    row_flip = lax.axis_index("bcol") * per_piece
    col_flip = lax.axis_index("brow") * per_piece
    spare = n_out * per_piece

    for g in range(slots // GROUP):
        at = [table[rows_ref[g * GROUP + s] ^ row_flip] * masks[s] for s in range(GROUP)]
        block = tiles_ref[g * GROUP : (g + 1) * GROUP].reshape(LANES, LANES)
        out = jnp.dot(jnp.concatenate(at, axis=0), block, preferred_element_type=F32)
        for s in range(GROUP):
            t = g * GROUP + s
            part = out[2 * width * s : 2 * width * (s + 1)]
            part = jnp.where(low, part[:width], part[width:])
            c = jnp.where(t < count, cols_ref[t] ^ col_flip, spare)
            acc = acc_a if s % 2 == 0 else acc_b
            acc[c] += part

    for n in range(n_out):
        h = n // 2
        dest = keep_ref.at[h] if n % 2 == 0 else give_refs[h // per_give].at[h % per_give]
        for p in range(per_piece // 2):
            at = n * per_piece + 2 * p
            a = acc_a[at] + acc_b[at]
            b = acc_a[at + 1] + acc_b[at + 1]
            dest[:, p * LANES : (p + 1) * LANES] = jnp.where(low, a, b) + pltpu.roll(
                jnp.where(low, b, a), TILE, 1
            )


def backward(segment, tiles, tile_rows, tile_cols, counts, n_out, after):
    n_in, width, piece = segment.shape
    per_piece = piece // TILE
    half = jax.ShapeDtypeStruct((n_out // 2, width, piece), F32)
    quarter = jax.ShapeDtypeStruct((n_out // 4, width, piece), F32)
    return pl.pallas_call(
        backward_kernel,
        in_specs=[SMEM] * 3 + [VMEM] * 3 + [ANY],
        out_specs=[VMEM] * 3,
        out_shape=[half, quarter, quarter],
        scratch_shapes=[
            pltpu.VMEM((n_in * per_piece, 2 * width, LANES), BF16),
            pltpu.VMEM((n_out * per_piece + 1, width, LANES), F32),
            pltpu.VMEM((n_out * per_piece + 1, width, LANES), F32),
        ],
        compiler_params=PARAMS,
        cost_estimate=pl.CostEstimate(
            flops=2 * tiles.size * 64, bytes_accessed=4 * tiles.size, transcendentals=0
        ),
        name="transpose_product",
    )(tile_rows, tile_cols, counts, row_spread(), tiles, segment, after)


def double_table(pieces, table):
    width, piece = pieces[0].shape
    low = lax.broadcasted_iota(jnp.int32, (width, LANES), 1) < TILE
    for n, ref in enumerate(pieces):
        for p in range(piece // LANES):
            pair = ref[:, p * LANES : (p + 1) * LANES].astype(F32)
            turned = pltpu.roll(pair, TILE, 1)
            at = (n * piece + p * LANES) // TILE
            table[at] = jnp.where(low, pair, turned)
            table[at + 1] = jnp.where(low, turned, pair)


def forward_kernel(
    rows_ref,
    cols_ref,
    count_ref,
    fold_ref,
    tiles_ref,
    same_ref,
    other_ref,
    after_ref,
    keep_ref,
    give_ref,
    table,
    acc_a,
    acc_b,
):
    pieces = [ref.at[h] for h in range(same_ref.shape[0]) for ref in (same_ref, other_ref)]
    n_out = 2 * keep_ref.shape[0]
    width, piece = pieces[0].shape
    per_piece = piece // TILE
    slots = tiles_ref.shape[0]
    double_table(pieces, table)
    for acc in (acc_a, acc_b):
        acc[...] = jnp.zeros_like(acc)
    lane = lax.broadcasted_iota(jnp.int32, (width, LANES), 1)
    masks = [lane // HALF == s for s in range(GROUP)]
    wide_lane = lax.broadcasted_iota(jnp.int32, (LANES, LANES), 1)
    parity = [(wide_lane // TILE == e).astype(BF16) for e in range(2)]
    count = count_ref[0, 0]
    row_flip = lax.axis_index("bcol") * per_piece
    col_flip = lax.axis_index("brow") * per_piece
    spare = n_out * per_piece

    for g in range(slots // GROUP):
        at = [table[cols_ref[g * GROUP + s] ^ col_flip] for s in range(GROUP)]
        block = tiles_ref[g * GROUP : (g + 1) * GROUP].reshape(LANES, LANES)
        turned = jnp.concatenate([block[LANES // 2 :], block[: LANES // 2]], axis=0)
        out = lax.dot_general(
            jnp.concatenate(at, axis=0).astype(BF16),
            jnp.concatenate([block * parity[0], turned * parity[1]], axis=0),
            (((1,), (1,)), ((), ())),
            preferred_element_type=F32,
        )
        for s in range(GROUP):
            t = g * GROUP + s
            part = out[width * s : width * (s + 1)]
            r = jnp.where(t < count, rows_ref[t] ^ row_flip, spare)
            part = jnp.where(
                masks[s], part[:, :LANES], jnp.where(masks[(s + 2) % GROUP], part[:, LANES:], 0.0)
            )
            acc = acc_a if s < 2 else acc_b
            acc[r] += part

    fold = fold_ref[...]
    pairs = per_piece // 2
    for n in range(n_out):
        blocks = []
        for q in range(2):
            for acc in (acc_a, acc_b):
                both = acc[n * per_piece : (n + 1) * per_piece].reshape(pairs, 2 * width, LANES)
                blocks.append(both[:, q * width : (q + 1) * width, :].reshape(pairs * width, LANES))
        wide = jnp.concatenate(blocks, axis=1)
        first = wide.astype(BF16)
        rest = (wide - first.astype(F32)).astype(BF16)
        out = jnp.dot(first, fold, preferred_element_type=F32)
        out = out + jnp.dot(rest, fold, preferred_element_type=F32)
        parts = [out[p * width : (p + 1) * width] for p in range(pairs)]
        if n % 2 == 0:
            for p in range(pairs):
                keep_ref[n // 2, :, p * LANES : (p + 1) * LANES] = parts[p]
        else:
            encode(parts, give_ref.at[n // 2])


def forward(same, other, tiles, tile_rows, tile_cols, counts, n_out, after):
    n_chips, width, piece = same.shape
    per_piece = piece // TILE
    half = jax.ShapeDtypeStruct((n_out // 2, width, piece), F32)
    coded = jax.ShapeDtypeStruct((n_out // 2, width, piece + LANES), jnp.int16)
    return pl.pallas_call(
        forward_kernel,
        in_specs=[SMEM] * 3 + [VMEM] * 4 + [ANY],
        out_specs=[VMEM] * 2,
        out_shape=[half, coded],
        scratch_shapes=[
            pltpu.VMEM((2 * n_chips * per_piece, width, LANES), F32),
            pltpu.VMEM((n_out * per_piece + 1, width, LANES), F32),
            pltpu.VMEM((n_out * per_piece + 1, width, LANES), F32),
        ],
        compiler_params=PARAMS,
        cost_estimate=pl.CostEstimate(
            flops=2 * tiles.size * 64, bytes_accessed=4 * tiles.size, transcendentals=0
        ),
        name="forward_product",
    )(tile_rows, tile_cols, counts, row_fold(), tiles, same, other, after)


def stack_kernel(n_after, *refs):
    out_ref, at = refs[-1], 0
    for ref in refs[: -1 - n_after]:
        if len(ref.shape) == 2:
            out_ref[at] = ref[...]
            at += 1
        else:
            out_ref[at : at + ref.shape[0]] = ref[...]
            at += ref.shape[0]


def stack(*parts, after=()):
    total = sum(x.shape[0] if x.ndim == 3 else 1 for x in parts)
    return pl.pallas_call(
        functools.partial(stack_kernel, len(after)),
        in_specs=[VMEM] * len(parts) + [ANY] * len(after),
        out_specs=VMEM,
        out_shape=jax.ShapeDtypeStruct((total,) + parts[0].shape[-2:], parts[0].dtype),
        compiler_params=PARAMS,
        name="stack_pieces",
    )(*parts, *after)


def pair_sum_kernel(keep_ref, *refs):
    n_chips = keep_ref.shape[0]
    gots, outs = refs[: 1 - n_chips], refs[1 - n_chips :]
    got = [ref.at[h] for ref in gots for h in range(ref.shape[0])]
    for h, out in enumerate(outs):
        out[...] = keep_ref[h + 1] + got[h + 1][...]


def pair_sum(keep, gots):
    parts, width, piece = keep.shape
    return pl.pallas_call(
        pair_sum_kernel,
        in_specs=[VMEM] * (1 + len(gots)),
        out_specs=[VMEM] * (parts - 1),
        out_shape=[jax.ShapeDtypeStruct((width, piece), F32)] * (parts - 1),
        compiler_params=PARAMS,
        name="core_pair_sum",
    )(keep, *gots)


def split_sum_kernel(keep_ref, got_ref, after_ref, next_keep, next_give):
    for h in range(next_keep.shape[0]):
        for n, got in enumerate(decode(got_ref.at[2 * h])):
            at = pl.ds(n * LANES, LANES)
            next_keep[h, :, at] = keep_ref[2 * h, :, at] + got
        sums = [
            keep_ref[2 * h + 1, :, n * LANES : (n + 1) * LANES] + got
            for n, got in enumerate(decode(got_ref.at[2 * h + 1]))
        ]
        encode(sums, next_give.at[h])


def split_sum(keep, got, after):
    parts, width, piece = keep.shape
    return pl.pallas_call(
        split_sum_kernel,
        in_specs=[VMEM] * 2 + [ANY],
        out_specs=[VMEM] * 2,
        out_shape=[
            jax.ShapeDtypeStruct((parts // 2, width, piece), F32),
            jax.ShapeDtypeStruct((parts // 2,) + got.shape[1:], got.dtype),
        ],
        compiler_params=PARAMS,
        name="halving_sum",
    )(keep, got, after)


def last_sum_kernel(*refs):
    chips, (brow_keep, brow_got, keep_ref, got_ref, out_ref) = refs[:-5], refs[-5:]
    for n, got in enumerate(decode(got_ref.at[0])):
        at = pl.ds(n * LANES, LANES)
        total = brow_keep[0, :, at] + brow_got[0, :, at]
        for ref in chips:
            total = total + ref[:, at]
        out_ref[:, at] = total + (keep_ref[0, :, at] + got)


def last_sum(keep, got, brow_keep, brow_got, chips):
    return pl.pallas_call(
        last_sum_kernel,
        in_specs=[VMEM] * (4 + len(chips)),
        out_specs=VMEM,
        out_shape=jax.ShapeDtypeStruct(keep.shape[1:], F32),
        compiler_params=PARAMS,
        name="last_sum",
    )(*chips, brow_keep, brow_got, keep, got)


def swap(x, axis, size, d):
    return lax.ppermute(x, axis, [(i, i ^ d) for i in range(size)])


def body(vectors, tiles, tile_rows, tile_cols, counts):
    n_rows = lax.axis_size("brow")
    n_cols = lax.axis_size("bcol")
    own = stack(vectors)
    chips = [swap(vectors, "brow", n_rows, 2 * h) for h in range(1, n_rows // 2)]
    segment, d = own, n_cols // 2
    while d > 0:
        first = d == n_cols // 2
        segment = stack(segment, swap(vectors[None] if first else segment, "bcol", n_cols, d))
        d //= 2
    blocks = prep(tiles)
    same = stack(own, *chips, after=(blocks,))
    other = swap(same, "brow", n_rows, 1)

    col_keep, *col_give = backward(segment, blocks, tile_rows, tile_cols, counts, n_rows, same)
    row_keep, give = forward(same, other, blocks, tile_rows, tile_cols, counts, n_cols, col_give[0])
    col_got = [swap(x, "brow", n_rows, 1) for x in col_give]
    sums = pair_sum(col_keep, col_got)
    from_chips = [swap(x, "brow", n_rows, 2 * (h + 1)) for h, x in enumerate(sums)]
    row_got, d = swap(give, "bcol", n_cols, 1), 2
    while d < n_cols:
        row_keep, give = split_sum(row_keep, row_got, sums[0])
        row_got = swap(give, "bcol", n_cols, d)
        d *= 2
    return last_sum(row_keep, row_got, col_keep, col_got[0], from_chips)


def solution(mesh):
    return jax.shard_map(
        body,
        mesh=mesh,
        in_specs=(
            P(None, ("brow", "bcol")),
            P(("brow", "bcol"), None),
            P(("brow", "bcol")),
            P(("brow", "bcol")),
            P("brow", "bcol"),
        ),
        out_specs=P(None, ("brow", "bcol")),
        check_vma=False,
    )
```

```python
import functools

import jax
import jax.numpy as jnp
import numpy as np
from jax import lax
from jax.experimental import pallas as pl
from jax.experimental.pallas import tpu as pltpu
from jax.sharding import PartitionSpec as P

TILE = 64
LANES = 128
HALF = TILE // 2
GROUP = LANES // HALF
STEPS = 32000.0
F32 = jnp.float32
BF16 = jnp.bfloat16
VMEM = pl.BlockSpec(memory_space=pltpu.VMEM)
ANY = pl.BlockSpec(memory_space=pl.ANY)
SMEM = pl.BlockSpec(memory_space=pltpu.SMEM)
PARAMS = pltpu.CompilerParams(vmem_limit_bytes=48 * 1024 * 1024)


def row_spread():
    out = np.zeros((LANES, 2, 2, GROUP, HALF), np.float32)
    for q in range(2):
        for e in range(2):
            for m in range(HALF):
                out[q * TILE + 2 * m + e, q, e, :, m] = 1
    return jnp.asarray(out.reshape(LANES, 4 * LANES), BF16)


def row_fold():
    out = np.zeros((2, 2, 2, GROUP // 2, HALF, LANES), np.float32)
    for q in range(2):
        for e in range(2):
            for m in range(HALF):
                out[q, 0, e, :, m, q * TILE + 2 * m + e] = 1
                out[q, 1, 1 - e, :, m, q * TILE + 2 * m + e] = 1
    return jnp.asarray(out.reshape(4 * LANES, LANES), BF16)


def encode(values, out_ref):
    width, piece = values[0].shape[0], LANES * len(values)
    lane = lax.broadcasted_iota(jnp.int32, (width, LANES), 1)
    exponents = jnp.zeros((width, LANES), F32)
    for n, value in enumerate(values):
        top = jnp.max(jnp.abs(value), axis=1, keepdims=True)
        e = jnp.clip(jnp.ceil(jnp.log2(top)), -100.0, 100.0)
        exponents = jnp.where(lane == n, e, exponents)
        scaled = jnp.floor(value * (STEPS * jnp.exp2(-e)) + 0.5)
        out_ref[:, n * LANES : (n + 1) * LANES] = scaled.astype(jnp.int32).astype(jnp.int16)
    out_ref[:, piece:] = exponents.astype(jnp.int32).astype(jnp.int16)


def decode(ref):
    chunks = ref.shape[1] // LANES - 1
    exponents = ref[:, chunks * LANES :].astype(jnp.int32).astype(F32)
    scales = jnp.exp2(exponents) * (1.0 / STEPS)
    return [
        ref[:, n * LANES : (n + 1) * LANES].astype(jnp.int32).astype(F32) * scales[:, n : n + 1]
        for n in range(chunks)
    ]


def prep_kernel(tiles_ref, after_ref, out_ref, wide):
    for b in range(tiles_ref.shape[0]):
        wide[b] = tiles_ref[b].astype(F32).reshape(HALF * 8, LANES)
        for s in range(8):
            out_ref[8 * b + s] = wide[b, pl.ds(s, HALF, stride=8), :].astype(BF16)


def prep(tiles, after):
    slots = tiles.shape[0]
    blocks = slots // 8
    view = tiles.reshape(blocks, 8, HALF, LANES).swapaxes(1, 2)
    return pl.pallas_call(
        prep_kernel,
        in_specs=[VMEM, ANY],
        out_specs=VMEM,
        out_shape=jax.ShapeDtypeStruct((slots, HALF, LANES), BF16),
        scratch_shapes=[pltpu.VMEM((blocks, HALF * 8, LANES), F32)],
        compiler_params=PARAMS,
        cost_estimate=pl.CostEstimate(flops=0, bytes_accessed=4 * tiles.size, transcendentals=0),
        name="prep_tiles",
    )(view, after)


def doubled(size):
    order, d = [0], size // 2
    while d > 0:
        order += [x ^ d for x in order]
        d //= 2
    return order


def build_table(pieces, spread, table):
    width, piece = pieces[0].shape
    pairs = piece // LANES
    for n, ref in enumerate(pieces):
        rows = jnp.concatenate([ref[:, p * LANES : (p + 1) * LANES] for p in range(pairs)], axis=0)
        wide = jnp.dot(rows, spread, preferred_element_type=F32)
        wide = wide.reshape(pairs, width, 4 * LANES)
        for q in range(2):
            both = jnp.concatenate(
                [wide[:, :, (2 * q + e) * LANES : (2 * q + e + 1) * LANES] for e in range(2)], axis=1
            ).astype(BF16)
            for p in range(pairs):
                table[n * 2 * pairs + 2 * p + q] = both[p]


def backward_kernel(
    rows_ref, cols_ref, count_ref, spread_ref, tiles_ref, seg_ref, after_ref, keep_ref, *refs
):
    pieces = [seg_ref.at[at] for at in np.argsort(doubled(seg_ref.shape[0]))]
    *give_refs, table, acc_a, acc_b = refs
    per_give = give_refs[0].shape[0]
    n_out = 2 * keep_ref.shape[0]
    width, piece = pieces[0].shape
    per_piece = piece // TILE
    slots = tiles_ref.shape[0]
    build_table(pieces, spread_ref[...], table)
    for acc in (acc_a, acc_b):
        acc[...] = jnp.zeros_like(acc)
    lane = lax.broadcasted_iota(jnp.int32, (2 * width, LANES), 1)
    masks = [(lane // HALF == s).astype(BF16) for s in range(GROUP)]
    low = lax.broadcasted_iota(jnp.int32, (width, LANES), 1) < TILE
    count = count_ref[0, 0]
    row_flip = lax.axis_index("bcol") * per_piece
    col_flip = lax.axis_index("brow") * per_piece
    spare = n_out * per_piece

    for g in range(slots // GROUP):
        at = [table[rows_ref[g * GROUP + s] ^ row_flip] * masks[s] for s in range(GROUP)]
        block = tiles_ref[g * GROUP : (g + 1) * GROUP].reshape(LANES, LANES)
        out = jnp.dot(jnp.concatenate(at, axis=0), block, preferred_element_type=F32)
        for s in range(GROUP):
            t = g * GROUP + s
            part = out[2 * width * s : 2 * width * (s + 1)]
            part = jnp.where(low, part[:width], part[width:])
            c = jnp.where(t < count, cols_ref[t] ^ col_flip, spare)
            acc = acc_a if s % 2 == 0 else acc_b
            acc[c] += part

    for n in range(n_out):
        h = n // 2
        dest = keep_ref.at[h] if n % 2 == 0 else give_refs[h // per_give].at[h % per_give]
        for p in range(per_piece // 2):
            at = n * per_piece + 2 * p
            a = acc_a[at] + acc_b[at]
            b = acc_a[at + 1] + acc_b[at + 1]
            dest[:, p * LANES : (p + 1) * LANES] = jnp.where(low, a, b) + pltpu.roll(
                jnp.where(low, b, a), TILE, 1
            )


def backward(segment, tiles, tile_rows, tile_cols, counts, n_out, after):
    n_in, width, piece = segment.shape
    per_piece = piece // TILE
    half = jax.ShapeDtypeStruct((n_out // 2, width, piece), F32)
    quarter = jax.ShapeDtypeStruct((n_out // 4, width, piece), F32)
    return pl.pallas_call(
        backward_kernel,
        in_specs=[SMEM] * 3 + [VMEM] * 3 + [ANY],
        out_specs=[VMEM] * 3,
        out_shape=[half, quarter, quarter],
        scratch_shapes=[
            pltpu.VMEM((n_in * per_piece, 2 * width, LANES), BF16),
            pltpu.VMEM((n_out * per_piece + 1, width, LANES), F32),
            pltpu.VMEM((n_out * per_piece + 1, width, LANES), F32),
        ],
        compiler_params=PARAMS,
        cost_estimate=pl.CostEstimate(
            flops=2 * tiles.size * 64, bytes_accessed=4 * tiles.size, transcendentals=0
        ),
        name="transpose_product",
    )(tile_rows, tile_cols, counts, row_spread(), tiles, segment, after)


def double_table(pieces, table):
    width, piece = pieces[0].shape
    low = lax.broadcasted_iota(jnp.int32, (width, LANES), 1) < TILE
    for n, ref in enumerate(pieces):
        for p in range(piece // LANES):
            pair = ref[:, p * LANES : (p + 1) * LANES].astype(F32)
            turned = pltpu.roll(pair, TILE, 1)
            at = (n * piece + p * LANES) // TILE
            table[at] = jnp.where(low, pair, turned)
            table[at + 1] = jnp.where(low, turned, pair)


def forward_kernel(
    rows_ref,
    cols_ref,
    count_ref,
    fold_ref,
    tiles_ref,
    same_ref,
    other_ref,
    after_ref,
    keep_ref,
    give_ref,
    table,
    acc_a,
    acc_b,
):
    pieces = [ref.at[h] for h in range(same_ref.shape[0]) for ref in (same_ref, other_ref)]
    n_out = 2 * keep_ref.shape[0]
    width, piece = pieces[0].shape
    per_piece = piece // TILE
    slots = tiles_ref.shape[0]
    double_table(pieces, table)
    for acc in (acc_a, acc_b):
        acc[...] = jnp.zeros_like(acc)
    lane = lax.broadcasted_iota(jnp.int32, (width, LANES), 1)
    masks = [lane // HALF == s for s in range(GROUP)]
    wide_lane = lax.broadcasted_iota(jnp.int32, (LANES, LANES), 1)
    parity = [(wide_lane // TILE == e).astype(BF16) for e in range(2)]
    count = count_ref[0, 0]
    row_flip = lax.axis_index("bcol") * per_piece
    col_flip = lax.axis_index("brow") * per_piece
    spare = n_out * per_piece

    for g in range(slots // GROUP):
        at = [table[cols_ref[g * GROUP + s] ^ col_flip] for s in range(GROUP)]
        block = tiles_ref[g * GROUP : (g + 1) * GROUP].reshape(LANES, LANES)
        turned = jnp.concatenate([block[LANES // 2 :], block[: LANES // 2]], axis=0)
        out = lax.dot_general(
            jnp.concatenate(at, axis=0).astype(BF16),
            jnp.concatenate([block * parity[0], turned * parity[1]], axis=0),
            (((1,), (1,)), ((), ())),
            preferred_element_type=F32,
        )
        for s in range(GROUP):
            t = g * GROUP + s
            part = out[width * s : width * (s + 1)]
            r = jnp.where(t < count, rows_ref[t] ^ row_flip, spare)
            part = jnp.where(
                masks[s], part[:, :LANES], jnp.where(masks[(s + 2) % GROUP], part[:, LANES:], 0.0)
            )
            acc = acc_a if s < 2 else acc_b
            acc[r] += part

    fold = fold_ref[...]
    pairs = per_piece // 2
    for n in range(n_out):
        blocks = []
        for q in range(2):
            for acc in (acc_a, acc_b):
                both = acc[n * per_piece : (n + 1) * per_piece].reshape(pairs, 2 * width, LANES)
                blocks.append(both[:, q * width : (q + 1) * width, :].reshape(pairs * width, LANES))
        wide = jnp.concatenate(blocks, axis=1)
        first = wide.astype(BF16)
        rest = (wide - first.astype(F32)).astype(BF16)
        out = jnp.dot(first, fold, preferred_element_type=F32)
        out = out + jnp.dot(rest, fold, preferred_element_type=F32)
        parts = [out[p * width : (p + 1) * width] for p in range(pairs)]
        if n % 2 == 0:
            for p in range(pairs):
                keep_ref[n // 2, :, p * LANES : (p + 1) * LANES] = parts[p]
        else:
            encode(parts, give_ref.at[n // 2])


def forward(same, other, tiles, tile_rows, tile_cols, counts, n_out, after):
    n_chips, width, piece = same.shape
    per_piece = piece // TILE
    half = jax.ShapeDtypeStruct((n_out // 2, width, piece), F32)
    coded = jax.ShapeDtypeStruct((n_out // 2, width, piece + LANES), jnp.int16)
    return pl.pallas_call(
        forward_kernel,
        in_specs=[SMEM] * 3 + [VMEM] * 4 + [ANY],
        out_specs=[VMEM] * 2,
        out_shape=[half, coded],
        scratch_shapes=[
            pltpu.VMEM((2 * n_chips * per_piece, width, LANES), F32),
            pltpu.VMEM((n_out * per_piece + 1, width, LANES), F32),
            pltpu.VMEM((n_out * per_piece + 1, width, LANES), F32),
        ],
        compiler_params=PARAMS,
        cost_estimate=pl.CostEstimate(
            flops=2 * tiles.size * 64, bytes_accessed=4 * tiles.size, transcendentals=0
        ),
        name="forward_product",
    )(tile_rows, tile_cols, counts, row_fold(), tiles, same, other, after)


def stack_kernel(n_after, *refs):
    out_ref, at = refs[-1], 0
    for ref in refs[: -1 - n_after]:
        if len(ref.shape) == 2:
            out_ref[at] = ref[...]
            at += 1
        else:
            out_ref[at : at + ref.shape[0]] = ref[...]
            at += ref.shape[0]


def stack(*parts, after=()):
    total = sum(x.shape[0] if x.ndim == 3 else 1 for x in parts)
    return pl.pallas_call(
        functools.partial(stack_kernel, len(after)),
        in_specs=[VMEM] * len(parts) + [ANY] * len(after),
        out_specs=VMEM,
        out_shape=jax.ShapeDtypeStruct((total,) + parts[0].shape[-2:], parts[0].dtype),
        compiler_params=PARAMS,
        name="stack_pieces",
    )(*parts, *after)


def pair_sum_kernel(chips, keep_ref, *refs):
    outs = refs[-len(chips) :]
    gots = refs[: -1 - len(chips)]
    got = [ref.at[h] for ref in gots for h in range(ref.shape[0])]
    for h, out in zip(chips, outs):
        if out.dtype == F32:
            out[...] = keep_ref[h] + got[h][...]
        else:
            total = keep_ref[h] + got[h][...]
            encode([total[:, n : n + LANES] for n in range(0, total.shape[1], LANES)], out)


def pair_sum(chips, keep, gots, after, coded=False):
    _, width, piece = keep.shape
    one = jax.ShapeDtypeStruct((width, piece), F32)
    if coded:
        one = jax.ShapeDtypeStruct((width, piece + LANES), jnp.int16)
    return pl.pallas_call(
        functools.partial(pair_sum_kernel, chips),
        in_specs=[VMEM] * (1 + len(gots)) + [ANY],
        out_specs=[VMEM] * len(chips),
        out_shape=[one] * len(chips),
        compiler_params=PARAMS,
        name="core_pair_sum",
    )(keep, *gots, after)


def split_sum_kernel(keep_ref, got_ref, after_ref, next_keep, next_give):
    for h in range(next_keep.shape[0]):
        for n, got in enumerate(decode(got_ref.at[2 * h])):
            at = pl.ds(n * LANES, LANES)
            next_keep[h, :, at] = keep_ref[2 * h, :, at] + got
        sums = [
            keep_ref[2 * h + 1, :, n * LANES : (n + 1) * LANES] + got
            for n, got in enumerate(decode(got_ref.at[2 * h + 1]))
        ]
        encode(sums, next_give.at[h])


def split_sum(keep, got, after):
    parts, width, piece = keep.shape
    return pl.pallas_call(
        split_sum_kernel,
        in_specs=[VMEM] * 2 + [ANY],
        out_specs=[VMEM] * 2,
        out_shape=[
            jax.ShapeDtypeStruct((parts // 2, width, piece), F32),
            jax.ShapeDtypeStruct((parts // 2,) + got.shape[1:], got.dtype),
        ],
        compiler_params=PARAMS,
        name="halving_sum",
    )(keep, got, after)


def last_sum_kernel(keep_ref, got_ref, brow_keep, brow_got, *refs):
    chips, out_ref = refs[:-1], refs[-1]
    for n, got in enumerate(decode(got_ref.at[0])):
        at = pl.ds(n * LANES, LANES)
        total = brow_keep[0, :, at] + brow_got[0, :, at]
        for ref in chips:
            total = total + ref[:, at]
        out_ref[:, at] = total + (keep_ref[0, :, at] + got)


def last_sum(keep, got, brow_keep, brow_got, chips):
    return pl.pallas_call(
        last_sum_kernel,
        in_specs=[VMEM] * (4 + len(chips)),
        out_specs=VMEM,
        out_shape=jax.ShapeDtypeStruct(keep.shape[1:], F32),
        compiler_params=PARAMS,
        name="last_sum",
    )(keep, got, brow_keep, brow_got, *chips)


def add_kernel(x_ref, y_ref, out_ref):
    for n, got in enumerate(decode(y_ref)):
        at = pl.ds(n * LANES, LANES)
        out_ref[:, at] = x_ref[:, at] + got


def add(x, y):
    return pl.pallas_call(
        add_kernel,
        in_specs=[VMEM] * 2,
        out_specs=VMEM,
        out_shape=jax.ShapeDtypeStruct(x.shape, x.dtype),
        compiler_params=PARAMS,
        name="add_last",
    )(x, y)


def swap(x, axis, size, d):
    return lax.ppermute(x, axis, [(i, i ^ d) for i in range(size)])


def body(vectors, tiles, tile_rows, tile_cols, counts):
    n_rows = lax.axis_size("brow")
    n_cols = lax.axis_size("bcol")
    own = stack(vectors)
    chips = [swap(vectors, "brow", n_rows, 2 * h) for h in range(1, n_rows // 2)]
    far = swap(vectors[None], "bcol", n_cols, n_cols // 2)
    segment, d = stack(own, far), n_cols // 4
    blocks = prep(tiles, own)
    while d > 0:
        segment = stack(segment, swap(segment, "bcol", n_cols, d))
        d //= 2
    same = stack(own, *chips, after=(blocks,))
    other = swap(same, "brow", n_rows, 1)

    col_keep, *col_give = backward(segment, blocks, tile_rows, tile_cols, counts, n_rows, same)
    row_keep, give = forward(same, other, blocks, tile_rows, tile_cols, counts, n_cols, col_give[0])
    col_got = [swap(x, "brow", n_rows, 1) for x in col_give]
    sums = pair_sum(tuple(range(2, n_rows // 2)), col_keep, col_got, give)
    from_chips = [swap(x, "brow", n_rows, 2 * (h + 2)) for h, x in enumerate(sums)]
    row_got, d = swap(give, "bcol", n_cols, 1), 2
    while d < n_cols:
        row_keep, give = split_sum(row_keep, row_got, sums[0])
        row_got = swap(give, "bcol", n_cols, d)
        d *= 2
    (last,) = pair_sum((1,), col_keep, col_got, give, coded=True)
    total = last_sum(row_keep, row_got, col_keep, col_got[0], from_chips)
    return add(total, swap(last, "brow", n_rows, 2))


def solution(mesh):
    return jax.shard_map(
        body,
        mesh=mesh,
        in_specs=(
            P(None, ("brow", "bcol")),
            P(("brow", "bcol"), None),
            P(("brow", "bcol")),
            P(("brow", "bcol")),
            P("brow", "bcol"),
        ),
        out_specs=P(None, ("brow", "bcol")),
        check_vma=False,
    )
```

```python
import functools

import jax
import jax.numpy as jnp
import numpy as np
from jax import lax
from jax.experimental import pallas as pl
from jax.experimental.pallas import tpu as pltpu
from jax.sharding import PartitionSpec as P

TILE = 64
LANES = 128
HALF = TILE // 2
GROUP = LANES // HALF
STEPS = 32000.0
F32 = jnp.float32
BF16 = jnp.bfloat16
VMEM = pl.BlockSpec(memory_space=pltpu.VMEM)
ANY = pl.BlockSpec(memory_space=pl.ANY)
SMEM = pl.BlockSpec(memory_space=pltpu.SMEM)
PARAMS = pltpu.CompilerParams(vmem_limit_bytes=48 * 1024 * 1024)


def row_spread():
    out = np.zeros((LANES, 2, 2, GROUP, HALF), np.float32)
    for q in range(2):
        for e in range(2):
            for m in range(HALF):
                out[q * TILE + 2 * m + e, q, e, :, m] = 1
    return jnp.asarray(out.reshape(LANES, 4 * LANES), BF16)


def row_fold():
    out = np.zeros((2, 2, 2, GROUP // 2, HALF, LANES), np.float32)
    for q in range(2):
        for e in range(2):
            for m in range(HALF):
                out[q, 0, e, :, m, q * TILE + 2 * m + e] = 1
                out[q, 1, 1 - e, :, m, q * TILE + 2 * m + e] = 1
    return jnp.asarray(out.reshape(4 * LANES, LANES), BF16)


def encode(values, out_ref):
    width, piece = values[0].shape[0], LANES * len(values)
    lane = lax.broadcasted_iota(jnp.int32, (width, LANES), 1)
    exponents = jnp.zeros((width, LANES), F32)
    for n, value in enumerate(values):
        top = jnp.max(jnp.abs(value), axis=1, keepdims=True)
        e = jnp.clip(jnp.ceil(jnp.log2(top)), -100.0, 100.0)
        exponents = jnp.where(lane == n, e, exponents)
        scaled = jnp.floor(value * (STEPS * jnp.exp2(-e)) + 0.5)
        out_ref[:, n * LANES : (n + 1) * LANES] = scaled.astype(jnp.int32).astype(jnp.int16)
    out_ref[:, piece:] = exponents.astype(jnp.int32).astype(jnp.int16)


def decode(ref):
    chunks = ref.shape[1] // LANES - 1
    exponents = ref[:, chunks * LANES :].astype(jnp.int32).astype(F32)
    scales = jnp.exp2(exponents) * (1.0 / STEPS)
    return [
        ref[:, n * LANES : (n + 1) * LANES].astype(jnp.int32).astype(F32) * scales[:, n : n + 1]
        for n in range(chunks)
    ]


def prep_kernel(tiles_ref, after_ref, out_ref, wide):
    for b in range(tiles_ref.shape[0]):
        wide[b] = tiles_ref[b].astype(F32).reshape(HALF * 8, LANES)
        for s in range(8):
            out_ref[8 * b + s] = wide[b, pl.ds(s, HALF, stride=8), :].astype(BF16)


def prep(tiles, after):
    slots = tiles.shape[0]
    blocks = slots // 8
    view = tiles.reshape(blocks, 8, HALF, LANES).swapaxes(1, 2)
    return pl.pallas_call(
        prep_kernel,
        in_specs=[VMEM, ANY],
        out_specs=VMEM,
        out_shape=jax.ShapeDtypeStruct((slots, HALF, LANES), BF16),
        scratch_shapes=[pltpu.VMEM((blocks, HALF * 8, LANES), F32)],
        compiler_params=PARAMS,
        cost_estimate=pl.CostEstimate(flops=0, bytes_accessed=4 * tiles.size, transcendentals=0),
        name="prep_tiles",
    )(view, after)


def doubled(size):
    order, d = [0], size // 2
    while d > 0:
        order += [x ^ d for x in order]
        d //= 2
    return order


def build_table(pieces, spread, table):
    width, piece = pieces[0].shape
    pairs = piece // LANES
    for n, ref in enumerate(pieces):
        rows = jnp.concatenate([ref[:, p * LANES : (p + 1) * LANES] for p in range(pairs)], axis=0)
        wide = jnp.dot(rows, spread, preferred_element_type=F32)
        wide = wide.reshape(pairs, width, 4 * LANES)
        for q in range(2):
            both = jnp.concatenate(
                [wide[:, :, (2 * q + e) * LANES : (2 * q + e + 1) * LANES] for e in range(2)], axis=1
            ).astype(BF16)
            for p in range(pairs):
                table[n * 2 * pairs + 2 * p + q] = both[p]


def backward_kernel(
    rows_ref, cols_ref, count_ref, spread_ref, tiles_ref, seg_ref, after_ref, keep_ref, *refs
):
    pieces = [seg_ref.at[at] for at in np.argsort(doubled(seg_ref.shape[0]))]
    *give_refs, table, acc_a, acc_b = refs
    per_give = give_refs[0].shape[0]
    n_out = 2 * keep_ref.shape[0]
    width, piece = pieces[0].shape
    per_piece = piece // TILE
    slots = tiles_ref.shape[0]
    build_table(pieces, spread_ref[...], table)
    for acc in (acc_a, acc_b):
        acc[...] = jnp.zeros_like(acc)
    lane = lax.broadcasted_iota(jnp.int32, (2 * width, LANES), 1)
    masks = [(lane // HALF == s).astype(BF16) for s in range(GROUP)]
    low = lax.broadcasted_iota(jnp.int32, (width, LANES), 1) < TILE
    count = count_ref[0, 0]
    row_flip = lax.axis_index("bcol") * per_piece
    col_flip = lax.axis_index("brow") * per_piece
    spare = n_out * per_piece

    for g in range(slots // GROUP):
        at = [table[rows_ref[g * GROUP + s] ^ row_flip] * masks[s] for s in range(GROUP)]
        block = tiles_ref[g * GROUP : (g + 1) * GROUP].reshape(LANES, LANES)
        out = jnp.dot(jnp.concatenate(at, axis=0), block, preferred_element_type=F32)
        for s in range(GROUP):
            t = g * GROUP + s
            part = out[2 * width * s : 2 * width * (s + 1)]
            part = jnp.where(low, part[:width], part[width:])
            c = jnp.where(t < count, cols_ref[t] ^ col_flip, spare)
            acc = acc_a if s % 2 == 0 else acc_b
            acc[c] += part

    for n in range(n_out):
        h = n // 2
        dest = keep_ref.at[h] if n % 2 == 0 else give_refs[h // per_give].at[h % per_give]
        for p in range(per_piece // 2):
            at = n * per_piece + 2 * p
            a = acc_a[at] + acc_b[at]
            b = acc_a[at + 1] + acc_b[at + 1]
            dest[:, p * LANES : (p + 1) * LANES] = jnp.where(low, a, b) + pltpu.roll(
                jnp.where(low, b, a), TILE, 1
            )


def backward(segment, tiles, tile_rows, tile_cols, counts, n_out, after):
    n_in, width, piece = segment.shape
    per_piece = piece // TILE
    half = jax.ShapeDtypeStruct((n_out // 2, width, piece), F32)
    quarter = jax.ShapeDtypeStruct((n_out // 4, width, piece), F32)
    return pl.pallas_call(
        backward_kernel,
        in_specs=[SMEM] * 3 + [VMEM] * 3 + [ANY],
        out_specs=[VMEM] * 3,
        out_shape=[half, quarter, quarter],
        scratch_shapes=[
            pltpu.VMEM((n_in * per_piece, 2 * width, LANES), BF16),
            pltpu.VMEM((n_out * per_piece + 1, width, LANES), F32),
            pltpu.VMEM((n_out * per_piece + 1, width, LANES), F32),
        ],
        compiler_params=PARAMS,
        cost_estimate=pl.CostEstimate(
            flops=2 * tiles.size * 64, bytes_accessed=4 * tiles.size, transcendentals=0
        ),
        name="transpose_product",
    )(tile_rows, tile_cols, counts, row_spread(), tiles, segment, after)


def double_table(pieces, table):
    width, piece = pieces[0].shape
    low = lax.broadcasted_iota(jnp.int32, (width, LANES), 1) < TILE
    for n, ref in enumerate(pieces):
        for p in range(piece // LANES):
            pair = ref[:, p * LANES : (p + 1) * LANES].astype(F32)
            turned = pltpu.roll(pair, TILE, 1)
            at = (n * piece + p * LANES) // TILE
            table[at] = jnp.where(low, pair, turned)
            table[at + 1] = jnp.where(low, turned, pair)


def forward_kernel(
    rows_ref,
    cols_ref,
    count_ref,
    fold_ref,
    tiles_ref,
    same_ref,
    other_ref,
    after_ref,
    keep_ref,
    *refs,
):
    *give_refs, table, acc_a, acc_b = refs
    pieces = [ref.at[h] for h in range(same_ref.shape[0]) for ref in (same_ref, other_ref)]
    n_out = 1 + len(give_refs)
    width, piece = pieces[0].shape
    per_piece = piece // TILE
    slots = tiles_ref.shape[0]
    double_table(pieces, table)
    for acc in (acc_a, acc_b):
        acc[...] = jnp.zeros_like(acc)
    lane = lax.broadcasted_iota(jnp.int32, (width, LANES), 1)
    masks = [lane // HALF == s for s in range(GROUP)]
    wide_lane = lax.broadcasted_iota(jnp.int32, (LANES, LANES), 1)
    parity = [(wide_lane // TILE == e).astype(BF16) for e in range(2)]
    count = count_ref[0, 0]
    row_flip = lax.axis_index("bcol") * per_piece
    col_flip = lax.axis_index("brow") * per_piece
    spare = n_out * per_piece

    for g in range(slots // GROUP):
        at = [table[cols_ref[g * GROUP + s] ^ col_flip] for s in range(GROUP)]
        block = tiles_ref[g * GROUP : (g + 1) * GROUP].reshape(LANES, LANES)
        turned = jnp.concatenate([block[LANES // 2 :], block[: LANES // 2]], axis=0)
        out = lax.dot_general(
            jnp.concatenate(at, axis=0).astype(BF16),
            jnp.concatenate([block * parity[0], turned * parity[1]], axis=0),
            (((1,), (1,)), ((), ())),
            preferred_element_type=F32,
        )
        for s in range(GROUP):
            t = g * GROUP + s
            part = out[width * s : width * (s + 1)]
            r = jnp.where(t < count, rows_ref[t] ^ row_flip, spare)
            part = jnp.where(
                masks[s], part[:, :LANES], jnp.where(masks[(s + 2) % GROUP], part[:, LANES:], 0.0)
            )
            acc = acc_a if s < 2 else acc_b
            acc[r] += part

    fold = fold_ref[...]
    pairs = per_piece // 2
    for n in range(n_out):
        blocks = []
        for q in range(2):
            for acc in (acc_a, acc_b):
                both = acc[n * per_piece : (n + 1) * per_piece].reshape(pairs, 2 * width, LANES)
                blocks.append(both[:, q * width : (q + 1) * width, :].reshape(pairs * width, LANES))
        wide = jnp.concatenate(blocks, axis=1)
        first = wide.astype(BF16)
        rest = (wide - first.astype(F32)).astype(BF16)
        out = jnp.dot(first, fold, preferred_element_type=F32)
        out = out + jnp.dot(rest, fold, preferred_element_type=F32)
        parts = [out[p * width : (p + 1) * width] for p in range(pairs)]
        if n == 0:
            for p in range(pairs):
                keep_ref[:, p * LANES : (p + 1) * LANES] = parts[p]
        else:
            encode(parts, give_refs[n - 1])


def forward(same, other, tiles, tile_rows, tile_cols, counts, n_out, after):
    n_chips, width, piece = same.shape
    per_piece = piece // TILE
    own = jax.ShapeDtypeStruct((width, piece), F32)
    coded = jax.ShapeDtypeStruct((width, piece + LANES), jnp.int16)
    return pl.pallas_call(
        forward_kernel,
        in_specs=[SMEM] * 3 + [VMEM] * 4 + [ANY],
        out_specs=[VMEM] * n_out,
        out_shape=[own] + [coded] * (n_out - 1),
        scratch_shapes=[
            pltpu.VMEM((2 * n_chips * per_piece, width, LANES), F32),
            pltpu.VMEM((n_out * per_piece + 1, width, LANES), F32),
            pltpu.VMEM((n_out * per_piece + 1, width, LANES), F32),
        ],
        compiler_params=PARAMS,
        cost_estimate=pl.CostEstimate(
            flops=2 * tiles.size * 64, bytes_accessed=4 * tiles.size, transcendentals=0
        ),
        name="forward_product",
    )(tile_rows, tile_cols, counts, row_fold(), tiles, same, other, after)


def stack_kernel(n_after, *refs):
    out_ref, at = refs[-1], 0
    for ref in refs[: -1 - n_after]:
        if len(ref.shape) == 2:
            out_ref[at] = ref[...].astype(out_ref.dtype)
            at += 1
        else:
            out_ref[at : at + ref.shape[0]] = ref[...]
            at += ref.shape[0]


def stack(*parts, after=()):
    total = sum(x.shape[0] if x.ndim == 3 else 1 for x in parts)
    return pl.pallas_call(
        functools.partial(stack_kernel, len(after)),
        in_specs=[VMEM] * len(parts) + [ANY] * len(after),
        out_specs=VMEM,
        out_shape=jax.ShapeDtypeStruct((total,) + parts[0].shape[-2:], parts[0].dtype),
        compiler_params=PARAMS,
        name="stack_pieces",
    )(*parts, *after)


def split_sum_kernel(keep_ref, *refs):
    gots, (next_keep, next_give) = refs[:-3], refs[-2:]
    got = [ref.at[h] for ref in gots for h in range(ref.shape[0])]
    for h in range(next_keep.shape[0]):
        next_keep[h] = keep_ref[2 * h] + got[2 * h][...]
        odd = keep_ref[2 * h + 1] + got[2 * h + 1][...]
        if next_give.dtype == F32:
            next_give[h] = odd
        else:
            chunks = [odd[:, n : n + LANES] for n in range(0, odd.shape[1], LANES)]
            encode(chunks, next_give.at[h])


def split_sum(keep, gots, after):
    parts, width, piece = keep.shape
    half = jax.ShapeDtypeStruct((parts // 2, width, piece), F32)
    coded = jax.ShapeDtypeStruct((parts // 2, width, piece + LANES), jnp.int16)
    return pl.pallas_call(
        split_sum_kernel,
        in_specs=[VMEM] * (1 + len(gots)) + [ANY],
        out_specs=[VMEM] * 2,
        out_shape=[half, half if parts > 2 else coded],
        compiler_params=PARAMS,
        name="halving_sum",
    )(keep, *gots, after)


def z_sum_kernel(mine_ref, *refs):
    gots, out_ref = refs[:-1], refs[-1]
    parts = [decode(ref) for ref in gots]
    for n in range(mine_ref.shape[1] // LANES):
        at = pl.ds(n * LANES, LANES)
        total = mine_ref[:, at]
        for part in parts:
            total = total + part[n]
        out_ref[:, at] = total


def z_sum(mine, gots):
    return pl.pallas_call(
        z_sum_kernel,
        in_specs=[VMEM] * (1 + len(gots)),
        out_specs=VMEM,
        out_shape=jax.ShapeDtypeStruct(mine.shape, F32),
        compiler_params=PARAMS,
        name="z_sum",
    )(mine, *gots)


def last_sum_kernel(total_ref, keep_ref, got_ref, out_ref):
    for n, got in enumerate(decode(got_ref.at[0])):
        at = pl.ds(n * LANES, LANES)
        out_ref[:, at] = total_ref[:, at] + (keep_ref[0, :, at] + got)


def last_sum(total, keep, got):
    return pl.pallas_call(
        last_sum_kernel,
        in_specs=[VMEM] * 3,
        out_specs=VMEM,
        out_shape=jax.ShapeDtypeStruct(total.shape, F32),
        compiler_params=PARAMS,
        name="last_sum",
    )(total, keep, got)


def take_kernel(x_ref, out_ref, wide_ref):
    out_ref[0] = x_ref[...]
    wide_ref[...] = x_ref[...].astype(F32)


def take(x):
    return pl.pallas_call(
        take_kernel,
        in_specs=[VMEM],
        out_specs=[VMEM] * 2,
        out_shape=[
            jax.ShapeDtypeStruct((1,) + x.shape, x.dtype),
            jax.ShapeDtypeStruct(x.shape, F32),
        ],
        compiler_params=PARAMS,
        name="take_piece",
    )(x)


def swap(x, axis, size, d):
    return lax.ppermute(x, axis, [(i, i ^ d) for i in range(size)])


def body(vectors, tiles, tile_rows, tile_cols, counts):
    n_rows = lax.axis_size("brow")
    n_cols = lax.axis_size("bcol")
    own, wide = take(vectors)
    chips = [swap(wide, "brow", n_rows, 2 * h) for h in range(1, n_rows // 2)]
    far = swap(vectors[None], "bcol", n_cols, n_cols // 2)
    segment, d = stack(own, far), n_cols // 4
    blocks = prep(tiles, own)
    while d > 0:
        segment = stack(segment, swap(segment, "bcol", n_cols, d))
        d //= 2
    same = stack(own, *chips, after=(blocks,))
    other = swap(same, "brow", n_rows, 1)

    col_keep, *col_give = backward(segment, blocks, tile_rows, tile_cols, counts, n_rows, same)
    mine, *give = forward(same, other, blocks, tile_rows, tile_cols, counts, n_cols, col_give[0])
    col_got, d = [swap(x, "brow", n_rows, 1) for x in col_give], 2
    while d < n_rows:
        col_keep, x = split_sum(col_keep, col_got, mine)
        col_got = [swap(x, "brow", n_rows, d)]
        d *= 2
    total = z_sum(mine, [swap(x, "bcol", n_cols, d + 1) for d, x in reversed(list(enumerate(give)))])
    return last_sum(total, col_keep, col_got[0])


def solution(mesh):
    return jax.shard_map(
        body,
        mesh=mesh,
        in_specs=(
            P(None, ("brow", "bcol")),
            P(("brow", "bcol"), None),
            P(("brow", "bcol")),
            P(("brow", "bcol")),
            P("brow", "bcol"),
        ),
        out_specs=P(None, ("brow", "bcol")),
        check_vma=False,
    )
```

```python
import functools

import jax
import jax.numpy as jnp
import numpy as np
from jax import lax
from jax.experimental import pallas as pl
from jax.experimental.pallas import tpu as pltpu
from jax.sharding import PartitionSpec as P

TILE = 64
LANES = 128
HALF = TILE // 2
GROUP = LANES // HALF
STEPS = 32000.0
F32 = jnp.float32
BF16 = jnp.bfloat16
VMEM = pl.BlockSpec(memory_space=pltpu.VMEM)
ANY = pl.BlockSpec(memory_space=pl.ANY)
SMEM = pl.BlockSpec(memory_space=pltpu.SMEM)
PARAMS = pltpu.CompilerParams(vmem_limit_bytes=48 * 1024 * 1024)


def row_spread():
    source = lax.broadcasted_iota(jnp.int32, (LANES, LANES), 0)
    m = lax.broadcasted_iota(jnp.int32, (LANES, LANES), 1) % HALF
    blocks = [source == q * TILE + 2 * m + e for q in range(2) for e in range(2)]
    return jnp.concatenate([block.astype(F32) for block in blocks], axis=1).astype(BF16)


def row_fold():
    out = np.zeros((2, 2, 2, GROUP // 2, HALF, LANES), np.float32)
    for q in range(2):
        for e in range(2):
            for m in range(HALF):
                out[q, 0, e, :, m, q * TILE + 2 * m + e] = 1
                out[q, 1, 1 - e, :, m, q * TILE + 2 * m + e] = 1
    return jnp.asarray(out.reshape(4 * LANES, LANES), BF16)


def encode(values, out_ref):
    width, piece = values[0].shape[0], LANES * len(values)
    lane = lax.broadcasted_iota(jnp.int32, (width, LANES), 1)
    exponents = jnp.zeros((width, LANES), F32)
    for n, value in enumerate(values):
        top = jnp.max(jnp.abs(value), axis=1, keepdims=True)
        e = jnp.clip(jnp.ceil(jnp.log2(top)), -100.0, 100.0)
        exponents = jnp.where(lane == n, e, exponents)
        scaled = jnp.floor(value * (STEPS * jnp.exp2(-e)) + 0.5)
        out_ref[:, n * LANES : (n + 1) * LANES] = scaled.astype(jnp.int32).astype(jnp.int16)
    out_ref[:, piece:] = exponents.astype(jnp.int32).astype(jnp.int16)


def decode(ref):
    chunks = ref.shape[1] // LANES - 1
    exponents = ref[:, chunks * LANES :].astype(jnp.int32).astype(F32)
    scales = jnp.exp2(exponents) * (1.0 / STEPS)
    return [
        ref[:, n * LANES : (n + 1) * LANES].astype(jnp.int32).astype(F32) * scales[:, n : n + 1]
        for n in range(chunks)
    ]


def prep_kernel(tiles_ref, out_ref, wide):
    for b in range(tiles_ref.shape[0]):
        wide[b] = tiles_ref[b].astype(F32).reshape(HALF * 8, LANES)
        for s in range(8):
            out_ref[8 * b + s] = wide[b, pl.ds(s, HALF, stride=8), :].astype(BF16)


def prep(tiles):
    slots = tiles.shape[0]
    blocks = slots // 8
    view = tiles.reshape(blocks, 8, HALF, LANES).swapaxes(1, 2)
    return pl.pallas_call(
        prep_kernel,
        in_specs=[VMEM],
        out_specs=VMEM,
        out_shape=jax.ShapeDtypeStruct((slots, HALF, LANES), BF16),
        scratch_shapes=[pltpu.VMEM((blocks, HALF * 8, LANES), F32)],
        compiler_params=PARAMS,
        cost_estimate=pl.CostEstimate(flops=0, bytes_accessed=4 * tiles.size, transcendentals=0),
        name="prep_tiles",
    )(view)


def build_table(pieces, spread, table):
    width, piece = pieces[0].shape
    pairs = piece // LANES
    for n, ref in enumerate(pieces):
        rows = jnp.concatenate([ref[:, p * LANES : (p + 1) * LANES] for p in range(pairs)], axis=0)
        wide = jnp.dot(rows, spread, preferred_element_type=F32)
        wide = wide.reshape(pairs, width, 4 * LANES)
        for q in range(2):
            both = jnp.concatenate(
                [wide[:, :, (2 * q + e) * LANES : (2 * q + e + 1) * LANES] for e in range(2)], axis=1
            ).astype(BF16)
            for p in range(pairs):
                table[n * 2 * pairs + 2 * p + q] = both[p]


def backward_kernel(
    rows_ref, cols_ref, count_ref, tiles_ref, seg_ref, after_ref, keep_ref, *refs
):
    pieces = [seg_ref.at[n] for n in range(seg_ref.shape[0])]
    *give_refs, table, acc_a, acc_b = refs
    per_give = give_refs[0].shape[0]
    n_out = 2 * keep_ref.shape[0]
    width, piece = pieces[0].shape
    per_piece = piece // TILE
    slots = tiles_ref.shape[0]
    build_table(pieces, row_spread(), table)
    for acc in (acc_a, acc_b):
        acc[...] = jnp.zeros_like(acc)
    lane = lax.broadcasted_iota(jnp.int32, (2 * width, LANES), 1)
    masks = [(lane // HALF == s).astype(BF16) for s in range(GROUP)]
    low = lax.broadcasted_iota(jnp.int32, (width, LANES), 1) < TILE
    count = count_ref[0, 0]
    row_flip = lax.axis_index("bcol") * per_piece
    col_flip = lax.axis_index("brow") * per_piece
    spare = n_out * per_piece

    for g in range(slots // GROUP):
        at = [table[rows_ref[g * GROUP + s] ^ row_flip] * masks[s] for s in range(GROUP)]
        block = tiles_ref[g * GROUP : (g + 1) * GROUP].reshape(LANES, LANES)
        out = jnp.dot(jnp.concatenate(at, axis=0), block, preferred_element_type=F32)
        for s in range(GROUP):
            t = g * GROUP + s
            part = out[2 * width * s : 2 * width * (s + 1)]
            part = jnp.where(low, part[:width], part[width:])
            c = jnp.where(t < count, cols_ref[t] ^ col_flip, spare)
            acc = acc_a if s % 2 == 0 else acc_b
            acc[c] += part

    for n in range(n_out):
        h = n // 2
        dest = keep_ref.at[h] if n % 2 == 0 else give_refs[h // per_give].at[h % per_give]
        for p in range(per_piece // 2):
            at = n * per_piece + 2 * p
            a = acc_a[at] + acc_b[at]
            b = acc_a[at + 1] + acc_b[at + 1]
            dest[:, p * LANES : (p + 1) * LANES] = jnp.where(low, a, b) + pltpu.roll(
                jnp.where(low, b, a), TILE, 1
            )


def backward(segment, tiles, tile_rows, tile_cols, counts, n_out, after):
    n_in, width, piece = segment.shape
    per_piece = piece // TILE
    half = jax.ShapeDtypeStruct((n_out // 2, width, piece), F32)
    quarter = jax.ShapeDtypeStruct((n_out // 4, width, piece), F32)
    return pl.pallas_call(
        backward_kernel,
        in_specs=[SMEM] * 3 + [VMEM] * 2 + [ANY],
        out_specs=[VMEM] * 3,
        out_shape=[half, quarter, quarter],
        scratch_shapes=[
            pltpu.VMEM((n_in * per_piece, 2 * width, LANES), BF16),
            pltpu.VMEM((n_out * per_piece + 1, width, LANES), F32),
            pltpu.VMEM((n_out * per_piece + 1, width, LANES), F32),
        ],
        compiler_params=PARAMS,
        cost_estimate=pl.CostEstimate(
            flops=2 * tiles.size * 64, bytes_accessed=4 * tiles.size, transcendentals=0
        ),
        name="transpose_product",
    )(tile_rows, tile_cols, counts, tiles, segment, after)


def double_table(pieces, table):
    width, piece = pieces[0].shape
    low = lax.broadcasted_iota(jnp.int32, (width, LANES), 1) < TILE
    for n, ref in enumerate(pieces):
        for p in range(piece // LANES):
            pair = ref[:, p * LANES : (p + 1) * LANES].astype(F32)
            turned = pltpu.roll(pair, TILE, 1)
            at = (n * piece + p * LANES) // TILE
            table[at] = jnp.where(low, pair, turned)
            table[at + 1] = jnp.where(low, turned, pair)


def forward_kernel(
    rows_ref,
    cols_ref,
    count_ref,
    fold_ref,
    tiles_ref,
    same_ref,
    other_ref,
    after_ref,
    keep_ref,
    near_ref,
    give_ref,
    table,
    acc_a,
    acc_b,
):
    pieces = [ref.at[h] for h in range(same_ref.shape[0]) for ref in (same_ref, other_ref)]
    n_out = 2 * keep_ref.shape[0]
    width, piece = pieces[0].shape
    per_piece = piece // TILE
    slots = tiles_ref.shape[0]
    double_table(pieces, table)
    for acc in (acc_a, acc_b):
        acc[...] = jnp.zeros_like(acc)
    lane = lax.broadcasted_iota(jnp.int32, (width, LANES), 1)
    masks = [lane // HALF == s for s in range(GROUP)]
    wide_lane = lax.broadcasted_iota(jnp.int32, (LANES, LANES), 1)
    parity = [(wide_lane // TILE == e).astype(BF16) for e in range(2)]
    count = count_ref[0, 0]
    row_flip = lax.axis_index("bcol") * per_piece
    col_flip = lax.axis_index("brow") * per_piece
    spare = n_out * per_piece

    for g in range(slots // GROUP):
        at = [table[cols_ref[g * GROUP + s] ^ col_flip] for s in range(GROUP)]
        block = tiles_ref[g * GROUP : (g + 1) * GROUP].reshape(LANES, LANES)
        turned = jnp.concatenate([block[LANES // 2 :], block[: LANES // 2]], axis=0)
        out = lax.dot_general(
            jnp.concatenate(at, axis=0).astype(BF16),
            jnp.concatenate([block * parity[0], turned * parity[1]], axis=0),
            (((1,), (1,)), ((), ())),
            preferred_element_type=F32,
        )
        for s in range(GROUP):
            t = g * GROUP + s
            part = out[width * s : width * (s + 1)]
            r = jnp.where(t < count, rows_ref[t] ^ row_flip, spare)
            part = jnp.where(
                masks[s], part[:, :LANES], jnp.where(masks[(s + 2) % GROUP], part[:, LANES:], 0.0)
            )
            acc = acc_a if s < 2 else acc_b
            acc[r] += part

    fold = fold_ref[...]
    pairs = per_piece // 2
    for n in range(n_out):
        blocks = []
        for q in range(2):
            for acc in (acc_a, acc_b):
                both = acc[n * per_piece : (n + 1) * per_piece].reshape(pairs, 2 * width, LANES)
                blocks.append(both[:, q * width : (q + 1) * width, :].reshape(pairs * width, LANES))
        wide = jnp.concatenate(blocks, axis=1)
        first = wide.astype(BF16)
        rest = (wide - first.astype(F32)).astype(BF16)
        out = jnp.dot(first, fold, preferred_element_type=F32)
        out = out + jnp.dot(rest, fold, preferred_element_type=F32)
        parts = [out[p * width : (p + 1) * width] for p in range(pairs)]
        if n % 2 == 0:
            for p in range(pairs):
                keep_ref[n // 2, :, p * LANES : (p + 1) * LANES] = parts[p]
        else:
            encode(parts, near_ref.at[0] if n == 1 else give_ref.at[n // 2 - 1])


def forward(same, other, tiles, tile_rows, tile_cols, counts, n_out, after):
    n_chips, width, piece = same.shape
    per_piece = piece // TILE
    half = jax.ShapeDtypeStruct((n_out // 2, width, piece), F32)
    near = jax.ShapeDtypeStruct((1, width, piece + LANES), jnp.int16)
    rest = jax.ShapeDtypeStruct((n_out // 2 - 1, width, piece + LANES), jnp.int16)
    return pl.pallas_call(
        forward_kernel,
        in_specs=[SMEM] * 3 + [VMEM] * 4 + [ANY],
        out_specs=[VMEM] * 3,
        out_shape=[half, near, rest],
        scratch_shapes=[
            pltpu.VMEM((2 * n_chips * per_piece, width, LANES), F32),
            pltpu.VMEM((n_out * per_piece + 1, width, LANES), F32),
            pltpu.VMEM((n_out * per_piece + 1, width, LANES), F32),
        ],
        compiler_params=PARAMS,
        cost_estimate=pl.CostEstimate(
            flops=2 * tiles.size * 64, bytes_accessed=4 * tiles.size, transcendentals=0
        ),
        name="forward_product",
    )(tile_rows, tile_cols, counts, row_fold(), tiles, same, other, after)


def stack_kernel(n_after, *refs):
    out_ref, at = refs[-1], 0
    for ref in refs[: -1 - n_after]:
        if len(ref.shape) == 2:
            out_ref[at] = ref[...].astype(out_ref.dtype)
            at += 1
        else:
            out_ref[at : at + ref.shape[0]] = ref[...]
            at += ref.shape[0]


def stack(*parts, after=()):
    total = sum(x.shape[0] if x.ndim == 3 else 1 for x in parts)
    return pl.pallas_call(
        functools.partial(stack_kernel, len(after)),
        in_specs=[VMEM] * len(parts) + [ANY] * len(after),
        out_specs=VMEM,
        out_shape=jax.ShapeDtypeStruct((total,) + parts[0].shape[-2:], parts[0].dtype),
        compiler_params=PARAMS,
        name="stack_pieces",
    )(*parts, *after)


def pair_sum_kernel(keep_ref, *refs):
    n_chips = keep_ref.shape[0]
    gots, outs = refs[: 1 - n_chips], refs[1 - n_chips :]
    got = [ref.at[h] for ref in gots for h in range(ref.shape[0])]
    for h, out in enumerate(outs):
        out[...] = keep_ref[h + 1] + got[h + 1][...]


def pair_sum(keep, gots):
    parts, width, piece = keep.shape
    return pl.pallas_call(
        pair_sum_kernel,
        in_specs=[VMEM] * (1 + len(gots)),
        out_specs=[VMEM] * (parts - 1),
        out_shape=[jax.ShapeDtypeStruct((width, piece), F32)] * (parts - 1),
        compiler_params=PARAMS,
        name="core_pair_sum",
    )(keep, *gots)


def split_sum_kernel(keep_ref, got_ref, after_ref, next_keep, near_ref, *rest_refs):
    spans = [pl.ds(n, LANES) for n in range(0, keep_ref.shape[2], LANES)]
    for h in range(keep_ref.shape[0]):
        sums = [keep_ref[h, :, at] for at in spans]
        if h > 0:
            sums = [x + got for x, got in zip(sums, decode(got_ref.at[h - 1]))]
        if h % 2 == 0:
            for at, x in zip(spans, sums):
                next_keep[h // 2, :, at] = x
        elif h == 1:
            encode(sums, near_ref.at[0])
        else:
            encode(sums, rest_refs[0].at[h // 2 - 1])


def split_sum(keep, got, after):
    parts, width, piece = keep.shape
    shapes = [jax.ShapeDtypeStruct((parts // 2, width, piece), F32)]
    shapes += [
        jax.ShapeDtypeStruct((n, width, piece + LANES), got.dtype) for n in (1, parts // 2 - 1) if n
    ]
    keep, near, *rest = pl.pallas_call(
        split_sum_kernel,
        in_specs=[VMEM] * 2 + [ANY],
        out_specs=[VMEM] * len(shapes),
        out_shape=shapes,
        compiler_params=PARAMS,
        name="halving_sum",
    )(keep, got, after)
    return keep, near, rest


def part_sum_kernel(keep_ref, got_ref, brow_keep, brow_got, *refs):
    chips, out_ref = refs[:-1], refs[-1]
    for n, got in enumerate(decode(got_ref.at[0])):
        at = pl.ds(n * LANES, LANES)
        total = brow_keep[0, :, at] + brow_got[0, :, at]
        for ref in chips:
            total = total + ref[:, at]
        out_ref[:, at] = total + (keep_ref[0, :, at] + got)


def part_sum(keep, got, brow_keep, brow_got, chips):
    return pl.pallas_call(
        part_sum_kernel,
        in_specs=[VMEM] * (4 + len(chips)),
        out_specs=VMEM,
        out_shape=jax.ShapeDtypeStruct(keep.shape[1:], F32),
        compiler_params=PARAMS,
        name="part_sum",
    )(keep, got, brow_keep, brow_got, *chips)


def last_sum_kernel(total_ref, *refs):
    gots, out_ref = refs[:-1], refs[-1]
    parts = [decode(ref.at[0]) for ref in gots]
    for n in range(total_ref.shape[1] // LANES):
        at = pl.ds(n * LANES, LANES)
        total = total_ref[:, at]
        for part in parts:
            total = total + part[n]
        out_ref[:, at] = total


def last_sum(total, gots):
    return pl.pallas_call(
        last_sum_kernel,
        in_specs=[VMEM] * (1 + len(gots)),
        out_specs=VMEM,
        out_shape=jax.ShapeDtypeStruct(total.shape, F32),
        compiler_params=PARAMS,
        name="last_sum",
    )(total, *gots)


def take_kernel(x_ref, out_ref, wide_ref):
    out_ref[0] = x_ref[...]
    wide_ref[...] = x_ref[...].astype(F32)


def take(x):
    return pl.pallas_call(
        take_kernel,
        in_specs=[VMEM],
        out_specs=[VMEM] * 2,
        out_shape=[
            jax.ShapeDtypeStruct((1,) + x.shape, x.dtype),
            jax.ShapeDtypeStruct(x.shape, F32),
        ],
        compiler_params=PARAMS,
        name="take_piece",
    )(x)


def swap(x, axis, size, d):
    return lax.ppermute(x, axis, [(i, i ^ d) for i in range(size)])


def body(vectors, tiles, tile_rows, tile_cols, counts):
    n_rows = lax.axis_size("brow")
    n_cols = lax.axis_size("bcol")
    own, wide = take(vectors)
    chips = [swap(wide, "brow", n_rows, 2 * h) for h in range(1, n_rows // 2)]
    segment, d = own, 1
    while d < n_cols:
        segment = stack(segment, swap(segment if d > 1 else vectors[None], "bcol", n_cols, d))
        d *= 2
    blocks = prep(tiles)
    same = stack(own, *chips, after=(blocks,))
    other = swap(same, "brow", n_rows, 1)

    col_keep, *col_give = backward(segment, blocks, tile_rows, tile_cols, counts, n_rows, same)
    row_keep, near, rest = forward(same, other, blocks, tile_rows, tile_cols, counts, n_cols, col_give[0])
    col_got = [swap(x, "brow", n_rows, 1) for x in col_give]
    sums = pair_sum(col_keep, col_got)
    from_chips = [swap(x, "brow", n_rows, 2 * (h + 1)) for h, x in enumerate(sums)]
    d, later = 1, []
    while 2 * d < n_cols:
        row_got = swap(rest, "bcol", n_cols, d)
        later.append((near, d))
        row_keep, near, rest = split_sum(row_keep, row_got, sums[0])
        rest = rest[0] if rest else None
        d *= 2
    far = swap(near, "bcol", n_cols, d)
    total = part_sum(row_keep, far, col_keep, col_got[0], from_chips)
    return last_sum(total, [swap(x, "bcol", n_cols, d) for x, d in later])


def solution(mesh):
    return jax.shard_map(
        body,
        mesh=mesh,
        in_specs=(
            P(None, ("brow", "bcol")),
            P(("brow", "bcol"), None),
            P(("brow", "bcol")),
            P(("brow", "bcol")),
            P("brow", "bcol"),
        ),
        out_specs=P(None, ("brow", "bcol")),
        check_vma=False,
    )
```

```python
import functools

import jax
import jax.numpy as jnp
import numpy as np
from jax import lax
from jax.experimental import pallas as pl
from jax.experimental.pallas import tpu as pltpu
from jax.sharding import PartitionSpec as P

TILE = 64
LANES = 128
HALF = TILE // 2
GROUP = LANES // HALF
STEPS = 32000.0
F32 = jnp.float32
BF16 = jnp.bfloat16
VMEM = pl.BlockSpec(memory_space=pltpu.VMEM)
ANY = pl.BlockSpec(memory_space=pl.ANY)
SMEM = pl.BlockSpec(memory_space=pltpu.SMEM)
PARAMS = pltpu.CompilerParams(vmem_limit_bytes=48 * 1024 * 1024)


def row_spread():
    out = np.zeros((LANES, 2, 2, GROUP, HALF), np.float32)
    for q in range(2):
        for e in range(2):
            for m in range(HALF):
                out[q * TILE + 2 * m + e, q, e, :, m] = 1
    return jnp.asarray(out.reshape(LANES, 4 * LANES), BF16)


def row_fold():
    out = np.zeros((2, 2, 2, GROUP // 2, HALF, LANES), np.float32)
    for q in range(2):
        for e in range(2):
            for m in range(HALF):
                out[q, 0, e, :, m, q * TILE + 2 * m + e] = 1
                out[q, 1, 1 - e, :, m, q * TILE + 2 * m + e] = 1
    return jnp.asarray(out.reshape(4 * LANES, LANES), BF16)


def encode(values, out_ref):
    width, piece = values[0].shape[0], LANES * len(values)
    lane = lax.broadcasted_iota(jnp.int32, (width, LANES), 1)
    exponents = jnp.zeros((width, LANES), F32)
    for n, value in enumerate(values):
        top = jnp.max(jnp.abs(value), axis=1, keepdims=True)
        e = jnp.clip(jnp.ceil(jnp.log2(top)), -100.0, 100.0)
        exponents = jnp.where(lane == n, e, exponents)
        scaled = jnp.floor(value * (STEPS * jnp.exp2(-e)) + 0.5)
        out_ref[:, n * LANES : (n + 1) * LANES] = scaled.astype(jnp.int32).astype(jnp.int16)
    out_ref[:, piece:] = exponents.astype(jnp.int32).astype(jnp.int16)


def decode(ref):
    chunks = ref.shape[1] // LANES - 1
    exponents = ref[:, chunks * LANES :].astype(jnp.int32).astype(F32)
    scales = jnp.exp2(exponents) * (1.0 / STEPS)
    return [
        ref[:, n * LANES : (n + 1) * LANES].astype(jnp.int32).astype(F32) * scales[:, n : n + 1]
        for n in range(chunks)
    ]


def prep_kernel(tiles_ref, out_ref, wide):
    for b in range(tiles_ref.shape[0]):
        wide[b] = tiles_ref[b].astype(F32).reshape(HALF * 8, LANES)
        for s in range(8):
            out_ref[8 * b + s] = wide[b, pl.ds(s, HALF, stride=8), :].astype(BF16)


def prep(tiles):
    slots = tiles.shape[0]
    blocks = slots // 8
    view = tiles.reshape(blocks, 8, HALF, LANES).swapaxes(1, 2)
    return pl.pallas_call(
        prep_kernel,
        in_specs=[VMEM],
        out_specs=VMEM,
        out_shape=jax.ShapeDtypeStruct((slots, HALF, LANES), BF16),
        scratch_shapes=[pltpu.VMEM((blocks, HALF * 8, LANES), F32)],
        compiler_params=PARAMS,
        cost_estimate=pl.CostEstimate(flops=0, bytes_accessed=4 * tiles.size, transcendentals=0),
        name="prep_tiles",
    )(view)


def build_table(pieces, spread, table):
    width, piece = pieces[0].shape
    pairs = piece // LANES
    for n, ref in enumerate(pieces):
        rows = jnp.concatenate([ref[:, p * LANES : (p + 1) * LANES] for p in range(pairs)], axis=0)
        wide = jnp.dot(rows, spread, preferred_element_type=F32)
        wide = wide.reshape(pairs, width, 4 * LANES)
        for q in range(2):
            both = jnp.concatenate(
                [wide[:, :, (2 * q + e) * LANES : (2 * q + e + 1) * LANES] for e in range(2)], axis=1
            ).astype(BF16)
            for p in range(pairs):
                table[n * 2 * pairs + 2 * p + q] = both[p]


def backward_kernel(
    rows_ref, cols_ref, count_ref, spread_ref, tiles_ref, seg_ref, after_ref, keep_ref, *refs
):
    pieces = [seg_ref.at[n] for n in range(seg_ref.shape[0])]
    *give_refs, table, acc_a, acc_b = refs
    per_give = give_refs[0].shape[0]
    n_out = 2 * keep_ref.shape[0]
    width, piece = pieces[0].shape
    per_piece = piece // TILE
    slots = tiles_ref.shape[0]
    build_table(pieces, spread_ref[...], table)
    for acc in (acc_a, acc_b):
        acc[...] = jnp.zeros_like(acc)
    lane = lax.broadcasted_iota(jnp.int32, (2 * width, LANES), 1)
    masks = [(lane // HALF == s).astype(BF16) for s in range(GROUP)]
    low = lax.broadcasted_iota(jnp.int32, (width, LANES), 1) < TILE
    count = count_ref[0, 0]
    row_flip = lax.axis_index("bcol") * per_piece
    col_flip = lax.axis_index("brow") * per_piece
    spare = n_out * per_piece

    for g in range(slots // GROUP):
        at = [table[rows_ref[g * GROUP + s] ^ row_flip] * masks[s] for s in range(GROUP)]
        block = tiles_ref[g * GROUP : (g + 1) * GROUP].reshape(LANES, LANES)
        out = jnp.dot(jnp.concatenate(at, axis=0), block, preferred_element_type=F32)
        for s in range(GROUP):
            t = g * GROUP + s
            part = out[2 * width * s : 2 * width * (s + 1)]
            part = jnp.where(low, part[:width], part[width:])
            c = jnp.where(t < count, cols_ref[t] ^ col_flip, spare)
            acc = acc_a if s % 2 == 0 else acc_b
            acc[c] += part

    for n in range(n_out):
        h = n // 2
        dest = keep_ref.at[h] if n % 2 == 0 else give_refs[h // per_give].at[h % per_give]
        for p in range(per_piece // 2):
            at = n * per_piece + 2 * p
            a = acc_a[at] + acc_b[at]
            b = acc_a[at + 1] + acc_b[at + 1]
            dest[:, p * LANES : (p + 1) * LANES] = jnp.where(low, a, b) + pltpu.roll(
                jnp.where(low, b, a), TILE, 1
            )


def backward(segment, tiles, tile_rows, tile_cols, counts, n_out, after):
    n_in, width, piece = segment.shape
    per_piece = piece // TILE
    half = jax.ShapeDtypeStruct((n_out // 2, width, piece), F32)
    quarter = jax.ShapeDtypeStruct((n_out // 4, width, piece), F32)
    return pl.pallas_call(
        backward_kernel,
        in_specs=[SMEM] * 3 + [VMEM] * 3 + [ANY],
        out_specs=[VMEM] * 3,
        out_shape=[half, quarter, quarter],
        scratch_shapes=[
            pltpu.VMEM((n_in * per_piece, 2 * width, LANES), BF16),
            pltpu.VMEM((n_out * per_piece + 1, width, LANES), F32),
            pltpu.VMEM((n_out * per_piece + 1, width, LANES), F32),
        ],
        compiler_params=PARAMS,
        cost_estimate=pl.CostEstimate(
            flops=2 * tiles.size * 64, bytes_accessed=4 * tiles.size, transcendentals=0
        ),
        name="transpose_product",
    )(tile_rows, tile_cols, counts, row_spread(), tiles, segment, after)


def double_table(pieces, table):
    width, piece = pieces[0].shape
    low = lax.broadcasted_iota(jnp.int32, (width, LANES), 1) < TILE
    for n, ref in enumerate(pieces):
        for p in range(piece // LANES):
            pair = ref[:, p * LANES : (p + 1) * LANES].astype(F32)
            turned = pltpu.roll(pair, TILE, 1)
            at = (n * piece + p * LANES) // TILE
            table[at] = jnp.where(low, pair, turned)
            table[at + 1] = jnp.where(low, turned, pair)


def forward_kernel(
    rows_ref,
    cols_ref,
    count_ref,
    fold_ref,
    tiles_ref,
    same_ref,
    other_ref,
    after_ref,
    keep_ref,
    give_ref,
    table,
    acc_a,
    acc_b,
):
    pieces = [ref.at[h] for h in range(same_ref.shape[0]) for ref in (same_ref, other_ref)]
    n_out = 2 * keep_ref.shape[0]
    width, piece = pieces[0].shape
    per_piece = piece // TILE
    slots = tiles_ref.shape[0]
    double_table(pieces, table)
    for acc in (acc_a, acc_b):
        acc[...] = jnp.zeros_like(acc)
    lane = lax.broadcasted_iota(jnp.int32, (width, LANES), 1)
    masks = [lane // HALF == s for s in range(GROUP)]
    wide_lane = lax.broadcasted_iota(jnp.int32, (LANES, LANES), 1)
    parity = [(wide_lane // TILE == e).astype(BF16) for e in range(2)]
    count = count_ref[0, 0]
    row_flip = lax.axis_index("bcol") * per_piece
    col_flip = lax.axis_index("brow") * per_piece
    spare = n_out * per_piece

    for g in range(slots // GROUP):
        at = [table[cols_ref[g * GROUP + s] ^ col_flip] for s in range(GROUP)]
        block = tiles_ref[g * GROUP : (g + 1) * GROUP].reshape(LANES, LANES)
        turned = jnp.concatenate([block[LANES // 2 :], block[: LANES // 2]], axis=0)
        out = lax.dot_general(
            jnp.concatenate(at, axis=0).astype(BF16),
            jnp.concatenate([block * parity[0], turned * parity[1]], axis=0),
            (((1,), (1,)), ((), ())),
            preferred_element_type=F32,
        )
        for s in range(GROUP):
            t = g * GROUP + s
            part = out[width * s : width * (s + 1)]
            r = jnp.where(t < count, rows_ref[t] ^ row_flip, spare)
            part = jnp.where(
                masks[s], part[:, :LANES], jnp.where(masks[(s + 2) % GROUP], part[:, LANES:], 0.0)
            )
            acc = acc_a if s < 2 else acc_b
            acc[r] += part

    fold = fold_ref[...]
    pairs = per_piece // 2
    for n in range(n_out):
        blocks = []
        for q in range(2):
            for acc in (acc_a, acc_b):
                both = acc[n * per_piece : (n + 1) * per_piece].reshape(pairs, 2 * width, LANES)
                blocks.append(both[:, q * width : (q + 1) * width, :].reshape(pairs * width, LANES))
        wide = jnp.concatenate(blocks, axis=1)
        first = wide.astype(BF16)
        rest = (wide - first.astype(F32)).astype(BF16)
        out = jnp.dot(first, fold, preferred_element_type=F32)
        out = out + jnp.dot(rest, fold, preferred_element_type=F32)
        parts = [out[p * width : (p + 1) * width] for p in range(pairs)]
        if n % 2 == 0:
            for p in range(pairs):
                keep_ref[n // 2, :, p * LANES : (p + 1) * LANES] = parts[p]
        else:
            encode(parts, give_ref.at[n // 2])


def forward(same, other, tiles, tile_rows, tile_cols, counts, n_out, after):
    n_chips, width, piece = same.shape
    per_piece = piece // TILE
    half = jax.ShapeDtypeStruct((n_out // 2, width, piece), F32)
    coded = jax.ShapeDtypeStruct((n_out // 2, width, piece + LANES), jnp.int16)
    return pl.pallas_call(
        forward_kernel,
        in_specs=[SMEM] * 3 + [VMEM] * 4 + [ANY],
        out_specs=[VMEM] * 2,
        out_shape=[half, coded],
        scratch_shapes=[
            pltpu.VMEM((2 * n_chips * per_piece, width, LANES), F32),
            pltpu.VMEM((n_out * per_piece + 1, width, LANES), F32),
            pltpu.VMEM((n_out * per_piece + 1, width, LANES), F32),
        ],
        compiler_params=PARAMS,
        cost_estimate=pl.CostEstimate(
            flops=2 * tiles.size * 64, bytes_accessed=4 * tiles.size, transcendentals=0
        ),
        name="forward_product",
    )(tile_rows, tile_cols, counts, row_fold(), tiles, same, other, after)


def stack_kernel(n_after, *refs):
    out_ref, at = refs[-1], 0
    for ref in refs[: -1 - n_after]:
        if len(ref.shape) == 2:
            out_ref[at] = ref[...]
            at += 1
        else:
            out_ref[at : at + ref.shape[0]] = ref[...]
            at += ref.shape[0]


def stack(*parts, after=()):
    total = sum(x.shape[0] if x.ndim == 3 else 1 for x in parts)
    return pl.pallas_call(
        functools.partial(stack_kernel, len(after)),
        in_specs=[VMEM] * len(parts) + [ANY] * len(after),
        out_specs=VMEM,
        out_shape=jax.ShapeDtypeStruct((total,) + parts[0].shape[-2:], parts[0].dtype),
        compiler_params=PARAMS,
        name="stack_pieces",
    )(*parts, *after)


def pair_sum_kernel(keep_ref, *refs):
    n_chips = keep_ref.shape[0]
    gots, outs = refs[: 1 - n_chips], refs[1 - n_chips :]
    got = [ref.at[h] for ref in gots for h in range(ref.shape[0])]
    for h, out in enumerate(outs):
        out[...] = keep_ref[h + 1] + got[h + 1][...]


def pair_sum(keep, gots):
    parts, width, piece = keep.shape
    return pl.pallas_call(
        pair_sum_kernel,
        in_specs=[VMEM] * (1 + len(gots)),
        out_specs=[VMEM] * (parts - 1),
        out_shape=[jax.ShapeDtypeStruct((width, piece), F32)] * (parts - 1),
        compiler_params=PARAMS,
        name="core_pair_sum",
    )(keep, *gots)


def split_sum_kernel(keep_ref, got_ref, after_ref, next_keep, next_give):
    for h in range(next_keep.shape[0]):
        for n, got in enumerate(decode(got_ref.at[2 * h])):
            at = pl.ds(n * LANES, LANES)
            next_keep[h, :, at] = keep_ref[2 * h, :, at] + got
        sums = [
            keep_ref[2 * h + 1, :, n * LANES : (n + 1) * LANES] + got
            for n, got in enumerate(decode(got_ref.at[2 * h + 1]))
        ]
        encode(sums, next_give.at[h])


def split_sum(keep, got, after):
    parts, width, piece = keep.shape
    return pl.pallas_call(
        split_sum_kernel,
        in_specs=[VMEM] * 2 + [ANY],
        out_specs=[VMEM] * 2,
        out_shape=[
            jax.ShapeDtypeStruct((parts // 2, width, piece), F32),
            jax.ShapeDtypeStruct((parts // 2,) + got.shape[1:], got.dtype),
        ],
        compiler_params=PARAMS,
        name="halving_sum",
    )(keep, got, after)


def last_sum_kernel(*refs):
    chips, (brow_keep, brow_got, keep_ref, got_ref, out_ref) = refs[:-5], refs[-5:]
    for n, got in enumerate(decode(got_ref.at[0])):
        at = pl.ds(n * LANES, LANES)
        total = brow_keep[0, :, at] + brow_got[0, :, at]
        for ref in chips:
            total = total + ref[:, at]
        out_ref[:, at] = total + (keep_ref[0, :, at] + got)


def last_sum(keep, got, brow_keep, brow_got, chips):
    return pl.pallas_call(
        last_sum_kernel,
        in_specs=[VMEM] * (4 + len(chips)),
        out_specs=VMEM,
        out_shape=jax.ShapeDtypeStruct(keep.shape[1:], F32),
        compiler_params=PARAMS,
        name="last_sum",
    )(*chips, brow_keep, brow_got, keep, got)


def swap(x, axis, size, d):
    return lax.ppermute(x, axis, [(i, i ^ d) for i in range(size)])


def body(vectors, tiles, tile_rows, tile_cols, counts):
    n_rows = lax.axis_size("brow")
    n_cols = lax.axis_size("bcol")
    own = swap(vectors, "brow", n_rows, 0)[None]
    chips = [swap(vectors, "brow", n_rows, 2 * h) for h in range(1, n_rows // 2)]
    segment, d = own, 1
    while d < n_cols:
        segment = stack(segment, swap(segment if d > 1 else vectors[None], "bcol", n_cols, d))
        d *= 2
    blocks = prep(swap(tiles, "brow", n_rows, 0))
    same = stack(own, *chips, after=(blocks,))
    other = swap(same, "brow", n_rows, 1)

    col_keep, *col_give = backward(segment, blocks, tile_rows, tile_cols, counts, n_rows, same)
    row_keep, give = forward(same, other, blocks, tile_rows, tile_cols, counts, n_cols, col_give[0])
    col_got = [swap(x, "brow", n_rows, 1) for x in col_give]
    sums = pair_sum(col_keep, col_got)
    from_chips = [swap(x, "brow", n_rows, 2 * (h + 1)) for h, x in enumerate(sums)]
    row_got, d = swap(give, "bcol", n_cols, 1), 2
    while d < n_cols:
        row_keep, give = split_sum(row_keep, row_got, sums[0])
        row_got = swap(give, "bcol", n_cols, d)
        d *= 2
    return last_sum(row_keep, row_got, col_keep, col_got[0], from_chips)


def solution(mesh):
    return jax.shard_map(
        body,
        mesh=mesh,
        in_specs=(
            P(None, ("brow", "bcol")),
            P(("brow", "bcol"), None),
            P(("brow", "bcol")),
            P(("brow", "bcol")),
            P("brow", "bcol"),
        ),
        out_specs=P(None, ("brow", "bcol")),
        check_vma=False,
    )
```

```python
import functools

import jax
import jax.numpy as jnp
import numpy as np
from jax import lax
from jax.experimental import pallas as pl
from jax.experimental.pallas import tpu as pltpu
from jax.sharding import PartitionSpec as P

TILE = 64
LANES = 128
HALF = TILE // 2
GROUP = LANES // HALF
STEPS = 32000.0
F32 = jnp.float32
BF16 = jnp.bfloat16
VMEM = pl.BlockSpec(memory_space=pltpu.VMEM)
ANY = pl.BlockSpec(memory_space=pl.ANY)
SMEM = pl.BlockSpec(memory_space=pltpu.SMEM)
PARAMS = pltpu.CompilerParams(vmem_limit_bytes=48 * 1024 * 1024)


def row_spread():
    out = np.zeros((LANES, 2, 2, GROUP, HALF), np.float32)
    for q in range(2):
        for e in range(2):
            for m in range(HALF):
                out[q * TILE + 2 * m + e, q, e, :, m] = 1
    return jnp.asarray(out.reshape(LANES, 4 * LANES), BF16)


def row_fold():
    out = np.zeros((2, 2, 2, GROUP // 2, HALF, LANES), np.float32)
    for q in range(2):
        for e in range(2):
            for m in range(HALF):
                out[q, 0, e, :, m, q * TILE + 2 * m + e] = 1
                out[q, 1, 1 - e, :, m, q * TILE + 2 * m + e] = 1
    return jnp.asarray(out.reshape(4 * LANES, LANES), BF16)


def encode(values, out_ref):
    width, piece = values[0].shape[0], LANES * len(values)
    lane = lax.broadcasted_iota(jnp.int32, (width, LANES), 1)
    exponents = jnp.zeros((width, LANES), F32)
    for n, value in enumerate(values):
        top = jnp.max(jnp.abs(value), axis=1, keepdims=True)
        e = jnp.clip(jnp.ceil(jnp.log2(top)), -100.0, 100.0)
        exponents = jnp.where(lane == n, e, exponents)
        scaled = jnp.floor(value * (STEPS * jnp.exp2(-e)) + 0.5)
        out_ref[:, n * LANES : (n + 1) * LANES] = scaled.astype(jnp.int32).astype(jnp.int16)
    out_ref[:, piece:] = exponents.astype(jnp.int32).astype(jnp.int16)


def decode(ref):
    chunks = ref.shape[1] // LANES - 1
    exponents = ref[:, chunks * LANES :].astype(jnp.int32).astype(F32)
    scales = jnp.exp2(exponents) * (1.0 / STEPS)
    return [
        ref[:, n * LANES : (n + 1) * LANES].astype(jnp.int32).astype(F32) * scales[:, n : n + 1]
        for n in range(chunks)
    ]


def prep_kernel(tiles_ref, out_ref, wide):
    for b in range(tiles_ref.shape[0]):
        wide[b] = tiles_ref[b].astype(F32).reshape(HALF * 8, LANES)
        for s in range(8):
            out_ref[8 * b + s] = wide[b, pl.ds(s, HALF, stride=8), :].astype(BF16)


def prep(tiles):
    slots = tiles.shape[0]
    blocks = slots // 8
    view = tiles.reshape(blocks, 8, HALF, LANES).swapaxes(1, 2)
    return pl.pallas_call(
        prep_kernel,
        in_specs=[VMEM],
        out_specs=VMEM,
        out_shape=jax.ShapeDtypeStruct((slots, HALF, LANES), BF16),
        scratch_shapes=[pltpu.VMEM((blocks, HALF * 8, LANES), F32)],
        compiler_params=PARAMS,
        cost_estimate=pl.CostEstimate(flops=0, bytes_accessed=4 * tiles.size, transcendentals=0),
        name="prep_tiles",
    )(view)


def build_table(pieces, spread, table):
    width, piece = pieces[0].shape
    pairs = piece // LANES
    for n, ref in enumerate(pieces):
        rows = jnp.concatenate([ref[:, p * LANES : (p + 1) * LANES] for p in range(pairs)], axis=0)
        wide = jnp.dot(rows, spread, preferred_element_type=F32)
        wide = wide.reshape(pairs, width, 4 * LANES)
        for q in range(2):
            both = jnp.concatenate(
                [wide[:, :, (2 * q + e) * LANES : (2 * q + e + 1) * LANES] for e in range(2)], axis=1
            ).astype(BF16)
            for p in range(pairs):
                table[n * 2 * pairs + 2 * p + q] = both[p]


def backward_kernel(
    rows_ref, cols_ref, count_ref, spread_ref, tiles_ref, seg_ref, after_ref, keep_ref, *refs
):
    pieces = [seg_ref.at[n] for n in range(seg_ref.shape[0])]
    *give_refs, table, acc_a, acc_b = refs
    per_give = give_refs[0].shape[0]
    n_out = 2 * keep_ref.shape[0]
    width, piece = pieces[0].shape
    per_piece = piece // TILE
    slots = tiles_ref.shape[0]
    build_table(pieces, spread_ref[...], table)
    for acc in (acc_a, acc_b):
        acc[...] = jnp.zeros_like(acc)
    lane = lax.broadcasted_iota(jnp.int32, (2 * width, LANES), 1)
    masks = [(lane // HALF == s).astype(BF16) for s in range(GROUP)]
    low = lax.broadcasted_iota(jnp.int32, (width, LANES), 1) < TILE
    count = count_ref[0, 0]
    row_flip = lax.axis_index("bcol") * per_piece
    col_flip = lax.axis_index("brow") * per_piece
    spare = n_out * per_piece

    for g in range(slots // GROUP):
        at = [table[rows_ref[g * GROUP + s] ^ row_flip] * masks[s] for s in range(GROUP)]
        block = tiles_ref[g * GROUP : (g + 1) * GROUP].reshape(LANES, LANES)
        out = jnp.dot(jnp.concatenate(at, axis=0), block, preferred_element_type=F32)
        for s in range(GROUP):
            t = g * GROUP + s
            part = out[2 * width * s : 2 * width * (s + 1)]
            part = jnp.where(low, part[:width], part[width:])
            c = jnp.where(t < count, cols_ref[t] ^ col_flip, spare)
            acc = acc_a if s % 2 == 0 else acc_b
            acc[c] += part

    for n in range(n_out):
        h = n // 2
        kept = (n % 2 == 0) == (h == 0)
        dest = keep_ref.at[h] if kept else give_refs[h // per_give].at[h % per_give]
        for p in range(per_piece // 2):
            at = n * per_piece + 2 * p
            a = acc_a[at] + acc_b[at]
            b = acc_a[at + 1] + acc_b[at + 1]
            dest[:, p * LANES : (p + 1) * LANES] = jnp.where(low, a, b) + pltpu.roll(
                jnp.where(low, b, a), TILE, 1
            )


def backward(segment, tiles, tile_rows, tile_cols, counts, n_out, after):
    n_in, width, piece = segment.shape
    per_piece = piece // TILE
    half = jax.ShapeDtypeStruct((n_out // 2, width, piece), F32)
    quarter = jax.ShapeDtypeStruct((n_out // 4, width, piece), F32)
    return pl.pallas_call(
        backward_kernel,
        in_specs=[SMEM] * 3 + [VMEM] * 3 + [ANY],
        out_specs=[VMEM] * 3,
        out_shape=[half, quarter, quarter],
        scratch_shapes=[
            pltpu.VMEM((n_in * per_piece, 2 * width, LANES), BF16),
            pltpu.VMEM((n_out * per_piece + 1, width, LANES), F32),
            pltpu.VMEM((n_out * per_piece + 1, width, LANES), F32),
        ],
        compiler_params=PARAMS,
        cost_estimate=pl.CostEstimate(
            flops=2 * tiles.size * 64, bytes_accessed=4 * tiles.size, transcendentals=0
        ),
        name="transpose_product",
    )(tile_rows, tile_cols, counts, row_spread(), tiles, segment, after)


def double_table(pieces, table):
    width, piece = pieces[0].shape
    low = lax.broadcasted_iota(jnp.int32, (width, LANES), 1) < TILE
    for n, ref in enumerate(pieces):
        for p in range(piece // LANES):
            pair = ref[:, p * LANES : (p + 1) * LANES].astype(F32)
            turned = pltpu.roll(pair, TILE, 1)
            at = (n * piece + p * LANES) // TILE
            table[at] = jnp.where(low, pair, turned)
            table[at + 1] = jnp.where(low, turned, pair)


def forward_kernel(
    rows_ref,
    cols_ref,
    count_ref,
    fold_ref,
    tiles_ref,
    same_ref,
    other_ref,
    after_ref,
    keep_ref,
    give_ref,
    table,
    acc_a,
    acc_b,
):
    pieces = []
    for h in range(same_ref.shape[0]):
        pair = [same_ref.at[h], other_ref.at[h]]
        pieces += pair if h == 0 else pair[::-1]
    n_out = 2 * keep_ref.shape[0]
    width, piece = pieces[0].shape
    per_piece = piece // TILE
    slots = tiles_ref.shape[0]
    double_table(pieces, table)
    for acc in (acc_a, acc_b):
        acc[...] = jnp.zeros_like(acc)
    lane = lax.broadcasted_iota(jnp.int32, (width, LANES), 1)
    masks = [lane // HALF == s for s in range(GROUP)]
    wide_lane = lax.broadcasted_iota(jnp.int32, (LANES, LANES), 1)
    parity = [(wide_lane // TILE == e).astype(BF16) for e in range(2)]
    count = count_ref[0, 0]
    row_flip = lax.axis_index("bcol") * per_piece
    col_flip = lax.axis_index("brow") * per_piece
    spare = n_out * per_piece

    for g in range(slots // GROUP):
        at = [table[cols_ref[g * GROUP + s] ^ col_flip] for s in range(GROUP)]
        block = tiles_ref[g * GROUP : (g + 1) * GROUP].reshape(LANES, LANES)
        turned = jnp.concatenate([block[LANES // 2 :], block[: LANES // 2]], axis=0)
        out = lax.dot_general(
            jnp.concatenate(at, axis=0).astype(BF16),
            jnp.concatenate([block * parity[0], turned * parity[1]], axis=0),
            (((1,), (1,)), ((), ())),
            preferred_element_type=F32,
        )
        for s in range(GROUP):
            t = g * GROUP + s
            part = out[width * s : width * (s + 1)]
            r = jnp.where(t < count, rows_ref[t] ^ row_flip, spare)
            part = jnp.where(
                masks[s], part[:, :LANES], jnp.where(masks[(s + 2) % GROUP], part[:, LANES:], 0.0)
            )
            acc = acc_a if s < 2 else acc_b
            acc[r] += part

    fold = fold_ref[...]
    pairs = per_piece // 2
    for n in range(n_out):
        blocks = []
        for q in range(2):
            for acc in (acc_a, acc_b):
                both = acc[n * per_piece : (n + 1) * per_piece].reshape(pairs, 2 * width, LANES)
                blocks.append(both[:, q * width : (q + 1) * width, :].reshape(pairs * width, LANES))
        wide = jnp.concatenate(blocks, axis=1)
        first = wide.astype(BF16)
        rest = (wide - first.astype(F32)).astype(BF16)
        out = jnp.dot(first, fold, preferred_element_type=F32)
        out = out + jnp.dot(rest, fold, preferred_element_type=F32)
        parts = [out[p * width : (p + 1) * width] for p in range(pairs)]
        if n % 2 == 0:
            for p in range(pairs):
                keep_ref[n // 2, :, p * LANES : (p + 1) * LANES] = parts[p]
        else:
            encode(parts, give_ref.at[n // 2])


def forward(same, other, tiles, tile_rows, tile_cols, counts, n_out, after):
    n_chips, width, piece = same.shape
    per_piece = piece // TILE
    half = jax.ShapeDtypeStruct((n_out // 2, width, piece), F32)
    coded = jax.ShapeDtypeStruct((n_out // 2, width, piece + LANES), jnp.int16)
    return pl.pallas_call(
        forward_kernel,
        in_specs=[SMEM] * 3 + [VMEM] * 4 + [ANY],
        out_specs=[VMEM] * 2,
        out_shape=[half, coded],
        scratch_shapes=[
            pltpu.VMEM((2 * n_chips * per_piece, width, LANES), F32),
            pltpu.VMEM((n_out * per_piece + 1, width, LANES), F32),
            pltpu.VMEM((n_out * per_piece + 1, width, LANES), F32),
        ],
        compiler_params=PARAMS,
        cost_estimate=pl.CostEstimate(
            flops=2 * tiles.size * 64, bytes_accessed=4 * tiles.size, transcendentals=0
        ),
        name="forward_product",
    )(tile_rows, tile_cols, counts, row_fold(), tiles, same, other, after)


def stack_kernel(n_after, *refs):
    out_ref, at = refs[-1], 0
    for ref in refs[: -1 - n_after]:
        if len(ref.shape) == 2:
            out_ref[at] = ref[...]
            at += 1
        else:
            out_ref[at : at + ref.shape[0]] = ref[...]
            at += ref.shape[0]


def stack(*parts, after=()):
    total = sum(x.shape[0] if x.ndim == 3 else 1 for x in parts)
    return pl.pallas_call(
        functools.partial(stack_kernel, len(after)),
        in_specs=[VMEM] * len(parts) + [ANY] * len(after),
        out_specs=VMEM,
        out_shape=jax.ShapeDtypeStruct((total,) + parts[0].shape[-2:], parts[0].dtype),
        compiler_params=PARAMS,
        name="stack_pieces",
    )(*parts, *after)


def pair_sum_kernel(keep_ref, *refs):
    n_chips = keep_ref.shape[0]
    gots, outs = refs[: 1 - n_chips], refs[1 - n_chips :]
    got = [ref.at[h] for ref in gots for h in range(ref.shape[0])]
    for h, out in enumerate(outs):
        out[...] = keep_ref[h + 1] + got[h + 1][...]


def pair_sum(keep, gots):
    parts, width, piece = keep.shape
    return pl.pallas_call(
        pair_sum_kernel,
        in_specs=[VMEM] * (1 + len(gots)),
        out_specs=[VMEM] * (parts - 1),
        out_shape=[jax.ShapeDtypeStruct((width, piece), F32)] * (parts - 1),
        compiler_params=PARAMS,
        name="core_pair_sum",
    )(keep, *gots)


def split_sum_kernel(keep_ref, got_ref, after_ref, next_keep, next_give):
    for h in range(next_keep.shape[0]):
        for n, got in enumerate(decode(got_ref.at[2 * h])):
            at = pl.ds(n * LANES, LANES)
            next_keep[h, :, at] = keep_ref[2 * h, :, at] + got
        sums = [
            keep_ref[2 * h + 1, :, n * LANES : (n + 1) * LANES] + got
            for n, got in enumerate(decode(got_ref.at[2 * h + 1]))
        ]
        encode(sums, next_give.at[h])


def split_sum(keep, got, after):
    parts, width, piece = keep.shape
    return pl.pallas_call(
        split_sum_kernel,
        in_specs=[VMEM] * 2 + [ANY],
        out_specs=[VMEM] * 2,
        out_shape=[
            jax.ShapeDtypeStruct((parts // 2, width, piece), F32),
            jax.ShapeDtypeStruct((parts // 2,) + got.shape[1:], got.dtype),
        ],
        compiler_params=PARAMS,
        name="halving_sum",
    )(keep, got, after)


def last_sum_kernel(*refs):
    chips, (brow_keep, brow_got, keep_ref, got_ref, out_ref) = refs[:-5], refs[-5:]
    for n, got in enumerate(decode(got_ref.at[0])):
        at = pl.ds(n * LANES, LANES)
        total = brow_keep[0, :, at] + brow_got[0, :, at]
        for ref in chips:
            total = total + ref[:, at]
        out_ref[:, at] = total + (keep_ref[0, :, at] + got)


def last_sum(keep, got, brow_keep, brow_got, chips):
    return pl.pallas_call(
        last_sum_kernel,
        in_specs=[VMEM] * (4 + len(chips)),
        out_specs=VMEM,
        out_shape=jax.ShapeDtypeStruct(keep.shape[1:], F32),
        compiler_params=PARAMS,
        name="last_sum",
    )(*chips, brow_keep, brow_got, keep, got)


def swap(x, axis, size, d):
    return lax.ppermute(x, axis, [(i, i ^ d) for i in range(size)])


def body(vectors, tiles, tile_rows, tile_cols, counts):
    n_rows = lax.axis_size("brow")
    n_cols = lax.axis_size("bcol")
    own = stack(vectors)
    chips = [swap(vectors, "brow", n_rows, 2 * h + 1) for h in range(1, n_rows // 2)]
    segment, d = own, 1
    while d < n_cols:
        segment = stack(segment, swap(segment if d > 1 else vectors[None], "bcol", n_cols, d))
        d *= 2
    blocks = prep(tiles)
    same = stack(own, *chips, after=(blocks,))
    other = swap(same, "brow", n_rows, 1)

    col_keep, *col_give = backward(segment, blocks, tile_rows, tile_cols, counts, n_rows, same)
    row_keep, give = forward(same, other, blocks, tile_rows, tile_cols, counts, n_cols, col_give[0])
    col_got = [swap(x, "brow", n_rows, 1) for x in col_give]
    sums = pair_sum(col_keep, col_got)
    from_chips = [swap(x, "brow", n_rows, 2 * h + 3) for h, x in enumerate(sums)]
    row_got, d = swap(give, "bcol", n_cols, 1), 2
    while d < n_cols:
        row_keep, give = split_sum(row_keep, row_got, sums[0])
        row_got = swap(give, "bcol", n_cols, d)
        d *= 2
    return last_sum(row_keep, row_got, col_keep, col_got[0], from_chips)


def solution(mesh):
    return jax.shard_map(
        body,
        mesh=mesh,
        in_specs=(
            P(None, ("brow", "bcol")),
            P(("brow", "bcol"), None),
            P(("brow", "bcol")),
            P(("brow", "bcol")),
            P("brow", "bcol"),
        ),
        out_specs=P(None, ("brow", "bcol")),
        check_vma=False,
    )
```

```python
import functools

import jax
import jax.numpy as jnp
import numpy as np
from jax import lax
from jax.experimental import pallas as pl
from jax.experimental.pallas import tpu as pltpu
from jax.sharding import PartitionSpec as P

TILE = 64
LANES = 128
HALF = TILE // 2
GROUP = LANES // HALF
STEPS = 32000.0
F32 = jnp.float32
BF16 = jnp.bfloat16
VMEM = pl.BlockSpec(memory_space=pltpu.VMEM)
ANY = pl.BlockSpec(memory_space=pl.ANY)
SMEM = pl.BlockSpec(memory_space=pltpu.SMEM)
PARAMS = pltpu.CompilerParams(vmem_limit_bytes=48 * 1024 * 1024)


def row_spread():
    out = np.zeros((LANES, 2, 2, GROUP, HALF), np.float32)
    for q in range(2):
        for e in range(2):
            for m in range(HALF):
                out[q * TILE + 2 * m + e, q, e, :, m] = 1
    return jnp.asarray(out.reshape(LANES, 4 * LANES), BF16)


def row_fold():
    out = np.zeros((2, 2, 2, GROUP // 2, HALF, LANES), np.float32)
    for q in range(2):
        for e in range(2):
            for m in range(HALF):
                out[q, 0, e, :, m, q * TILE + 2 * m + e] = 1
                out[q, 1, 1 - e, :, m, q * TILE + 2 * m + e] = 1
    return jnp.asarray(out.reshape(4 * LANES, LANES), BF16)


def encode(values, out_ref):
    width, piece = values[0].shape[0], LANES * len(values)
    lane = lax.broadcasted_iota(jnp.int32, (width, LANES), 1)
    exponents = jnp.zeros((width, LANES), F32)
    for n, value in enumerate(values):
        top = jnp.max(jnp.abs(value), axis=1, keepdims=True)
        e = jnp.clip(jnp.ceil(jnp.log2(top)), -100.0, 100.0)
        exponents = jnp.where(lane == n, e, exponents)
        scaled = jnp.floor(value * (STEPS * jnp.exp2(-e)) + 0.5)
        out_ref[:, n * LANES : (n + 1) * LANES] = scaled.astype(jnp.int32).astype(jnp.int16)
    out_ref[:, piece:] = exponents.astype(jnp.int32).astype(jnp.int16)


def decode(ref):
    chunks = ref.shape[1] // LANES - 1
    exponents = ref[:, chunks * LANES :].astype(jnp.int32).astype(F32)
    scales = jnp.exp2(exponents) * (1.0 / STEPS)
    return [
        ref[:, n * LANES : (n + 1) * LANES].astype(jnp.int32).astype(F32) * scales[:, n : n + 1]
        for n in range(chunks)
    ]


def prep_kernel(tiles_ref, out_ref, wide):
    for b in range(tiles_ref.shape[0]):
        wide[b] = tiles_ref[b].astype(F32).reshape(HALF * 8, LANES)
        for s in range(8):
            out_ref[8 * b + s] = wide[b, pl.ds(s, HALF, stride=8), :].astype(BF16)


def prep(tiles):
    slots = tiles.shape[0]
    blocks = slots // 8
    view = tiles.reshape(blocks, 8, HALF, LANES).swapaxes(1, 2)
    return pl.pallas_call(
        prep_kernel,
        in_specs=[VMEM],
        out_specs=VMEM,
        out_shape=jax.ShapeDtypeStruct((slots, HALF, LANES), BF16),
        scratch_shapes=[pltpu.VMEM((blocks, HALF * 8, LANES), F32)],
        compiler_params=PARAMS,
        cost_estimate=pl.CostEstimate(flops=0, bytes_accessed=4 * tiles.size, transcendentals=0),
        name="prep_tiles",
    )(view)


def doubled(size):
    order, d = [0], size // 2
    while d > 0:
        order += [x ^ d for x in order]
        d //= 2
    return order


def build_table(pieces, spread, table):
    width, piece = pieces[0].shape
    pairs = piece // LANES
    for n, ref in enumerate(pieces):
        rows = jnp.concatenate([ref[:, p * LANES : (p + 1) * LANES] for p in range(pairs)], axis=0)
        wide = jnp.dot(rows, spread, preferred_element_type=F32)
        wide = wide.reshape(pairs, width, 4 * LANES)
        for q in range(2):
            both = jnp.concatenate(
                [wide[:, :, (2 * q + e) * LANES : (2 * q + e + 1) * LANES] for e in range(2)], axis=1
            ).astype(BF16)
            for p in range(pairs):
                table[n * 2 * pairs + 2 * p + q] = both[p]


def backward_kernel(
    rows_ref, cols_ref, count_ref, spread_ref, tiles_ref, seg_ref, after_ref, keep_ref, *refs
):
    pieces = [seg_ref.at[at] for at in np.argsort(doubled(seg_ref.shape[0]))]
    *give_refs, table, acc_a, acc_b = refs
    per_give = give_refs[0].shape[0]
    n_out = 2 * keep_ref.shape[0]
    width, piece = pieces[0].shape
    per_piece = piece // TILE
    slots = tiles_ref.shape[0]
    build_table(pieces, spread_ref[...], table)
    for acc in (acc_a, acc_b):
        acc[...] = jnp.zeros_like(acc)
    lane = lax.broadcasted_iota(jnp.int32, (2 * width, LANES), 1)
    masks = [(lane // HALF == s).astype(BF16) for s in range(GROUP)]
    low = lax.broadcasted_iota(jnp.int32, (width, LANES), 1) < TILE
    count = count_ref[0, 0]
    row_flip = lax.axis_index("bcol") * per_piece
    col_flip = lax.axis_index("brow") * per_piece
    spare = n_out * per_piece

    for g in range(slots // GROUP):
        at = [table[rows_ref[g * GROUP + s] ^ row_flip] * masks[s] for s in range(GROUP)]
        block = tiles_ref[g * GROUP : (g + 1) * GROUP].reshape(LANES, LANES)
        out = jnp.dot(jnp.concatenate(at, axis=0), block, preferred_element_type=F32)
        for s in range(GROUP):
            t = g * GROUP + s
            part = out[2 * width * s : 2 * width * (s + 1)]
            part = jnp.where(low, part[:width], part[width:])
            c = jnp.where(t < count, cols_ref[t] ^ col_flip, spare)
            acc = acc_a if s % 2 == 0 else acc_b
            acc[c] += part

    for n in range(n_out):
        h = n // 2
        kept = (n % 2 == 0) == (h == 0)
        dest = keep_ref.at[h] if kept else give_refs[h // per_give].at[h % per_give]
        for p in range(per_piece // 2):
            at = n * per_piece + 2 * p
            a = acc_a[at] + acc_b[at]
            b = acc_a[at + 1] + acc_b[at + 1]
            dest[:, p * LANES : (p + 1) * LANES] = jnp.where(low, a, b) + pltpu.roll(
                jnp.where(low, b, a), TILE, 1
            )


def backward(segment, tiles, tile_rows, tile_cols, counts, n_out, after):
    n_in, width, piece = segment.shape
    per_piece = piece // TILE
    half = jax.ShapeDtypeStruct((n_out // 2, width, piece), F32)
    quarter = jax.ShapeDtypeStruct((n_out // 4, width, piece), F32)
    return pl.pallas_call(
        backward_kernel,
        in_specs=[SMEM] * 3 + [VMEM] * 3 + [ANY],
        out_specs=[VMEM] * 3,
        out_shape=[half, quarter, quarter],
        scratch_shapes=[
            pltpu.VMEM((n_in * per_piece, 2 * width, LANES), BF16),
            pltpu.VMEM((n_out * per_piece + 1, width, LANES), F32),
            pltpu.VMEM((n_out * per_piece + 1, width, LANES), F32),
        ],
        compiler_params=PARAMS,
        cost_estimate=pl.CostEstimate(
            flops=2 * tiles.size * 64, bytes_accessed=4 * tiles.size, transcendentals=0
        ),
        name="transpose_product",
    )(tile_rows, tile_cols, counts, row_spread(), tiles, segment, after)


def double_table(pieces, table):
    width, piece = pieces[0].shape
    low = lax.broadcasted_iota(jnp.int32, (width, LANES), 1) < TILE
    for n, ref in enumerate(pieces):
        for p in range(piece // LANES):
            pair = ref[:, p * LANES : (p + 1) * LANES].astype(F32)
            turned = pltpu.roll(pair, TILE, 1)
            at = (n * piece + p * LANES) // TILE
            table[at] = jnp.where(low, pair, turned)
            table[at + 1] = jnp.where(low, turned, pair)


def forward_kernel(
    rows_ref,
    cols_ref,
    count_ref,
    fold_ref,
    tiles_ref,
    same_ref,
    other_ref,
    after_ref,
    keep_ref,
    give_ref,
    table,
    acc_a,
    acc_b,
):
    pieces = []
    for h in range(same_ref.shape[0]):
        pair = [same_ref.at[h], other_ref.at[h]]
        pieces += pair if h == 0 else pair[::-1]
    n_out = 2 * keep_ref.shape[0]
    width, piece = pieces[0].shape
    per_piece = piece // TILE
    slots = tiles_ref.shape[0]
    double_table(pieces, table)
    for acc in (acc_a, acc_b):
        acc[...] = jnp.zeros_like(acc)
    lane = lax.broadcasted_iota(jnp.int32, (width, LANES), 1)
    masks = [lane // HALF == s for s in range(GROUP)]
    wide_lane = lax.broadcasted_iota(jnp.int32, (LANES, LANES), 1)
    parity = [(wide_lane // TILE == e).astype(BF16) for e in range(2)]
    count = count_ref[0, 0]
    row_flip = lax.axis_index("bcol") * per_piece
    col_flip = lax.axis_index("brow") * per_piece
    spare = n_out * per_piece

    for g in range(slots // GROUP):
        at = [table[cols_ref[g * GROUP + s] ^ col_flip] for s in range(GROUP)]
        block = tiles_ref[g * GROUP : (g + 1) * GROUP].reshape(LANES, LANES)
        turned = jnp.concatenate([block[LANES // 2 :], block[: LANES // 2]], axis=0)
        out = lax.dot_general(
            jnp.concatenate(at, axis=0).astype(BF16),
            jnp.concatenate([block * parity[0], turned * parity[1]], axis=0),
            (((1,), (1,)), ((), ())),
            preferred_element_type=F32,
        )
        for s in range(GROUP):
            t = g * GROUP + s
            part = out[width * s : width * (s + 1)]
            r = jnp.where(t < count, rows_ref[t] ^ row_flip, spare)
            part = jnp.where(
                masks[s], part[:, :LANES], jnp.where(masks[(s + 2) % GROUP], part[:, LANES:], 0.0)
            )
            acc = acc_a if s < 2 else acc_b
            acc[r] += part

    fold = fold_ref[...]
    pairs = per_piece // 2
    for n in range(n_out):
        blocks = []
        for q in range(2):
            for acc in (acc_a, acc_b):
                both = acc[n * per_piece : (n + 1) * per_piece].reshape(pairs, 2 * width, LANES)
                blocks.append(both[:, q * width : (q + 1) * width, :].reshape(pairs * width, LANES))
        wide = jnp.concatenate(blocks, axis=1)
        first = wide.astype(BF16)
        rest = (wide - first.astype(F32)).astype(BF16)
        out = jnp.dot(first, fold, preferred_element_type=F32)
        out = out + jnp.dot(rest, fold, preferred_element_type=F32)
        parts = [out[p * width : (p + 1) * width] for p in range(pairs)]
        if n % 2 == 0:
            for p in range(pairs):
                keep_ref[n // 2, :, p * LANES : (p + 1) * LANES] = parts[p]
        else:
            encode(parts, give_ref.at[n // 2])


def forward(same, other, tiles, tile_rows, tile_cols, counts, n_out, after):
    n_chips, width, piece = same.shape
    per_piece = piece // TILE
    half = jax.ShapeDtypeStruct((n_out // 2, width, piece), F32)
    coded = jax.ShapeDtypeStruct((n_out // 2, width, piece + LANES), jnp.int16)
    return pl.pallas_call(
        forward_kernel,
        in_specs=[SMEM] * 3 + [VMEM] * 4 + [ANY],
        out_specs=[VMEM] * 2,
        out_shape=[half, coded],
        scratch_shapes=[
            pltpu.VMEM((2 * n_chips * per_piece, width, LANES), F32),
            pltpu.VMEM((n_out * per_piece + 1, width, LANES), F32),
            pltpu.VMEM((n_out * per_piece + 1, width, LANES), F32),
        ],
        compiler_params=PARAMS,
        cost_estimate=pl.CostEstimate(
            flops=2 * tiles.size * 64, bytes_accessed=4 * tiles.size, transcendentals=0
        ),
        name="forward_product",
    )(tile_rows, tile_cols, counts, row_fold(), tiles, same, other, after)


def stack_kernel(n_after, *refs):
    out_ref, at = refs[-1], 0
    for ref in refs[: -1 - n_after]:
        if len(ref.shape) == 2:
            out_ref[at] = ref[...]
            at += 1
        else:
            out_ref[at : at + ref.shape[0]] = ref[...]
            at += ref.shape[0]


def stack(*parts, after=()):
    total = sum(x.shape[0] if x.ndim == 3 else 1 for x in parts)
    return pl.pallas_call(
        functools.partial(stack_kernel, len(after)),
        in_specs=[VMEM] * len(parts) + [ANY] * len(after),
        out_specs=VMEM,
        out_shape=jax.ShapeDtypeStruct((total,) + parts[0].shape[-2:], parts[0].dtype),
        compiler_params=PARAMS,
        name="stack_pieces",
    )(*parts, *after)


def pair_sum_kernel(keep_ref, *refs):
    n_chips = keep_ref.shape[0]
    gots, outs = refs[: 1 - n_chips], refs[1 - n_chips :]
    got = [ref.at[h] for ref in gots for h in range(ref.shape[0])]
    for h, out in enumerate(outs):
        out[...] = keep_ref[h + 1] + got[h + 1][...]


def pair_sum(keep, gots):
    parts, width, piece = keep.shape
    return pl.pallas_call(
        pair_sum_kernel,
        in_specs=[VMEM] * (1 + len(gots)),
        out_specs=[VMEM] * (parts - 1),
        out_shape=[jax.ShapeDtypeStruct((width, piece), F32)] * (parts - 1),
        compiler_params=PARAMS,
        name="core_pair_sum",
    )(keep, *gots)


def split_sum_kernel(keep_ref, got_ref, after_ref, next_keep, next_give):
    for h in range(next_keep.shape[0]):
        for n, got in enumerate(decode(got_ref.at[2 * h])):
            at = pl.ds(n * LANES, LANES)
            next_keep[h, :, at] = keep_ref[2 * h, :, at] + got
        sums = [
            keep_ref[2 * h + 1, :, n * LANES : (n + 1) * LANES] + got
            for n, got in enumerate(decode(got_ref.at[2 * h + 1]))
        ]
        encode(sums, next_give.at[h])


def split_sum(keep, got, after):
    parts, width, piece = keep.shape
    return pl.pallas_call(
        split_sum_kernel,
        in_specs=[VMEM] * 2 + [ANY],
        out_specs=[VMEM] * 2,
        out_shape=[
            jax.ShapeDtypeStruct((parts // 2, width, piece), F32),
            jax.ShapeDtypeStruct((parts // 2,) + got.shape[1:], got.dtype),
        ],
        compiler_params=PARAMS,
        name="halving_sum",
    )(keep, got, after)


def last_sum_kernel(*refs):
    chips, (brow_keep, brow_got, keep_ref, got_ref, out_ref) = refs[:-5], refs[-5:]
    for n, got in enumerate(decode(got_ref.at[0])):
        at = pl.ds(n * LANES, LANES)
        total = brow_keep[0, :, at] + brow_got[0, :, at]
        for ref in chips:
            total = total + ref[:, at]
        out_ref[:, at] = total + (keep_ref[0, :, at] + got)


def last_sum(keep, got, brow_keep, brow_got, chips):
    return pl.pallas_call(
        last_sum_kernel,
        in_specs=[VMEM] * (4 + len(chips)),
        out_specs=VMEM,
        out_shape=jax.ShapeDtypeStruct(keep.shape[1:], F32),
        compiler_params=PARAMS,
        name="last_sum",
    )(*chips, brow_keep, brow_got, keep, got)


def swap(x, axis, size, d):
    return lax.ppermute(x, axis, [(i, i ^ d) for i in range(size)])


def body(vectors, tiles, tile_rows, tile_cols, counts):
    n_rows = lax.axis_size("brow")
    n_cols = lax.axis_size("bcol")
    own = stack(vectors)
    chips = [swap(vectors, "brow", n_rows, 2 * h + 1) for h in range(1, n_rows // 2)]
    segment, d = own, n_cols // 2
    while d > 0:
        first = d == n_cols // 2
        segment = stack(segment, swap(vectors[None] if first else segment, "bcol", n_cols, d))
        d //= 2
    blocks = prep(tiles)
    same = stack(own, *chips, after=(blocks,))
    other = swap(same, "brow", n_rows, 1)

    col_keep, *col_give = backward(segment, blocks, tile_rows, tile_cols, counts, n_rows, same)
    row_keep, give = forward(same, other, blocks, tile_rows, tile_cols, counts, n_cols, col_give[0])
    col_got = [swap(x, "brow", n_rows, 1) for x in col_give]
    sums = pair_sum(col_keep, col_got)
    from_chips = [swap(x, "brow", n_rows, 2 * h + 3) for h, x in enumerate(sums)]
    row_got, d = swap(give, "bcol", n_cols, 1), 2
    while d < n_cols:
        row_keep, give = split_sum(row_keep, row_got, sums[0])
        row_got = swap(give, "bcol", n_cols, d)
        d *= 2
    return last_sum(row_keep, row_got, col_keep, col_got[0], from_chips)


def solution(mesh):
    return jax.shard_map(
        body,
        mesh=mesh,
        in_specs=(
            P(None, ("brow", "bcol")),
            P(("brow", "bcol"), None),
            P(("brow", "bcol")),
            P(("brow", "bcol")),
            P("brow", "bcol"),
        ),
        out_specs=P(None, ("brow", "bcol")),
        check_vma=False,
    )
```

```python
import functools

import jax
import jax.numpy as jnp
import numpy as np
from jax import lax
from jax.experimental import pallas as pl
from jax.experimental.pallas import tpu as pltpu
from jax.sharding import PartitionSpec as P

TILE = 64
LANES = 128
HALF = TILE // 2
GROUP = LANES // HALF
STEPS = 32000.0
F32 = jnp.float32
BF16 = jnp.bfloat16
VMEM = pl.BlockSpec(memory_space=pltpu.VMEM)
ANY = pl.BlockSpec(memory_space=pl.ANY)
SMEM = pl.BlockSpec(memory_space=pltpu.SMEM)
PARAMS = pltpu.CompilerParams(vmem_limit_bytes=48 * 1024 * 1024)


def row_spread():
    source = lax.broadcasted_iota(jnp.int32, (LANES, LANES), 0)
    m = lax.broadcasted_iota(jnp.int32, (LANES, LANES), 1) % HALF
    blocks = [source == q * TILE + 2 * m + e for q in range(2) for e in range(2)]
    return jnp.concatenate([block.astype(F32) for block in blocks], axis=1).astype(BF16)


def row_fold():
    out = np.zeros((2, 2, 2, GROUP // 2, HALF, LANES), np.float32)
    for q in range(2):
        for e in range(2):
            for m in range(HALF):
                out[q, 0, e, :, m, q * TILE + 2 * m + e] = 1
                out[q, 1, 1 - e, :, m, q * TILE + 2 * m + e] = 1
    return jnp.asarray(out.reshape(4 * LANES, LANES), BF16)


def encode(values, out_ref):
    width, piece = values[0].shape[0], LANES * len(values)
    lane = lax.broadcasted_iota(jnp.int32, (width, LANES), 1)
    exponents = jnp.zeros((width, LANES), F32)
    for n, value in enumerate(values):
        top = jnp.max(jnp.abs(value), axis=1, keepdims=True)
        e = jnp.clip(jnp.ceil(jnp.log2(top)), -100.0, 100.0)
        exponents = jnp.where(lane == n, e, exponents)
        scaled = jnp.floor(value * (STEPS * jnp.exp2(-e)) + 0.5)
        out_ref[:, n * LANES : (n + 1) * LANES] = scaled.astype(jnp.int32).astype(jnp.int16)
    out_ref[:, piece:] = exponents.astype(jnp.int32).astype(jnp.int16)


def decode(ref):
    chunks = ref.shape[1] // LANES - 1
    exponents = ref[:, chunks * LANES :].astype(jnp.int32).astype(F32)
    scales = jnp.exp2(exponents) * (1.0 / STEPS)
    return [
        ref[:, n * LANES : (n + 1) * LANES].astype(jnp.int32).astype(F32) * scales[:, n : n + 1]
        for n in range(chunks)
    ]


def prep_kernel(tiles_ref, out_ref, wide):
    for b in range(tiles_ref.shape[0]):
        wide[b] = tiles_ref[b].astype(F32).reshape(HALF * 8, LANES)
        for s in range(8):
            out_ref[8 * b + s] = wide[b, pl.ds(s, HALF, stride=8), :].astype(BF16)


def prep(tiles):
    slots = tiles.shape[0]
    blocks = slots // 8
    view = tiles.reshape(blocks, 8, HALF, LANES).swapaxes(1, 2)
    return pl.pallas_call(
        prep_kernel,
        in_specs=[VMEM],
        out_specs=VMEM,
        out_shape=jax.ShapeDtypeStruct((slots, HALF, LANES), BF16),
        scratch_shapes=[pltpu.VMEM((blocks, HALF * 8, LANES), F32)],
        compiler_params=PARAMS,
        cost_estimate=pl.CostEstimate(flops=0, bytes_accessed=4 * tiles.size, transcendentals=0),
        name="prep_tiles",
    )(view)


def doubled(size):
    order, d = [0], size // 2
    while d > 0:
        order += [x ^ d for x in order]
        d //= 2
    return order


def build_table(pieces, spread, table):
    width, piece = pieces[0].shape
    pairs = piece // LANES
    for n, ref in enumerate(pieces):
        rows = jnp.concatenate([ref[:, p * LANES : (p + 1) * LANES] for p in range(pairs)], axis=0)
        wide = jnp.dot(rows, spread, preferred_element_type=F32)
        wide = wide.reshape(pairs, width, 4 * LANES)
        for q in range(2):
            both = jnp.concatenate(
                [wide[:, :, (2 * q + e) * LANES : (2 * q + e + 1) * LANES] for e in range(2)], axis=1
            ).astype(BF16)
            for p in range(pairs):
                table[n * 2 * pairs + 2 * p + q] = both[p]


def backward_kernel(
    rows_ref, cols_ref, count_ref, tiles_ref, seg_ref, after_ref, keep_ref, *refs
):
    pieces = [seg_ref.at[at] for at in np.argsort(doubled(seg_ref.shape[0]))]
    *give_refs, table, acc_a, acc_b = refs
    per_give = give_refs[0].shape[0]
    n_out = 2 * keep_ref.shape[0]
    width, piece = pieces[0].shape
    per_piece = piece // TILE
    slots = tiles_ref.shape[0]
    build_table(pieces, row_spread(), table)
    for acc in (acc_a, acc_b):
        acc[...] = jnp.zeros_like(acc)
    lane = lax.broadcasted_iota(jnp.int32, (2 * width, LANES), 1)
    masks = [(lane // HALF == s).astype(BF16) for s in range(GROUP)]
    low = lax.broadcasted_iota(jnp.int32, (width, LANES), 1) < TILE
    count = count_ref[0, 0]
    row_flip = lax.axis_index("bcol") * per_piece
    col_flip = lax.axis_index("brow") * per_piece
    spare = n_out * per_piece

    for g in range(slots // GROUP):
        at = [table[rows_ref[g * GROUP + s] ^ row_flip] * masks[s] for s in range(GROUP)]
        block = tiles_ref[g * GROUP : (g + 1) * GROUP].reshape(LANES, LANES)
        out = jnp.dot(jnp.concatenate(at, axis=0), block, preferred_element_type=F32)
        for s in range(GROUP):
            t = g * GROUP + s
            part = out[2 * width * s : 2 * width * (s + 1)]
            part = jnp.where(low, part[:width], part[width:])
            c = jnp.where(t < count, cols_ref[t] ^ col_flip, spare)
            acc = acc_a if s % 2 == 0 else acc_b
            acc[c] += part

    for n in range(n_out):
        h = n // 2
        kept = (n % 2 == 0) == (h == 0)
        dest = keep_ref.at[h] if kept else give_refs[h // per_give].at[h % per_give]
        for p in range(per_piece // 2):
            at = n * per_piece + 2 * p
            a = acc_a[at] + acc_b[at]
            b = acc_a[at + 1] + acc_b[at + 1]
            dest[:, p * LANES : (p + 1) * LANES] = jnp.where(low, a, b) + pltpu.roll(
                jnp.where(low, b, a), TILE, 1
            )


def backward(segment, tiles, tile_rows, tile_cols, counts, n_out, after):
    n_in, width, piece = segment.shape
    per_piece = piece // TILE
    half = jax.ShapeDtypeStruct((n_out // 2, width, piece), F32)
    quarter = jax.ShapeDtypeStruct((n_out // 4, width, piece), F32)
    return pl.pallas_call(
        backward_kernel,
        in_specs=[SMEM] * 3 + [VMEM] * 2 + [ANY],
        out_specs=[VMEM] * 3,
        out_shape=[half, quarter, quarter],
        scratch_shapes=[
            pltpu.VMEM((n_in * per_piece, 2 * width, LANES), BF16),
            pltpu.VMEM((n_out * per_piece + 1, width, LANES), F32),
            pltpu.VMEM((n_out * per_piece + 1, width, LANES), F32),
        ],
        compiler_params=PARAMS,
        cost_estimate=pl.CostEstimate(
            flops=2 * tiles.size * 64, bytes_accessed=4 * tiles.size, transcendentals=0
        ),
        name="transpose_product",
    )(tile_rows, tile_cols, counts, tiles, segment, after)


def double_table(pieces, table):
    width, piece = pieces[0].shape
    low = lax.broadcasted_iota(jnp.int32, (width, LANES), 1) < TILE
    for n, ref in enumerate(pieces):
        for p in range(piece // LANES):
            pair = ref[:, p * LANES : (p + 1) * LANES].astype(F32)
            turned = pltpu.roll(pair, TILE, 1)
            at = (n * piece + p * LANES) // TILE
            table[at] = jnp.where(low, pair, turned)
            table[at + 1] = jnp.where(low, turned, pair)


def forward_kernel(
    rows_ref,
    cols_ref,
    count_ref,
    fold_ref,
    tiles_ref,
    same_ref,
    other_ref,
    after_ref,
    keep_ref,
    near_ref,
    give_ref,
    table,
    acc_a,
    acc_b,
):
    pieces = []
    for h in range(same_ref.shape[0]):
        pair = [same_ref.at[h], other_ref.at[h]]
        pieces += pair if h == 0 else pair[::-1]
    n_out = 2 * keep_ref.shape[0]
    width, piece = pieces[0].shape
    per_piece = piece // TILE
    slots = tiles_ref.shape[0]
    double_table(pieces, table)
    for acc in (acc_a, acc_b):
        acc[...] = jnp.zeros_like(acc)
    lane = lax.broadcasted_iota(jnp.int32, (width, LANES), 1)
    masks = [lane // HALF == s for s in range(GROUP)]
    wide_lane = lax.broadcasted_iota(jnp.int32, (LANES, LANES), 1)
    parity = [(wide_lane // TILE == e).astype(BF16) for e in range(2)]
    count = count_ref[0, 0]
    row_flip = lax.axis_index("bcol") * per_piece
    col_flip = lax.axis_index("brow") * per_piece
    spare = n_out * per_piece

    for g in range(slots // GROUP):
        at = [table[cols_ref[g * GROUP + s] ^ col_flip] for s in range(GROUP)]
        block = tiles_ref[g * GROUP : (g + 1) * GROUP].reshape(LANES, LANES)
        turned = jnp.concatenate([block[LANES // 2 :], block[: LANES // 2]], axis=0)
        out = lax.dot_general(
            jnp.concatenate(at, axis=0).astype(BF16),
            jnp.concatenate([block * parity[0], turned * parity[1]], axis=0),
            (((1,), (1,)), ((), ())),
            preferred_element_type=F32,
        )
        for s in range(GROUP):
            t = g * GROUP + s
            part = out[width * s : width * (s + 1)]
            r = jnp.where(t < count, rows_ref[t] ^ row_flip, spare)
            part = jnp.where(
                masks[s], part[:, :LANES], jnp.where(masks[(s + 2) % GROUP], part[:, LANES:], 0.0)
            )
            acc = acc_a if s < 2 else acc_b
            acc[r] += part

    fold = fold_ref[...]
    pairs = per_piece // 2
    for n in range(n_out):
        blocks = []
        for q in range(2):
            for acc in (acc_a, acc_b):
                both = acc[n * per_piece : (n + 1) * per_piece].reshape(pairs, 2 * width, LANES)
                blocks.append(both[:, q * width : (q + 1) * width, :].reshape(pairs * width, LANES))
        wide = jnp.concatenate(blocks, axis=1)
        first = wide.astype(BF16)
        rest = (wide - first.astype(F32)).astype(BF16)
        out = jnp.dot(first, fold, preferred_element_type=F32)
        out = out + jnp.dot(rest, fold, preferred_element_type=F32)
        parts = [out[p * width : (p + 1) * width] for p in range(pairs)]
        if n % 2 == 0:
            for p in range(pairs):
                keep_ref[n // 2, :, p * LANES : (p + 1) * LANES] = parts[p]
        else:
            encode(parts, near_ref.at[0] if n == 1 else give_ref.at[n // 2 - 1])


def forward(same, other, tiles, tile_rows, tile_cols, counts, n_out, after):
    n_chips, width, piece = same.shape
    per_piece = piece // TILE
    half = jax.ShapeDtypeStruct((n_out // 2, width, piece), F32)
    near = jax.ShapeDtypeStruct((1, width, piece + LANES), jnp.int16)
    rest = jax.ShapeDtypeStruct((n_out // 2 - 1, width, piece + LANES), jnp.int16)
    return pl.pallas_call(
        forward_kernel,
        in_specs=[SMEM] * 3 + [VMEM] * 4 + [ANY],
        out_specs=[VMEM] * 3,
        out_shape=[half, near, rest],
        scratch_shapes=[
            pltpu.VMEM((2 * n_chips * per_piece, width, LANES), F32),
            pltpu.VMEM((n_out * per_piece + 1, width, LANES), F32),
            pltpu.VMEM((n_out * per_piece + 1, width, LANES), F32),
        ],
        compiler_params=PARAMS,
        cost_estimate=pl.CostEstimate(
            flops=2 * tiles.size * 64, bytes_accessed=4 * tiles.size, transcendentals=0
        ),
        name="forward_product",
    )(tile_rows, tile_cols, counts, row_fold(), tiles, same, other, after)


def stack_kernel(n_after, *refs):
    out_ref, at = refs[-1], 0
    for ref in refs[: -1 - n_after]:
        if len(ref.shape) == 2:
            out_ref[at] = ref[...].astype(out_ref.dtype)
            at += 1
        else:
            out_ref[at : at + ref.shape[0]] = ref[...]
            at += ref.shape[0]


def stack(*parts, after=()):
    total = sum(x.shape[0] if x.ndim == 3 else 1 for x in parts)
    return pl.pallas_call(
        functools.partial(stack_kernel, len(after)),
        in_specs=[VMEM] * len(parts) + [ANY] * len(after),
        out_specs=VMEM,
        out_shape=jax.ShapeDtypeStruct((total,) + parts[0].shape[-2:], parts[0].dtype),
        compiler_params=PARAMS,
        name="stack_pieces",
    )(*parts, *after)


def pair_sum_kernel(keep_ref, *refs):
    n_chips = keep_ref.shape[0]
    gots, outs = refs[: 1 - n_chips], refs[1 - n_chips :]
    got = [ref.at[h] for ref in gots for h in range(ref.shape[0])]
    for h, out in enumerate(outs):
        out[...] = keep_ref[h + 1] + got[h + 1][...]


def pair_sum(keep, gots):
    parts, width, piece = keep.shape
    return pl.pallas_call(
        pair_sum_kernel,
        in_specs=[VMEM] * (1 + len(gots)),
        out_specs=[VMEM] * (parts - 1),
        out_shape=[jax.ShapeDtypeStruct((width, piece), F32)] * (parts - 1),
        compiler_params=PARAMS,
        name="core_pair_sum",
    )(keep, *gots)


def split_sum_kernel(keep_ref, got_ref, after_ref, next_keep, near_ref, *rest_refs):
    spans = [pl.ds(n, LANES) for n in range(0, keep_ref.shape[2], LANES)]
    for h in range(keep_ref.shape[0]):
        sums = [keep_ref[h, :, at] for at in spans]
        if h > 0:
            sums = [x + got for x, got in zip(sums, decode(got_ref.at[h - 1]))]
        if h % 2 == 0:
            for at, x in zip(spans, sums):
                next_keep[h // 2, :, at] = x
        elif h == 1:
            encode(sums, near_ref.at[0])
        else:
            encode(sums, rest_refs[0].at[h // 2 - 1])


def split_sum(keep, got, after):
    parts, width, piece = keep.shape
    shapes = [jax.ShapeDtypeStruct((parts // 2, width, piece), F32)]
    shapes += [
        jax.ShapeDtypeStruct((n, width, piece + LANES), got.dtype) for n in (1, parts // 2 - 1) if n
    ]
    keep, near, *rest = pl.pallas_call(
        split_sum_kernel,
        in_specs=[VMEM] * 2 + [ANY],
        out_specs=[VMEM] * len(shapes),
        out_shape=shapes,
        compiler_params=PARAMS,
        name="halving_sum",
    )(keep, got, after)
    return keep, near, rest


def part_sum_kernel(keep_ref, got_ref, brow_keep, brow_got, *refs):
    chips, out_ref = refs[:-1], refs[-1]
    for n, got in enumerate(decode(got_ref.at[0])):
        at = pl.ds(n * LANES, LANES)
        total = brow_keep[0, :, at] + brow_got[0, :, at]
        for ref in chips:
            total = total + ref[:, at]
        out_ref[:, at] = total + (keep_ref[0, :, at] + got)


def part_sum(keep, got, brow_keep, brow_got, chips):
    return pl.pallas_call(
        part_sum_kernel,
        in_specs=[VMEM] * (4 + len(chips)),
        out_specs=VMEM,
        out_shape=jax.ShapeDtypeStruct(keep.shape[1:], F32),
        compiler_params=PARAMS,
        name="part_sum",
    )(keep, got, brow_keep, brow_got, *chips)


def last_sum_kernel(total_ref, *refs):
    gots, out_ref = refs[:-1], refs[-1]
    parts = [decode(ref.at[0]) for ref in gots]
    for n in range(total_ref.shape[1] // LANES):
        at = pl.ds(n * LANES, LANES)
        total = total_ref[:, at]
        for part in parts:
            total = total + part[n]
        out_ref[:, at] = total


def last_sum(total, gots):
    return pl.pallas_call(
        last_sum_kernel,
        in_specs=[VMEM] * (1 + len(gots)),
        out_specs=VMEM,
        out_shape=jax.ShapeDtypeStruct(total.shape, F32),
        compiler_params=PARAMS,
        name="last_sum",
    )(total, *gots)


def take_kernel(x_ref, out_ref, wide_ref):
    out_ref[0] = x_ref[...]
    wide_ref[...] = x_ref[...].astype(F32)


def take(x):
    return pl.pallas_call(
        take_kernel,
        in_specs=[VMEM],
        out_specs=[VMEM] * 2,
        out_shape=[
            jax.ShapeDtypeStruct((1,) + x.shape, x.dtype),
            jax.ShapeDtypeStruct(x.shape, F32),
        ],
        compiler_params=PARAMS,
        name="take_piece",
    )(x)


def swap(x, axis, size, d):
    return lax.ppermute(x, axis, [(i, i ^ d) for i in range(size)])


def body(vectors, tiles, tile_rows, tile_cols, counts):
    n_rows = lax.axis_size("brow")
    n_cols = lax.axis_size("bcol")
    own, wide = take(vectors)
    chips = [swap(wide, "brow", n_rows, 2 * h + 1) for h in range(1, n_rows // 2)]
    segment, d = own, n_cols // 2
    while d > 0:
        first = d == n_cols // 2
        segment = stack(segment, swap(vectors[None] if first else segment, "bcol", n_cols, d))
        d //= 2
    blocks = prep(tiles)
    same = stack(own, *chips, after=(blocks,))
    other = swap(same, "brow", n_rows, 1)

    col_keep, *col_give = backward(segment, blocks, tile_rows, tile_cols, counts, n_rows, same)
    row_keep, near, rest = forward(same, other, blocks, tile_rows, tile_cols, counts, n_cols, col_give[0])
    col_got = [swap(x, "brow", n_rows, 1) for x in col_give]
    sums = pair_sum(col_keep, col_got)
    from_chips = [swap(x, "brow", n_rows, 2 * h + 3) for h, x in enumerate(sums)]
    d, later = 1, []
    while 2 * d < n_cols:
        row_got = swap(rest, "bcol", n_cols, d)
        later.append((near, d))
        row_keep, near, rest = split_sum(row_keep, row_got, sums[0])
        rest = rest[0] if rest else None
        d *= 2
    far = swap(near, "bcol", n_cols, d)
    total = part_sum(row_keep, far, col_keep, col_got[0], from_chips)
    return last_sum(total, [swap(x, "bcol", n_cols, d) for x, d in later])


def solution(mesh):
    return jax.shard_map(
        body,
        mesh=mesh,
        in_specs=(
            P(None, ("brow", "bcol")),
            P(("brow", "bcol"), None),
            P(("brow", "bcol")),
            P(("brow", "bcol")),
            P("brow", "bcol"),
        ),
        out_specs=P(None, ("brow", "bcol")),
        check_vma=False,
    )
```

```python
import functools

import jax
import jax.numpy as jnp
import numpy as np
from jax import lax
from jax.experimental import pallas as pl
from jax.experimental.pallas import tpu as pltpu
from jax.sharding import PartitionSpec as P

TILE = 64
LANES = 128
HALF = TILE // 2
GROUP = LANES // HALF
STEPS = 32000.0
F32 = jnp.float32
BF16 = jnp.bfloat16
VMEM = pl.BlockSpec(memory_space=pltpu.VMEM)
ANY = pl.BlockSpec(memory_space=pl.ANY)
SMEM = pl.BlockSpec(memory_space=pltpu.SMEM)
PARAMS = pltpu.CompilerParams(vmem_limit_bytes=48 * 1024 * 1024)


def row_spread():
    out = np.zeros((LANES, 2, 2, GROUP, HALF), np.float32)
    for q in range(2):
        for e in range(2):
            for m in range(HALF):
                out[q * TILE + 2 * m + e, q, e, :, m] = 1
    return jnp.asarray(out.reshape(LANES, 4 * LANES), BF16)


def row_fold():
    out = np.zeros((2, 2, 2, GROUP // 2, HALF, LANES), np.float32)
    for q in range(2):
        for e in range(2):
            for m in range(HALF):
                out[q, 0, e, :, m, q * TILE + 2 * m + e] = 1
                out[q, 1, 1 - e, :, m, q * TILE + 2 * m + e] = 1
    return jnp.asarray(out.reshape(4 * LANES, LANES), BF16)


def encode(values, out_ref):
    width, piece = values[0].shape[0], LANES * len(values)
    lane = lax.broadcasted_iota(jnp.int32, (width, LANES), 1)
    tops = jnp.zeros((width, LANES), F32)
    for n, value in enumerate(values):
        tops = jnp.where(lane == n, jnp.max(jnp.abs(value), axis=1, keepdims=True), tops)
    exponents = jnp.clip(jnp.ceil(jnp.log2(tops)), -100.0, 100.0)
    scales = STEPS * jnp.exp2(-exponents)
    for n, value in enumerate(values):
        scaled = jnp.floor(value * scales[:, n : n + 1] + 0.5)
        out_ref[:, n * LANES : (n + 1) * LANES] = scaled.astype(jnp.int32).astype(jnp.int16)
    out_ref[:, piece:] = exponents.astype(jnp.int32).astype(jnp.int16)


def decode(ref):
    chunks = ref.shape[1] // LANES - 1
    exponents = ref[:, chunks * LANES :].astype(jnp.int32).astype(F32)
    scales = jnp.exp2(exponents) * (1.0 / STEPS)
    return [
        ref[:, n * LANES : (n + 1) * LANES].astype(jnp.int32).astype(F32) * scales[:, n : n + 1]
        for n in range(chunks)
    ]


def prep_kernel(tiles_ref, out_ref, wide):
    for b in range(tiles_ref.shape[0]):
        wide[b] = tiles_ref[b].astype(F32).reshape(HALF * 8, LANES)
        for s in range(8):
            out_ref[8 * b + s] = wide[b, pl.ds(s, HALF, stride=8), :].astype(BF16)


def prep(tiles):
    slots = tiles.shape[0]
    blocks = slots // 8
    view = tiles.reshape(blocks, 8, HALF, LANES).swapaxes(1, 2)
    return pl.pallas_call(
        prep_kernel,
        in_specs=[VMEM],
        out_specs=VMEM,
        out_shape=jax.ShapeDtypeStruct((slots, HALF, LANES), BF16),
        scratch_shapes=[pltpu.VMEM((blocks, HALF * 8, LANES), F32)],
        compiler_params=PARAMS,
        cost_estimate=pl.CostEstimate(flops=0, bytes_accessed=4 * tiles.size, transcendentals=0),
        name="prep_tiles",
    )(view)


def doubled(size):
    order, d = [0], size // 2
    while d > 0:
        order += [x ^ d for x in order]
        d //= 2
    return order


def build_table(pieces, spread, table):
    width, piece = pieces[0].shape
    pairs = piece // LANES
    for n, ref in enumerate(pieces):
        rows = jnp.concatenate([ref[:, p * LANES : (p + 1) * LANES] for p in range(pairs)], axis=0)
        wide = jnp.dot(rows, spread, preferred_element_type=F32)
        wide = wide.reshape(pairs, width, 4 * LANES)
        for q in range(2):
            both = jnp.concatenate(
                [wide[:, :, (2 * q + e) * LANES : (2 * q + e + 1) * LANES] for e in range(2)], axis=1
            ).astype(BF16)
            for p in range(pairs):
                table[n * 2 * pairs + 2 * p + q] = both[p]


def backward_kernel(
    rows_ref, cols_ref, count_ref, spread_ref, tiles_ref, seg_ref, after_ref, keep_ref, *refs
):
    pieces = [seg_ref.at[at] for at in np.argsort(doubled(seg_ref.shape[0]))]
    *give_refs, table, acc_a, acc_b = refs
    per_give = give_refs[0].shape[0]
    n_out = 2 * keep_ref.shape[0]
    width, piece = pieces[0].shape
    per_piece = piece // TILE
    slots = tiles_ref.shape[0]
    build_table(pieces, spread_ref[...], table)
    for acc in (acc_a, acc_b):
        acc[...] = jnp.zeros_like(acc)
    lane = lax.broadcasted_iota(jnp.int32, (2 * width, LANES), 1)
    masks = [(lane // HALF == s).astype(BF16) for s in range(GROUP)]
    low = lax.broadcasted_iota(jnp.int32, (width, LANES), 1) < TILE
    count = count_ref[0, 0]
    row_flip = lax.axis_index("bcol") * per_piece
    col_flip = lax.axis_index("brow") * per_piece
    spare = n_out * per_piece

    for g in range(slots // GROUP):
        at = [table[rows_ref[g * GROUP + s] ^ row_flip] * masks[s] for s in range(GROUP)]
        block = tiles_ref[g * GROUP : (g + 1) * GROUP].reshape(LANES, LANES)
        out = jnp.dot(jnp.concatenate(at, axis=0), block, preferred_element_type=F32)
        for s in range(GROUP):
            t = g * GROUP + s
            part = out[2 * width * s : 2 * width * (s + 1)]
            part = jnp.where(low, part[:width], part[width:])
            c = jnp.where(t < count, cols_ref[t] ^ col_flip, spare)
            acc = acc_a if s % 2 == 0 else acc_b
            acc[c] += part

    for n in range(n_out):
        h = n // 2
        kept = (n % 2 == 0) == (h == 0)
        dest = keep_ref.at[h] if kept else give_refs[h // per_give].at[h % per_give]
        for p in range(per_piece // 2):
            at = n * per_piece + 2 * p
            a = acc_a[at] + acc_b[at]
            b = acc_a[at + 1] + acc_b[at + 1]
            dest[:, p * LANES : (p + 1) * LANES] = jnp.where(low, a, b) + pltpu.roll(
                jnp.where(low, b, a), TILE, 1
            )


def backward(segment, tiles, tile_rows, tile_cols, counts, n_out, after):
    n_in, width, piece = segment.shape
    per_piece = piece // TILE
    half = jax.ShapeDtypeStruct((n_out // 2, width, piece), F32)
    quarter = jax.ShapeDtypeStruct((n_out // 4, width, piece), F32)
    return pl.pallas_call(
        backward_kernel,
        in_specs=[SMEM] * 3 + [VMEM] * 3 + [ANY],
        out_specs=[VMEM] * 3,
        out_shape=[half, quarter, quarter],
        scratch_shapes=[
            pltpu.VMEM((n_in * per_piece, 2 * width, LANES), BF16),
            pltpu.VMEM((n_out * per_piece + 1, width, LANES), F32),
            pltpu.VMEM((n_out * per_piece + 1, width, LANES), F32),
        ],
        compiler_params=PARAMS,
        cost_estimate=pl.CostEstimate(
            flops=2 * tiles.size * 64, bytes_accessed=4 * tiles.size, transcendentals=0
        ),
        name="transpose_product",
    )(tile_rows, tile_cols, counts, row_spread(), tiles, segment, after)


def double_table(pieces, table):
    width, piece = pieces[0].shape
    low = lax.broadcasted_iota(jnp.int32, (width, LANES), 1) < TILE
    for n, ref in enumerate(pieces):
        for p in range(piece // LANES):
            pair = ref[:, p * LANES : (p + 1) * LANES].astype(F32)
            turned = pltpu.roll(pair, TILE, 1)
            at = (n * piece + p * LANES) // TILE
            table[at] = jnp.where(low, pair, turned)
            table[at + 1] = jnp.where(low, turned, pair)


def forward_kernel(
    rows_ref,
    cols_ref,
    count_ref,
    fold_ref,
    tiles_ref,
    same_ref,
    other_ref,
    after_ref,
    keep_ref,
    give_ref,
    table,
    acc_a,
    acc_b,
):
    pieces = []
    for h in range(same_ref.shape[0]):
        pair = [same_ref.at[h], other_ref.at[h]]
        pieces += pair if h == 0 else pair[::-1]
    n_out = 2 * keep_ref.shape[0]
    width, piece = pieces[0].shape
    per_piece = piece // TILE
    slots = tiles_ref.shape[0]
    double_table(pieces, table)
    for acc in (acc_a, acc_b):
        acc[...] = jnp.zeros_like(acc)
    lane = lax.broadcasted_iota(jnp.int32, (width, LANES), 1)
    masks = [lane // HALF == s for s in range(GROUP)]
    wide_lane = lax.broadcasted_iota(jnp.int32, (LANES, LANES), 1)
    parity = [(wide_lane // TILE == e).astype(BF16) for e in range(2)]
    count = count_ref[0, 0]
    row_flip = lax.axis_index("bcol") * per_piece
    col_flip = lax.axis_index("brow") * per_piece
    spare = n_out * per_piece

    for g in range(slots // GROUP):
        at = [table[cols_ref[g * GROUP + s] ^ col_flip] for s in range(GROUP)]
        block = tiles_ref[g * GROUP : (g + 1) * GROUP].reshape(LANES, LANES)
        turned = jnp.concatenate([block[LANES // 2 :], block[: LANES // 2]], axis=0)
        out = lax.dot_general(
            jnp.concatenate(at, axis=0).astype(BF16),
            jnp.concatenate([block * parity[0], turned * parity[1]], axis=0),
            (((1,), (1,)), ((), ())),
            preferred_element_type=F32,
        )
        for s in range(GROUP):
            t = g * GROUP + s
            part = out[width * s : width * (s + 1)]
            r = jnp.where(t < count, rows_ref[t] ^ row_flip, spare)
            part = jnp.where(
                masks[s], part[:, :LANES], jnp.where(masks[(s + 2) % GROUP], part[:, LANES:], 0.0)
            )
            acc = acc_a if s < 2 else acc_b
            acc[r] += part

    fold = fold_ref[...]
    pairs = per_piece // 2
    for n in range(n_out):
        blocks = []
        for q in range(2):
            for acc in (acc_a, acc_b):
                both = acc[n * per_piece : (n + 1) * per_piece].reshape(pairs, 2 * width, LANES)
                blocks.append(both[:, q * width : (q + 1) * width, :].reshape(pairs * width, LANES))
        wide = jnp.concatenate(blocks, axis=1)
        first = wide.astype(BF16)
        rest = (wide - first.astype(F32)).astype(BF16)
        out = jnp.dot(first, fold, preferred_element_type=F32)
        out = out + jnp.dot(rest, fold, preferred_element_type=F32)
        parts = [out[p * width : (p + 1) * width] for p in range(pairs)]
        if n % 2 == 0:
            for p in range(pairs):
                keep_ref[n // 2, :, p * LANES : (p + 1) * LANES] = parts[p]
        else:
            encode(parts, give_ref.at[n // 2])


def forward(same, other, tiles, tile_rows, tile_cols, counts, n_out, after):
    n_chips, width, piece = same.shape
    per_piece = piece // TILE
    half = jax.ShapeDtypeStruct((n_out // 2, width, piece), F32)
    coded = jax.ShapeDtypeStruct((n_out // 2, width, piece + LANES), jnp.int16)
    return pl.pallas_call(
        forward_kernel,
        in_specs=[SMEM] * 3 + [VMEM] * 4 + [ANY],
        out_specs=[VMEM] * 2,
        out_shape=[half, coded],
        scratch_shapes=[
            pltpu.VMEM((2 * n_chips * per_piece, width, LANES), F32),
            pltpu.VMEM((n_out * per_piece + 1, width, LANES), F32),
            pltpu.VMEM((n_out * per_piece + 1, width, LANES), F32),
        ],
        compiler_params=PARAMS,
        cost_estimate=pl.CostEstimate(
            flops=2 * tiles.size * 64, bytes_accessed=4 * tiles.size, transcendentals=0
        ),
        name="forward_product",
    )(tile_rows, tile_cols, counts, row_fold(), tiles, same, other, after)


def stack_kernel(n_after, *refs):
    out_ref, at = refs[-1], 0
    for ref in refs[: -1 - n_after]:
        if len(ref.shape) == 2:
            out_ref[at] = ref[...]
            at += 1
        else:
            out_ref[at : at + ref.shape[0]] = ref[...]
            at += ref.shape[0]


def stack(*parts, after=()):
    total = sum(x.shape[0] if x.ndim == 3 else 1 for x in parts)
    return pl.pallas_call(
        functools.partial(stack_kernel, len(after)),
        in_specs=[VMEM] * len(parts) + [ANY] * len(after),
        out_specs=VMEM,
        out_shape=jax.ShapeDtypeStruct((total,) + parts[0].shape[-2:], parts[0].dtype),
        compiler_params=PARAMS,
        name="stack_pieces",
    )(*parts, *after)


def pair_sum_kernel(keep_ref, *refs):
    n_chips = keep_ref.shape[0]
    gots, outs = refs[: 1 - n_chips], refs[1 - n_chips :]
    got = [ref.at[h] for ref in gots for h in range(ref.shape[0])]
    for h, out in enumerate(outs):
        out[...] = keep_ref[h + 1] + got[h + 1][...]


def pair_sum(keep, gots):
    parts, width, piece = keep.shape
    return pl.pallas_call(
        pair_sum_kernel,
        in_specs=[VMEM] * (1 + len(gots)),
        out_specs=[VMEM] * (parts - 1),
        out_shape=[jax.ShapeDtypeStruct((width, piece), F32)] * (parts - 1),
        compiler_params=PARAMS,
        name="core_pair_sum",
    )(keep, *gots)


def split_sum_kernel(keep_ref, got_ref, after_ref, next_keep, next_give):
    for h in range(next_keep.shape[0]):
        for n, got in enumerate(decode(got_ref.at[2 * h])):
            at = pl.ds(n * LANES, LANES)
            next_keep[h, :, at] = keep_ref[2 * h, :, at] + got
        sums = [
            keep_ref[2 * h + 1, :, n * LANES : (n + 1) * LANES] + got
            for n, got in enumerate(decode(got_ref.at[2 * h + 1]))
        ]
        encode(sums, next_give.at[h])


def split_sum(keep, got, after):
    parts, width, piece = keep.shape
    return pl.pallas_call(
        split_sum_kernel,
        in_specs=[VMEM] * 2 + [ANY],
        out_specs=[VMEM] * 2,
        out_shape=[
            jax.ShapeDtypeStruct((parts // 2, width, piece), F32),
            jax.ShapeDtypeStruct((parts // 2,) + got.shape[1:], got.dtype),
        ],
        compiler_params=PARAMS,
        name="halving_sum",
    )(keep, got, after)


def last_sum_kernel(*refs):
    chips, (brow_keep, brow_got, keep_ref, got_ref, out_ref) = refs[:-5], refs[-5:]
    for n, got in enumerate(decode(got_ref.at[0])):
        at = pl.ds(n * LANES, LANES)
        total = brow_keep[0, :, at] + brow_got[0, :, at]
        for ref in chips:
            total = total + ref[:, at]
        out_ref[:, at] = total + (keep_ref[0, :, at] + got)


def last_sum(keep, got, brow_keep, brow_got, chips):
    return pl.pallas_call(
        last_sum_kernel,
        in_specs=[VMEM] * (4 + len(chips)),
        out_specs=VMEM,
        out_shape=jax.ShapeDtypeStruct(keep.shape[1:], F32),
        compiler_params=PARAMS,
        name="last_sum",
    )(*chips, brow_keep, brow_got, keep, got)


def swap(x, axis, size, d):
    return lax.ppermute(x, axis, [(i, i ^ d) for i in range(size)])


def body(vectors, tiles, tile_rows, tile_cols, counts):
    n_rows = lax.axis_size("brow")
    n_cols = lax.axis_size("bcol")
    own = stack(vectors)
    chips = [swap(vectors, "brow", n_rows, 2 * h + 1) for h in range(1, n_rows // 2)]
    segment, d = own, n_cols // 2
    while d > 0:
        first = d == n_cols // 2
        segment = stack(segment, swap(vectors[None] if first else segment, "bcol", n_cols, d))
        d //= 2
    blocks = prep(tiles)
    same = stack(own, *chips, after=(blocks,))
    other = swap(same, "brow", n_rows, 1)

    col_keep, *col_give = backward(segment, blocks, tile_rows, tile_cols, counts, n_rows, same)
    row_keep, give = forward(same, other, blocks, tile_rows, tile_cols, counts, n_cols, col_give[0])
    col_got = [swap(x, "brow", n_rows, 1) for x in col_give]
    sums = pair_sum(col_keep, col_got)
    from_chips = [swap(x, "brow", n_rows, 2 * h + 3) for h, x in enumerate(sums)]
    row_got, d = swap(give, "bcol", n_cols, 1), 2
    while d < n_cols:
        row_keep, give = split_sum(row_keep, row_got, sums[0])
        row_got = swap(give, "bcol", n_cols, d)
        d *= 2
    return last_sum(row_keep, row_got, col_keep, col_got[0], from_chips)


def solution(mesh):
    return jax.shard_map(
        body,
        mesh=mesh,
        in_specs=(
            P(None, ("brow", "bcol")),
            P(("brow", "bcol"), None),
            P(("brow", "bcol")),
            P(("brow", "bcol")),
            P("brow", "bcol"),
        ),
        out_specs=P(None, ("brow", "bcol")),
        check_vma=False,
    )
```

```python
import functools

import jax
import jax.numpy as jnp
import numpy as np
from jax import lax
from jax.experimental import pallas as pl
from jax.experimental.pallas import tpu as pltpu
from jax.sharding import PartitionSpec as P

TILE = 64
LANES = 128
HALF = TILE // 2
GROUP = LANES // HALF
STEPS = 32000.0
F32 = jnp.float32
BF16 = jnp.bfloat16
VMEM = pl.BlockSpec(memory_space=pltpu.VMEM)
ANY = pl.BlockSpec(memory_space=pl.ANY)
SMEM = pl.BlockSpec(memory_space=pltpu.SMEM)
PARAMS = pltpu.CompilerParams(vmem_limit_bytes=48 * 1024 * 1024)


def row_spread():
    source = lax.broadcasted_iota(jnp.int32, (LANES, LANES), 0)
    m = lax.broadcasted_iota(jnp.int32, (LANES, LANES), 1) % HALF
    blocks = [source == q * TILE + 2 * m + e for q in range(2) for e in range(2)]
    return jnp.concatenate([block.astype(F32) for block in blocks], axis=1).astype(BF16)


def row_fold():
    out = np.zeros((2, 2, 2, GROUP // 2, HALF, LANES), np.float32)
    for q in range(2):
        for e in range(2):
            for m in range(HALF):
                out[q, 0, e, :, m, q * TILE + 2 * m + e] = 1
                out[q, 1, 1 - e, :, m, q * TILE + 2 * m + e] = 1
    return jnp.asarray(out.reshape(4 * LANES, LANES), BF16)


def encode(values, out_ref):
    width, piece = values[0].shape[0], LANES * len(values)
    lane = lax.broadcasted_iota(jnp.int32, (width, LANES), 1)
    exponents = jnp.zeros((width, LANES), F32)
    for n, value in enumerate(values):
        top = jnp.max(jnp.abs(value), axis=1, keepdims=True)
        e = jnp.clip(jnp.ceil(jnp.log2(top)), -100.0, 100.0)
        exponents = jnp.where(lane == n, e, exponents)
        scaled = jnp.floor(value * (STEPS * jnp.exp2(-e)) + 0.5)
        out_ref[:, n * LANES : (n + 1) * LANES] = scaled.astype(jnp.int32).astype(jnp.int16)
    out_ref[:, piece:] = exponents.astype(jnp.int32).astype(jnp.int16)


def decode(ref):
    chunks = ref.shape[1] // LANES - 1
    exponents = ref[:, chunks * LANES :].astype(jnp.int32).astype(F32)
    scales = jnp.exp2(exponents) * (1.0 / STEPS)
    return [
        ref[:, n * LANES : (n + 1) * LANES].astype(jnp.int32).astype(F32) * scales[:, n : n + 1]
        for n in range(chunks)
    ]


def prep_kernel(tiles_ref, out_ref, wide):
    for b in range(tiles_ref.shape[0]):
        wide[b] = tiles_ref[b].astype(F32).reshape(HALF * 8, LANES)
        for s in range(8):
            out_ref[8 * b + s] = wide[b, pl.ds(s, HALF, stride=8), :].astype(BF16)


def prep(tiles):
    slots = tiles.shape[0]
    blocks = slots // 8
    view = tiles.reshape(blocks, 8, HALF, LANES).swapaxes(1, 2)
    return pl.pallas_call(
        prep_kernel,
        in_specs=[VMEM],
        out_specs=VMEM,
        out_shape=jax.ShapeDtypeStruct((slots, HALF, LANES), BF16),
        scratch_shapes=[pltpu.VMEM((blocks, HALF * 8, LANES), F32)],
        compiler_params=PARAMS,
        cost_estimate=pl.CostEstimate(flops=0, bytes_accessed=4 * tiles.size, transcendentals=0),
        name="prep_tiles",
    )(view)


def doubled(size):
    order, d = [0], size // 2
    while d > 0:
        order += [x ^ d for x in order]
        d //= 2
    return order


def build_table(pieces, spread, table):
    width, piece = pieces[0].shape
    pairs = piece // LANES
    for n, ref in enumerate(pieces):
        rows = jnp.concatenate([ref[:, p * LANES : (p + 1) * LANES] for p in range(pairs)], axis=0)
        wide = jnp.dot(rows, spread, preferred_element_type=F32)
        wide = wide.reshape(pairs, width, 4 * LANES)
        for q in range(2):
            both = jnp.concatenate(
                [wide[:, :, (2 * q + e) * LANES : (2 * q + e + 1) * LANES] for e in range(2)], axis=1
            ).astype(BF16)
            for p in range(pairs):
                table[n * 2 * pairs + 2 * p + q] = both[p]


def backward_kernel(
    rows_ref, cols_ref, count_ref, tiles_ref, seg_ref, after_ref, keep_ref, *refs
):
    pieces = [seg_ref.at[at] for at in np.argsort(doubled(seg_ref.shape[0]))]
    *give_refs, table, acc_a, acc_b = refs
    per_give = give_refs[0].shape[0]
    n_out = 2 * keep_ref.shape[0]
    width, piece = pieces[0].shape
    per_piece = piece // TILE
    slots = tiles_ref.shape[0]
    build_table(pieces, row_spread(), table)
    for acc in (acc_a, acc_b):
        acc[...] = jnp.zeros_like(acc)
    lane = lax.broadcasted_iota(jnp.int32, (2 * width, LANES), 1)
    masks = [(lane // HALF == s).astype(BF16) for s in range(GROUP)]
    low = lax.broadcasted_iota(jnp.int32, (width, LANES), 1) < TILE
    count = count_ref[0, 0]
    row_flip = lax.axis_index("bcol") * per_piece
    col_flip = lax.axis_index("brow") * per_piece
    spare = n_out * per_piece

    for g in range(slots // GROUP):
        at = [table[rows_ref[g * GROUP + s] ^ row_flip] * masks[s] for s in range(GROUP)]
        block = tiles_ref[g * GROUP : (g + 1) * GROUP].reshape(LANES, LANES)
        out = jnp.dot(jnp.concatenate(at, axis=0), block, preferred_element_type=F32)
        for s in range(GROUP):
            t = g * GROUP + s
            part = out[2 * width * s : 2 * width * (s + 1)]
            part = jnp.where(low, part[:width], part[width:])
            c = jnp.where(t < count, cols_ref[t] ^ col_flip, spare)
            acc = acc_a if s % 2 == 0 else acc_b
            acc[c] += part

    for n in range(n_out):
        h = n // 2
        kept = (n % 2 == 0) == (h == 0)
        dest = keep_ref.at[h] if kept else give_refs[h // per_give].at[h % per_give]
        for p in range(per_piece // 2):
            at = n * per_piece + 2 * p
            a = acc_a[at] + acc_b[at]
            b = acc_a[at + 1] + acc_b[at + 1]
            dest[:, p * LANES : (p + 1) * LANES] = jnp.where(low, a, b) + pltpu.roll(
                jnp.where(low, b, a), TILE, 1
            )


def backward(segment, tiles, tile_rows, tile_cols, counts, n_out, after):
    n_in, width, piece = segment.shape
    per_piece = piece // TILE
    half = jax.ShapeDtypeStruct((n_out // 2, width, piece), F32)
    quarter = jax.ShapeDtypeStruct((n_out // 4, width, piece), F32)
    return pl.pallas_call(
        backward_kernel,
        in_specs=[SMEM] * 3 + [VMEM] * 2 + [ANY],
        out_specs=[VMEM] * 3,
        out_shape=[half, quarter, quarter],
        scratch_shapes=[
            pltpu.VMEM((n_in * per_piece, 2 * width, LANES), BF16),
            pltpu.VMEM((n_out * per_piece + 1, width, LANES), F32),
            pltpu.VMEM((n_out * per_piece + 1, width, LANES), F32),
        ],
        compiler_params=PARAMS,
        cost_estimate=pl.CostEstimate(
            flops=2 * tiles.size * 64, bytes_accessed=4 * tiles.size, transcendentals=0
        ),
        name="transpose_product",
    )(tile_rows, tile_cols, counts, tiles, segment, after)


def double_table(pieces, table):
    width, piece = pieces[0].shape
    low = lax.broadcasted_iota(jnp.int32, (width, LANES), 1) < TILE
    for n, ref in enumerate(pieces):
        for p in range(piece // LANES):
            pair = ref[:, p * LANES : (p + 1) * LANES].astype(F32)
            turned = pltpu.roll(pair, TILE, 1)
            at = (n * piece + p * LANES) // TILE
            table[at] = jnp.where(low, pair, turned)
            table[at + 1] = jnp.where(low, turned, pair)


def forward_kernel(
    rows_ref,
    cols_ref,
    count_ref,
    fold_ref,
    tiles_ref,
    same_ref,
    other_ref,
    after_ref,
    keep_ref,
    give_ref,
    table,
    acc_a,
    acc_b,
):
    pieces = []
    for h in range(same_ref.shape[0]):
        pair = [same_ref.at[h], other_ref.at[h]]
        pieces += pair if h == 0 else pair[::-1]
    n_out = 2 * keep_ref.shape[0]
    width, piece = pieces[0].shape
    per_piece = piece // TILE
    slots = tiles_ref.shape[0]
    double_table(pieces, table)
    for acc in (acc_a, acc_b):
        acc[...] = jnp.zeros_like(acc)
    lane = lax.broadcasted_iota(jnp.int32, (width, LANES), 1)
    masks = [lane // HALF == s for s in range(GROUP)]
    wide_lane = lax.broadcasted_iota(jnp.int32, (LANES, LANES), 1)
    parity = [(wide_lane // TILE == e).astype(BF16) for e in range(2)]
    count = count_ref[0, 0]
    row_flip = lax.axis_index("bcol") * per_piece
    col_flip = lax.axis_index("brow") * per_piece
    spare = n_out * per_piece

    for g in range(slots // GROUP):
        at = [table[cols_ref[g * GROUP + s] ^ col_flip] for s in range(GROUP)]
        block = tiles_ref[g * GROUP : (g + 1) * GROUP].reshape(LANES, LANES)
        turned = jnp.concatenate([block[LANES // 2 :], block[: LANES // 2]], axis=0)
        out = lax.dot_general(
            jnp.concatenate(at, axis=0).astype(BF16),
            jnp.concatenate([block * parity[0], turned * parity[1]], axis=0),
            (((1,), (1,)), ((), ())),
            preferred_element_type=F32,
        )
        for s in range(GROUP):
            t = g * GROUP + s
            part = out[width * s : width * (s + 1)]
            r = jnp.where(t < count, rows_ref[t] ^ row_flip, spare)
            part = jnp.where(
                masks[s], part[:, :LANES], jnp.where(masks[(s + 2) % GROUP], part[:, LANES:], 0.0)
            )
            acc = acc_a if s < 2 else acc_b
            acc[r] += part

    fold = fold_ref[...]
    pairs = per_piece // 2
    for n in range(n_out):
        blocks = []
        for q in range(2):
            for acc in (acc_a, acc_b):
                both = acc[n * per_piece : (n + 1) * per_piece].reshape(pairs, 2 * width, LANES)
                blocks.append(both[:, q * width : (q + 1) * width, :].reshape(pairs * width, LANES))
        wide = jnp.concatenate(blocks, axis=1)
        first = wide.astype(BF16)
        rest = (wide - first.astype(F32)).astype(BF16)
        out = jnp.dot(first, fold, preferred_element_type=F32)
        out = out + jnp.dot(rest, fold, preferred_element_type=F32)
        parts = [out[p * width : (p + 1) * width] for p in range(pairs)]
        if n % 2 == 0:
            for p in range(pairs):
                keep_ref[n // 2, :, p * LANES : (p + 1) * LANES] = parts[p]
        else:
            encode(parts, give_ref.at[n // 2])


def forward(same, other, tiles, tile_rows, tile_cols, counts, n_out, after):
    n_chips, width, piece = same.shape
    per_piece = piece // TILE
    half = jax.ShapeDtypeStruct((n_out // 2, width, piece), F32)
    coded = jax.ShapeDtypeStruct((n_out // 2, width, piece + LANES), jnp.int16)
    return pl.pallas_call(
        forward_kernel,
        in_specs=[SMEM] * 3 + [VMEM] * 4 + [ANY],
        out_specs=[VMEM] * 2,
        out_shape=[half, coded],
        scratch_shapes=[
            pltpu.VMEM((2 * n_chips * per_piece, width, LANES), F32),
            pltpu.VMEM((n_out * per_piece + 1, width, LANES), F32),
            pltpu.VMEM((n_out * per_piece + 1, width, LANES), F32),
        ],
        compiler_params=PARAMS,
        cost_estimate=pl.CostEstimate(
            flops=2 * tiles.size * 64, bytes_accessed=4 * tiles.size, transcendentals=0
        ),
        name="forward_product",
    )(tile_rows, tile_cols, counts, row_fold(), tiles, same, other, after)


def stack_kernel(n_after, *refs):
    out_ref, at = refs[-1], 0
    for ref in refs[: -1 - n_after]:
        if len(ref.shape) == 2:
            out_ref[at] = ref[...]
            at += 1
        else:
            out_ref[at : at + ref.shape[0]] = ref[...]
            at += ref.shape[0]


def stack(*parts, after=()):
    total = sum(x.shape[0] if x.ndim == 3 else 1 for x in parts)
    return pl.pallas_call(
        functools.partial(stack_kernel, len(after)),
        in_specs=[VMEM] * len(parts) + [ANY] * len(after),
        out_specs=VMEM,
        out_shape=jax.ShapeDtypeStruct((total,) + parts[0].shape[-2:], parts[0].dtype),
        compiler_params=PARAMS,
        name="stack_pieces",
    )(*parts, *after)


def pair_sum_kernel(keep_ref, *refs):
    n_chips = keep_ref.shape[0]
    gots, outs = refs[: 1 - n_chips], refs[1 - n_chips :]
    got = [ref.at[h] for ref in gots for h in range(ref.shape[0])]
    for h, out in enumerate(outs):
        out[...] = keep_ref[h + 1] + got[h + 1][...]


def pair_sum(keep, gots):
    parts, width, piece = keep.shape
    return pl.pallas_call(
        pair_sum_kernel,
        in_specs=[VMEM] * (1 + len(gots)),
        out_specs=[VMEM] * (parts - 1),
        out_shape=[jax.ShapeDtypeStruct((width, piece), F32)] * (parts - 1),
        compiler_params=PARAMS,
        name="core_pair_sum",
    )(keep, *gots)


def split_sum_kernel(keep_ref, got_ref, after_ref, next_keep, next_give):
    for h in range(next_keep.shape[0]):
        for n, got in enumerate(decode(got_ref.at[2 * h])):
            at = pl.ds(n * LANES, LANES)
            next_keep[h, :, at] = keep_ref[2 * h, :, at] + got
        sums = [
            keep_ref[2 * h + 1, :, n * LANES : (n + 1) * LANES] + got
            for n, got in enumerate(decode(got_ref.at[2 * h + 1]))
        ]
        encode(sums, next_give.at[h])


def split_sum(keep, got, after):
    parts, width, piece = keep.shape
    return pl.pallas_call(
        split_sum_kernel,
        in_specs=[VMEM] * 2 + [ANY],
        out_specs=[VMEM] * 2,
        out_shape=[
            jax.ShapeDtypeStruct((parts // 2, width, piece), F32),
            jax.ShapeDtypeStruct((parts // 2,) + got.shape[1:], got.dtype),
        ],
        compiler_params=PARAMS,
        name="halving_sum",
    )(keep, got, after)


def last_sum_kernel(*refs):
    chips, (brow_keep, brow_got, keep_ref, got_ref, out_ref) = refs[:-5], refs[-5:]
    for n, got in enumerate(decode(got_ref.at[0])):
        at = pl.ds(n * LANES, LANES)
        total = brow_keep[0, :, at] + brow_got[0, :, at]
        for ref in chips:
            total = total + ref[:, at]
        out_ref[:, at] = total + (keep_ref[0, :, at] + got)


def last_sum(keep, got, brow_keep, brow_got, chips):
    return pl.pallas_call(
        last_sum_kernel,
        in_specs=[VMEM] * (4 + len(chips)),
        out_specs=VMEM,
        out_shape=jax.ShapeDtypeStruct(keep.shape[1:], F32),
        compiler_params=PARAMS,
        name="last_sum",
    )(*chips, brow_keep, brow_got, keep, got)


def swap(x, axis, size, d):
    return lax.ppermute(x, axis, [(i, i ^ d) for i in range(size)])


def body(vectors, tiles, tile_rows, tile_cols, counts):
    n_rows = lax.axis_size("brow")
    n_cols = lax.axis_size("bcol")
    own = stack(vectors)
    chips = [swap(vectors, "brow", n_rows, 2 * h + 1) for h in range(1, n_rows // 2)]
    segment, d = own, n_cols // 2
    while d > 0:
        first = d == n_cols // 2
        segment = stack(segment, swap(vectors[None] if first else segment, "bcol", n_cols, d))
        d //= 2
    blocks = prep(tiles)
    same = stack(own, *chips, after=(blocks,))
    other = swap(same, "brow", n_rows, 1)

    col_keep, *col_give = backward(segment, blocks, tile_rows, tile_cols, counts, n_rows, same)
    row_keep, give = forward(same, other, blocks, tile_rows, tile_cols, counts, n_cols, col_give[0])
    col_got = [swap(x, "brow", n_rows, 1) for x in col_give]
    sums = pair_sum(col_keep, col_got)
    from_chips = [swap(x, "brow", n_rows, 2 * h + 3) for h, x in enumerate(sums)]
    row_got, d = swap(give, "bcol", n_cols, 1), 2
    while d < n_cols:
        row_keep, give = split_sum(row_keep, row_got, sums[0])
        row_got = swap(give, "bcol", n_cols, d)
        d *= 2
    return last_sum(row_keep, row_got, col_keep, col_got[0], from_chips)


def solution(mesh):
    return jax.shard_map(
        body,
        mesh=mesh,
        in_specs=(
            P(None, ("brow", "bcol")),
            P(("brow", "bcol"), None),
            P(("brow", "bcol")),
            P(("brow", "bcol")),
            P("brow", "bcol"),
        ),
        out_specs=P(None, ("brow", "bcol")),
        check_vma=False,
    )
```
